32 devices in a mesh: dp: 4 (over z), unit: 8 (over y, x, core).
Axes of the slice: x: 2, y: 2, z: 4, core: 2. Of those that a mesh axis runs over, the one named last changes fastest.
Arguments:
- token_ids: int32 [32, 1024], P(('dp', 'unit')), may hold values from 0 to 30719
- segment_ids: int32 [32, 1024], P(('dp', 'unit')), may hold values from 0 to 15, never falling along the last dimension, each value on 1 to 256 neighbouring positions
- real_mask: int32 [32, 1024], replicated, may hold values from 0 to 1, as said below
- positions: int32 [32, 64], P(('dp', 'unit')), may hold values from 0 to 1023
- targets: int32 [32, 64], replicated, may hold values from 0 to 30719
- teacher_states: bfloat16 [32, 1024, 768], P(('dp', 'unit')), may hold values from -6 to 6
- head_gate: float32 [2, 12], replicated, may hold values from 0.2 to 1
- layer_gate: float32 [2, 2], replicated, may hold values from 0.5 to 1
- hidden_gate: float32 [768], replicated, may hold values from 0.3 to 1
- unit_gate: float32 [2, 3072], replicated, may hold values from 0.2 to 1
- unit_keep: int32 [2, 3072], replicated, may hold values 0 or 1
- embedding: float32 [30720, 768], P('unit')
- attention: float32 [2, 4, 768, 768], replicated, may hold values from -0.21875 to 0.21875
- feed_forward: float32 [2, 2, 3072, 768], P(None, None, 'unit'), may hold values from -0.21875 to 0.21875
- map_weight: float32 [768, 768], replicated, may hold values from -0.21875 to 0.21875
- norm_params: float32 [10, 768], replicated, may hold values from 0.5 to 1.5
- embedding_rows: float32 [30720], P('unit'), may hold values from 1.7156695e-12 to 2.7450712e-11
- embedding_cols: float32 [768], replicated, may hold values from 4.2891737e-13 to 6.862678e-12
- attention_rows: float32 [2, 4, 768], P(None, None, 'unit'), may hold values from 1.7156695e-12 to 2.7450712e-11
- attention_cols: float32 [2, 4, 768], replicated, may hold values from 1.7156695e-12 to 2.7450712e-11
- feed_rows: float32 [2, 2, 3072], P(None, None, 'unit'), may hold values from 1.7156695e-12 to 2.7450712e-11
- feed_cols: float32 [2, 2, 768], replicated, may hold values from 1.7156695e-12 to 2.7450712e-11
- map_rows: float32 [768], P('unit'), may hold values from 1.7156695e-12 to 2.7450712e-11
- map_cols: float32 [768], replicated, may hold values from 1.7156695e-12 to 2.7450712e-11
- norm_moment: float32 [10, 768], replicated, may hold values from 2.7450712e-11 to 4.3463627e-10
Outputs:
- total_loss: float32 [], replicated
- real_count: float32 [], replicated
- grad_norm: float32 [], replicated
- new_embedding: float32 [30720, 768], P('unit')
- embedding_grad: float32 [30720, 768], P('unit')
- new_embedding_rows: float32 [30720], P('unit')
- new_embedding_cols: float32 [768], replicated
- new_attention: float32 [2, 4, 768, 768], P(None, None, 'unit')
- attention_grad: float32 [2, 4, 768, 768], P(None, None, 'unit')
- new_attention_rows: float32 [2, 4, 768], P(None, None, 'unit')
- new_attention_cols: float32 [2, 4, 768], replicated
- new_feed_forward: float32 [2, 2, 3072, 768], P(None, None, 'unit')
- feed_grad: float32 [2, 2, 3072, 768], P(None, None, 'unit')
- new_feed_rows: float32 [2, 2, 3072], P(None, None, 'unit')
- new_feed_cols: float32 [2, 2, 768], replicated
- new_map: float32 [768, 768], P('unit')
- map_grad: float32 [768, 768], P('unit')
- new_map_rows: float32 [768], P('unit')
- new_map_cols: float32 [768], replicated
- new_norm_params: float32 [10, 768], replicated
- norm_grad: float32 [10, 768], replicated
- new_norm_moment: float32 [10, 768], replicated
The draws below stay inside these ranges and needn't reach their ends.
Inputs may be any that keep to these rules, and one draw needn't show every extreme that they name: `real_mask`: position 0 of every sequence is real.
All inputs are finite; a program needn't handle non-finite values.
Results may differ from the reference program's by a relative error of at most 0.0061.
Values may be sent and summed in bfloat16 or wider, within the bound.
No kernel may reach another device: no remote copies, remote signals or barrier semaphores. Data moves between devices by JAX's collectives and lax.ppermute only.
A program may use at most 640 MiB of HBM per device.

```python
import math
import jax
import jax.numpy as jnp
import numpy as np
from jax import lax

D = 768
H = 12
HD = 64
FF = 3072
VOCAB = 30720
LAYERS = 2
LEN = 1024
POS = 64
SEQ_DEV = 1
SEQS = 32
NV = 10
N_DP = 4
N_UNIT = 8


def draw_real_mask(key, part):
    density = 300 + 650 * jnp.arange(SEQS) // max(SEQS - 1, 1)
    rolled = jax.random.randint(key, (SEQS, LEN), 0, 1000)
    flags = (rolled < density[:, None]).astype(jnp.int32)
    return flags.at[:, 0].set(1)


def draw_embedding(key, part):
    place = jnp.arange(VOCAB, dtype=jnp.float32) / max(VOCAB - 1, 1)
    row_scale = 1.0 + 2.0 * place
    base = jnp.clip(jax.random.normal(key, (VOCAB, D), jnp.float32), -6.0, 6.0)
    return base * row_scale[:, None] / jnp.sqrt(jnp.float32(D))


def touch_ends(entries, rng, smallest, high):
    spot = [jax.random.randint(jax.random.fold_in(rng, axis), (), 0, length) for axis, length in enumerate(entries.shape)]
    widest = entries.shape.index(max(entries.shape))
    next_to = spot[:widest] + [(spot[widest] + 1) % entries.shape[widest]] + spot[widest + 1:]
    return entries.at[tuple(spot)].set(smallest).at[tuple(next_to)].set(high)


def steps_of(stream_key, shape, cuts, low, high):
    factor_of = 1.0
    for axis_at, blocks in cuts:
        draws = jax.random.uniform(jax.random.fold_in(jax.random.fold_in(stream_key, 6), axis_at), (blocks,), jnp.float32, low / len(cuts), high / len(cuts))
        factor_of = factor_of * jnp.repeat(jnp.exp(draws), shape[axis_at] // blocks).reshape((-1,) + (1,) * (len(shape) - 1 - axis_at))
    return factor_of


def rank_table(number_of, lean):
    loads = [(1 << 20) // math.isqrt(grade ** lean) + 1 for grade in range(1, number_of + 1)]
    scale = 1 + sum(loads) // (1 << 30)
    return np.cumsum(np.array([max(1, weight // scale) for weight in loads]))


def ranked(rng, dims, number_of, slope):
    listing = rank_table(number_of, slope)
    lot = jax.random.randint(jax.random.fold_in(rng, 1), dims, 0, int(listing[number_of - 1]))
    grade = jnp.searchsorted(jnp.asarray(listing, jnp.int32), lot, side="right")
    return jax.random.permutation(jax.random.fold_in(rng, 2), number_of)[grade].astype(jnp.int32)


def split_up(number_of, total, reach, skew):
    weights = [(1 << 20) // math.isqrt(grade ** skew) + 1 for grade in range(2, number_of + 1)]
    spare, given = total - reach - (number_of - 1), [1] * (number_of - 1)
    while spare > 0:
        candidates = [i for i in range(number_of - 1) if given[i] < reach]
        whole, remaining = sum([weights[i] for i in candidates]), spare
        for i in candidates:
            more = min(reach - given[i], max(1, remaining * weights[i] // whole), spare)
            given[i] = given[i] + more
            spare = spare - more
    return np.array([reach] + given)


def ragged_sizes(rng, number_of, total, most, slope):
    if number_of == 2:
        one = jax.random.randint(rng, (), max(1, total - most), min(most, total - 1) + 1)
        return jnp.stack([one, total - one])
    tallies = jnp.asarray(split_up(number_of, total, most, slope), jnp.int32)
    couples = (number_of - 1) // 2
    donor, sink = tallies[1:1 + 2 * couples:2], tallies[2:2 + 2 * couples:2]
    room = jnp.minimum(donor - 1, most - sink)
    moved = jax.random.randint(jax.random.fold_in(rng, 1), (couples,), 0, 1 << 20) % (room + 1)
    tallies = tallies.at[1:1 + 2 * couples:2].set(donor - moved).at[2:2 + 2 * couples:2].set(sink + moved)
    return tallies[jax.random.permutation(jax.random.fold_in(rng, 2), number_of)]


def centred(key, extent, scale, limit, cuts=(), kind=jnp.bfloat16):
    loudness = steps_of(key, extent, cuts, -0.22, 0.18) if cuts else 1.0
    values = jax.random.normal(key, extent, jnp.float32) * scale * loudness
    return jnp.minimum(jnp.maximum(values, -limit), limit).astype(kind)


def setup_inputs(seed: int = 0) -> dict:
    arg_keys = jax.random.split(jax.random.key(seed), 26)
    token_ids = touch_ends(ranked(arg_keys[0], (SEQS, LEN), VOCAB, 2), jax.random.fold_in(arg_keys[0], 3), 0, VOCAB - 1).astype(jnp.int32)
    segment_ids = jax.vmap(lambda own: jnp.searchsorted(jnp.cumsum(ragged_sizes(own, max(8, LEN // 64), LEN, LEN // 4, 1)), jnp.arange(LEN), side="right"))(jax.random.split(arg_keys[1], SEQS)).reshape((SEQS, LEN)).astype(jnp.int32)
    real_mask = draw_real_mask(jax.random.fold_in(arg_keys[25], 71), 0)
    positions = touch_ends(jax.random.randint(arg_keys[3], (SEQS, POS), 0, LEN), jax.random.fold_in(arg_keys[3], 1), 0, LEN - 1).astype(jnp.int32)
    targets = touch_ends(ranked(arg_keys[4], (SEQS, POS), VOCAB, 2), jax.random.fold_in(arg_keys[4], 3), 0, VOCAB - 1).astype(jnp.int32)
    teacher_states = centred(arg_keys[5], (SEQS, LEN, D), 1.0, 6.0, ((0, 32),))
    head_gate = jnp.clip(jax.random.uniform(arg_keys[6], (LAYERS, H), jnp.float32, 0.2, 1.0), 0.2, 1.0)
    layer_gate = jnp.clip(jax.random.uniform(arg_keys[7], (LAYERS, 2), jnp.float32, 0.5, 1.0), 0.5, 1.0)
    hidden_gate = jnp.clip(jax.random.uniform(arg_keys[8], (D,), jnp.float32, 0.3, 1.0), 0.3, 1.0)
    unit_gate = jnp.clip(jax.random.uniform(arg_keys[9], (LAYERS, FF), jnp.float32, 0.2, 1.0), 0.2, 1.0)
    unit_keep = touch_ends((jax.random.randint(arg_keys[10], (LAYERS, FF), 0, 4) < 3).astype(jnp.int32), jax.random.fold_in(arg_keys[10], 1), 0, 1)
    embedding = draw_embedding(jax.random.fold_in(arg_keys[25], 71), 0)
    attention = centred(arg_keys[12], (LAYERS, 4, D, D), D ** -0.5, 0.21875, (), jnp.float32)
    feed_forward = centred(arg_keys[13], (LAYERS, 2, FF, D), D ** -0.5, 0.21875, ((2, 8),), jnp.float32)
    map_weight = centred(arg_keys[14], (D, D), D ** -0.5, 0.21875, (), jnp.float32)
    norm_params = jnp.clip(1.0 + 0.1 * jax.random.normal(arg_keys[15], (NV, D), jnp.float32), 0.5, 1.5)
    embedding_rows = jnp.clip(jnp.exp(math.log(2.7450711842513797e-11) - 2.7725887 * jax.random.uniform(arg_keys[16], (VOCAB,), jnp.float32) ** steps_of(arg_keys[16], (VOCAB,), ((0, 8),), -0.2, 0.2)), 1.7156694901571123e-12, 2.7450711842513797e-11)
    embedding_cols = jnp.clip(jnp.exp(jax.random.uniform(arg_keys[17], (D,), jnp.float32, math.log(4.289173725392781e-13), math.log(6.862677960628449e-12))), 4.289173725392781e-13, 6.862677960628449e-12)
    attention_rows = jnp.clip(jnp.exp(math.log(2.7450711842513797e-11) - 2.7725887 * jax.random.uniform(arg_keys[18], (LAYERS, 4, D), jnp.float32) ** steps_of(arg_keys[18], (LAYERS, 4, D), ((2, 8),), -0.2, 0.2)), 1.7156694901571123e-12, 2.7450711842513797e-11)
    attention_cols = jnp.clip(jnp.exp(jax.random.uniform(arg_keys[19], (LAYERS, 4, D), jnp.float32, math.log(1.7156694901571123e-12), math.log(2.7450711842513797e-11))), 1.7156694901571123e-12, 2.7450711842513797e-11)
    feed_rows = jnp.clip(jnp.exp(math.log(2.7450711842513797e-11) - 2.7725887 * jax.random.uniform(arg_keys[20], (LAYERS, 2, FF), jnp.float32) ** steps_of(arg_keys[20], (LAYERS, 2, FF), ((2, 8),), -0.2, 0.2)), 1.7156694901571123e-12, 2.7450711842513797e-11)
    feed_cols = jnp.clip(jnp.exp(jax.random.uniform(arg_keys[21], (LAYERS, 2, D), jnp.float32, math.log(1.7156694901571123e-12), math.log(2.7450711842513797e-11))), 1.7156694901571123e-12, 2.7450711842513797e-11)
    map_rows = jnp.clip(jnp.exp(math.log(2.7450711842513797e-11) - 2.7725887 * jax.random.uniform(arg_keys[22], (D,), jnp.float32) ** steps_of(arg_keys[22], (D,), ((0, 8),), -0.2, 0.2)), 1.7156694901571123e-12, 2.7450711842513797e-11)
    map_cols = jnp.clip(jnp.exp(jax.random.uniform(arg_keys[23], (D,), jnp.float32, math.log(1.7156694901571123e-12), math.log(2.7450711842513797e-11))), 1.7156694901571123e-12, 2.7450711842513797e-11)
    norm_moment = jnp.clip(jnp.exp(jax.random.uniform(arg_keys[24], (NV, D), jnp.float32, math.log(2.7450711842513797e-11), math.log(4.3463627141804295e-10))), 2.7450711842513797e-11, 4.3463627141804295e-10)
    return {"token_ids": token_ids, "segment_ids": segment_ids, "real_mask": real_mask, "positions": positions, "targets": targets, "teacher_states": teacher_states, "head_gate": head_gate, "layer_gate": layer_gate, "hidden_gate": hidden_gate, "unit_gate": unit_gate, "unit_keep": unit_keep, "embedding": embedding, "attention": attention, "feed_forward": feed_forward, "map_weight": map_weight, "norm_params": norm_params, "embedding_rows": embedding_rows, "embedding_cols": embedding_cols, "attention_rows": attention_rows, "attention_cols": attention_cols, "feed_rows": feed_rows, "feed_cols": feed_cols, "map_rows": map_rows, "map_cols": map_cols, "norm_moment": norm_moment}


@jax.custom_vjp
def low(v):
    return lax.optimization_barrier(v.astype(jnp.bfloat16)).astype(jnp.float32)

@jax.custom_vjp
def low_back(v):
    return v

def low_keep(v):
    return (low(v), None)

def low_pass(kept, grad):
    return (grad,)

def back_keep(v):
    return (v, None)

def back_low(kept, grad):
    return (low(grad),)
low.defvjp(low_keep, low_pass)
low_back.defvjp(back_keep, back_low)
LN_EPS = 1e-06
ADA_EPS = 1e-30
DECAY_RATE = 0.95
LEARN_RATE = 0.015
CLIP_LIMIT = 0.05
MASK_FILL = 1e+30
PRECISE = lax.Precision.HIGHEST

def round_both(value):
    return low_back(low(value))

def layer_norm(value, gain, shift):
    middle = lax.optimization_barrier(jnp.mean(value, axis=-1, keepdims=True))
    centered = value - middle
    spread = lax.optimization_barrier(jnp.mean(centered * centered, axis=-1, keepdims=True))
    return centered * lax.rsqrt(spread + LN_EPS) * gain + shift

def block_loss(params, fixed_inputs, batch_data):
    embedding, attention, feed_forward, map_weight, norm_params = params
    head_gate, layer_gate, hidden_gate, unit_scale, count = fixed_inputs
    token_ids, segment_ids, real_rows, positions, targets, teacher = batch_data
    seq_count = token_ids.shape[0]
    table_low = low(embedding)
    hidden = layer_norm(table_low[token_ids], norm_params[0], norm_params[1]) * hidden_gate
    places = jnp.arange(LEN)
    allowed = (segment_ids[:, :, None] == segment_ids[:, None, :]) & ((real_rows[:, None, :] > 0.5) | (places[:, None] == places[None, :])[None])
    score_scale = 1.0 / math.sqrt(HD)
    for layer_at in range(LAYERS):
        weights = low(attention[layer_at])
        hidden_low = low(hidden)
        projected = round_both(jnp.einsum('nld,jde->jnle', hidden_low, weights[:3], precision=PRECISE))
        query = projected[0].reshape(seq_count, LEN, H, HD)
        keys = projected[1].reshape(seq_count, LEN, H, HD)
        values = projected[2].reshape(seq_count, LEN, H, HD)
        scores = low_back(jnp.einsum('nqhd,nkhd->nhqk', query, keys, precision=PRECISE) * score_scale)
        scores = jnp.where(allowed[:, None], scores, -MASK_FILL)
        probability = low(jax.nn.softmax(scores, axis=-1))
        mixed = low_back(jnp.einsum('nhqk,nkhd->nqhd', probability, values, precision=PRECISE)).reshape(seq_count, LEN, D)
        gated_low = low(mixed * jnp.repeat(head_gate[layer_at], HD))
        branch = low_back(jnp.einsum('nld,de->nle', gated_low, weights[3], precision=PRECISE))
        hidden = layer_norm(hidden + branch * layer_gate[layer_at, 0] * hidden_gate, norm_params[2 + 4 * layer_at], norm_params[3 + 4 * layer_at])
        unit_weights = low(feed_forward[layer_at])
        pre_act = low_back(jnp.einsum('nld,fd->nlf', low(hidden), unit_weights[0], precision=PRECISE))
        activated = low(jax.nn.gelu(pre_act, approximate=False) * unit_scale[layer_at])
        result = low_back(jnp.einsum('nlf,fd->nld', activated, unit_weights[1], precision=PRECISE))
        hidden = layer_norm(hidden + result * layer_gate[layer_at, 1] * hidden_gate, norm_params[4 + 4 * layer_at], norm_params[5 + 4 * layer_at])
    final = low(hidden)
    mapped = low_back(jnp.einsum('nld,de->nle', final, low(map_weight), precision=PRECISE))
    diff = mapped - teacher
    squared_error = jnp.sum(lax.optimization_barrier(jnp.sum(diff * diff, axis=-1)) * real_rows) / D
    picked = jnp.take_along_axis(final, positions[:, :, None], axis=1)
    logits = low_back(jnp.einsum('npd,vd->npv', picked, table_low, precision=PRECISE))
    log_total = jax.nn.logsumexp(logits, axis=-1)
    target_logit = jnp.take_along_axis(logits, targets[:, :, None], axis=2)[:, :, 0]
    return (squared_error + jnp.sum(log_total - target_logit)) / count

def factored(weight, gradient, row_stats, col_stats):
    squares = gradient * gradient + ADA_EPS
    new_rows = DECAY_RATE * row_stats + (1 - DECAY_RATE) * lax.optimization_barrier(jnp.mean(squares, axis=-1))
    new_cols = DECAY_RATE * col_stats + (1 - DECAY_RATE) * lax.optimization_barrier(jnp.mean(squares, axis=-2))
    second = new_rows[..., :, None] * new_cols[..., None, :] / lax.optimization_barrier(jnp.mean(new_rows, axis=-1))[..., None, None]
    return (weight - LEARN_RATE * gradient * lax.rsqrt(second), new_rows, new_cols)

def reference(token_ids, segment_ids, real_mask, positions, targets, teacher_states, head_gate, layer_gate, hidden_gate, unit_gate, unit_keep, embedding, attention, feed_forward, map_weight, norm_params, embedding_rows, embedding_cols, attention_rows, attention_cols, feed_rows, feed_cols, map_rows, map_cols, norm_moment):
    count = jnp.sum(real_mask).astype(jnp.float32)
    unit_scale = unit_gate * unit_keep.astype(jnp.float32)
    teacher = teacher_states.astype(jnp.float32).reshape(N_DP, N_UNIT, SEQ_DEV, LEN, D)
    teacher = jnp.roll(teacher, -(N_UNIT // 2), axis=1).reshape(SEQS, LEN, D)
    per_block = math.gcd(SEQS, max(1, 4096 // LEN))

    def to_blocks(value):
        return value.reshape((SEQS // per_block, per_block) + value.shape[1:])
    batch_data = (to_blocks(token_ids), to_blocks(segment_ids), to_blocks(real_mask.astype(jnp.float32)), to_blocks(positions), to_blocks(targets), to_blocks(teacher))
    fixed_inputs = (head_gate, layer_gate, hidden_gate, unit_scale, count)
    params = (embedding, attention, feed_forward, map_weight, norm_params)

    def summed_loss(weights_all):
        checked = jax.checkpoint(lambda inner, blocks: block_loss(inner, fixed_inputs, blocks))

        def scan_step(running, blocks):
            return (running + checked(weights_all, blocks), None)
        running, _ = lax.scan(scan_step, jnp.zeros((), jnp.float32), batch_data)
        return running
    mean_loss, pullback = jax.vjp(summed_loss, params)
    total_loss = mean_loss * count
    gradients = pullback(jnp.ones((), jnp.float32))[0]
    grad_norm = jnp.sqrt(sum((jnp.sum(grad_part * grad_part) for grad_part in gradients)))
    clip_factor = jnp.minimum(1.0, CLIP_LIMIT / grad_norm)
    embedding_grad, attention_grad, feed_grad, map_grad, norm_grad = [grad_part * clip_factor for grad_part in gradients]
    new_embedding, new_embedding_rows, new_embedding_cols = factored(embedding, embedding_grad, embedding_rows, embedding_cols)
    new_attention, new_attention_rows, new_attention_cols = factored(attention, attention_grad, attention_rows, attention_cols)
    new_feed_forward, new_feed_rows, new_feed_cols = factored(feed_forward, feed_grad, feed_rows, feed_cols)
    new_map, new_map_rows, new_map_cols = factored(map_weight, map_grad, map_rows, map_cols)
    new_norm_moment = DECAY_RATE * norm_moment + (1 - DECAY_RATE) * (norm_grad * norm_grad + ADA_EPS)
    new_norm_params = norm_params - LEARN_RATE * norm_grad * lax.rsqrt(new_norm_moment)
    return (total_loss, count, grad_norm, new_embedding, embedding_grad, new_embedding_rows, new_embedding_cols, new_attention, attention_grad, new_attention_rows, new_attention_cols, new_feed_forward, feed_grad, new_feed_rows, new_feed_cols, new_map, map_grad, new_map_rows, new_map_cols, new_norm_params, norm_grad, new_norm_moment)
```

```python
import functools
import math

import jax
import jax.numpy as jnp
from jax import lax
from jax.experimental import pallas as pl
from jax.experimental.pallas import tpu as pltpu
from jax.sharding import PartitionSpec as P

H = 12
HD = 64
PAIR = 2 * HD
KEY_BLOCK = 128
QUERY_BLOCK = 256
ROW_BLOCK = 512
UNIT_BLOCK = 768

LN_EPS = 1e-06
ADA_EPS = 1e-30
DECAY_RATE = 0.95
LEARN_RATE = 0.015
CLIP_LIMIT = 0.05
MASK_FILL = 1e30

B = jnp.bfloat16
F = jnp.float32
NT = (((1,), (1,)), ((), ()))
TN = (((0,), (0,)), ((), ()))
TT = (((0,), (1,)), ((), ()))
VMEM_MOST = 58 * 2**20


def dot(left, right):
    return jnp.dot(left, right, preferred_element_type=F)


def contract(left, right, dims):
    return lax.dot_general(left, right, dims, preferred_element_type=F)


def query_windows(segments, block):
    first = segments[::block]
    last = segments[block - 1 :: block]
    start = jnp.sum((segments[None, :] < first[:, None]).astype(jnp.int32), axis=1)
    stop = jnp.sum((segments[None, :] <= last[:, None]).astype(jnp.int32), axis=1)
    low = start // KEY_BLOCK
    high = (stop + KEY_BLOCK - 1) // KEY_BLOCK
    return jnp.concatenate([low, high - low]).astype(jnp.int32)


def most_blocks(length, block):
    return min(length // KEY_BLOCK, block // KEY_BLOCK + 4)


def window_mask(segk_ref, segq_ref, start, width, first_query, block):
    key_seg = segk_ref[pl.ds(start, width), :]
    if block > KEY_BLOCK:
        key_seg = jnp.concatenate([key_seg] * (block // KEY_BLOCK), axis=1)
    query_seg = segq_ref[0:1, pl.ds(first_query, block)]
    key_at = start + lax.broadcasted_iota(jnp.int32, (width, block), 0)
    query_at = first_query + lax.broadcasted_iota(jnp.int32, (width, block), 1)
    return (key_seg == query_seg) | (key_at == query_at)


def head_rows(block, head):
    empty = jnp.zeros((HD, block.shape[1]), block.dtype)
    parts = [block[:HD], empty] if head == 0 else [empty, block[HD:]]
    return jnp.concatenate(parts, axis=0)


def head_lanes(block):
    lane = lax.broadcasted_iota(jnp.int32, block.shape, 1)
    empty = jnp.zeros_like(block)
    return jnp.concatenate(
        [jnp.where(lane < HD, block, empty), jnp.where(lane < HD, empty, block)], axis=0
    )


def attend_kernel(
    window_ref, gate_ref, k_ref, qt_ref, vt_ref, segk_ref, segq_ref, ot_ref, lse_ref, *, block
):
    pair = pl.program_id(0)
    length = k_ref.shape[1]
    count = length // block
    lse_ref[...] = jnp.zeros_like(lse_ref)
    for i in range(count):
        low = window_ref[i]
        number = window_ref[count + i]
        columns = pl.ds(i * block, block)
        for n in range(1, most_blocks(length, block) + 1):

            @pl.when(number == n)
            def _():
                width = n * KEY_BLOCK
                start = pl.multiple_of(low * KEY_BLOCK, KEY_BLOCK)
                keys = k_ref[0, pl.ds(start, width), :]
                mask = window_mask(segk_ref, segq_ref, start, width, i * block, block)
                queries = qt_ref[0, :, columns]
                for head in range(2):
                    rows = slice(head * HD, (head + 1) * HD)
                    scores = jnp.where(mask, dot(keys, head_rows(queries, head)), -MASK_FILL)
                    top = jnp.max(scores, axis=0, keepdims=True)
                    exponent = jnp.exp(scores - top)
                    total = jnp.sum(exponent, axis=0, keepdims=True)
                    mixed = dot(vt_ref[0, rows, pl.ds(start, width)], exponent.astype(B))
                    gated = mixed * (gate_ref[2 * pair + head] / total)
                    ot_ref[rows, columns] = gated.astype(B)
                    lse_ref[0, head : head + 1, columns] = top + jnp.log(total)


def attend(windows, gates, tokens, features, key_segments, query_segments):
    _, length, breadth = tokens.shape
    pairs = breadth // PAIR
    return pl.pallas_call(
        functools.partial(attend_kernel, block=QUERY_BLOCK),
        grid_spec=pltpu.PrefetchScalarGridSpec(
            num_scalar_prefetch=2,
            grid=(pairs,),
            in_specs=[
                pl.BlockSpec((1, length, PAIR), lambda p, *_: (1, 0, p)),
                pl.BlockSpec((1, PAIR, length), lambda p, *_: (0, p, 0)),
                pl.BlockSpec((1, PAIR, length), lambda p, *_: (2, p, 0)),
                pl.BlockSpec((length, KEY_BLOCK), lambda p, *_: (0, 0)),
                pl.BlockSpec((8, length), lambda p, *_: (0, 0)),
            ],
            out_specs=[
                pl.BlockSpec((PAIR, length), lambda p, *_: (p, 0)),
                pl.BlockSpec((1, 8, length), lambda p, *_: (p, 0, 0)),
            ],
        ),
        out_shape=[
            jax.ShapeDtypeStruct((breadth, length), B),
            jax.ShapeDtypeStruct((pairs, 8, length), F),
        ],
        compiler_params=pltpu.CompilerParams(vmem_limit_bytes=VMEM_MOST),
        cost_estimate=pl.CostEstimate(
            flops=2 * 2 * 2 * length * 512 * breadth,
            bytes_accessed=8 * length * breadth,
            transcendentals=length * 512 * 12,
        ),
        name="attend",
    )(windows, gates, tokens, features, features, key_segments, query_segments)


def attend_back_kernel(
    window_ref,
    k_ref,
    kt_ref,
    q_ref,
    qt_ref,
    v_ref,
    do_ref,
    dot_ref,
    segk_ref,
    segq_ref,
    lse_ref,
    grad_ref,
    dq_sum,
    dk_sum,
    dv_sum,
    *,
    block,
    score_scale,
):
    length = k_ref.shape[1]
    count = length // block
    dk_sum[...] = jnp.zeros_like(dk_sum)
    dv_sum[...] = jnp.zeros_like(dv_sum)
    for i in range(count):
        low = window_ref[i]
        number = window_ref[count + i]
        columns = pl.ds(i * block, block)
        for n in range(1, most_blocks(length, block) + 1):

            @pl.when(number == n)
            def _():
                width = n * KEY_BLOCK
                start = pl.multiple_of(low * KEY_BLOCK, KEY_BLOCK)
                window = pl.ds(start, width)
                keys = k_ref[0, window, :]
                values = v_ref[0, window, :]
                mask = window_mask(segk_ref, segq_ref, start, width, i * block, block)
                queries_t = qt_ref[0, :, columns]
                grads_t = dot_ref[:, columns]
                all_prob = []
                all_grad = []
                for head in range(2):
                    rows = slice(head * HD, (head + 1) * HD)
                    scores = jnp.where(mask, dot(keys, head_rows(queries_t, head)), -MASK_FILL)
                    prob = jnp.exp(scores - lse_ref[0, head : head + 1, columns])
                    weighted = prob * dot(values, head_rows(grads_t, head))
                    inner = jnp.sum(weighted, axis=0, keepdims=True)
                    grad = (weighted - prob * inner).astype(B)
                    dq_sum[rows, columns] = dot(kt_ref[0, rows, window], grad) * score_scale
                    all_prob.append(prob.astype(B))
                    all_grad.append(grad)
                dv_sum[window, :] += dot(
                    jnp.concatenate(all_prob, axis=1), head_lanes(do_ref[columns, :])
                )
                dk_sum[window, :] += dot(
                    jnp.concatenate(all_grad, axis=1), head_lanes(q_ref[0, columns, :])
                )

    grad_ref[0] = jnp.transpose(dq_sum[...]).astype(B)
    grad_ref[1] = dk_sum[...].astype(B)
    grad_ref[2] = dv_sum[...].astype(B)


def attend_back(
    windows, tokens, features, grads, grads_t, key_segments, query_segments, log_total
):
    _, length, breadth = tokens.shape
    pairs = breadth // PAIR

    def token_spec(which):
        return pl.BlockSpec((1, length, PAIR), lambda p, *_: (which, 0, p))

    def feature_spec(which):
        return pl.BlockSpec((1, PAIR, length), lambda p, *_: (which, p, 0))

    return pl.pallas_call(
        functools.partial(
            attend_back_kernel, block=QUERY_BLOCK, score_scale=1.0 / math.sqrt(HD)
        ),
        grid_spec=pltpu.PrefetchScalarGridSpec(
            num_scalar_prefetch=1,
            grid=(pairs,),
            in_specs=[
                token_spec(1),
                feature_spec(1),
                token_spec(0),
                feature_spec(0),
                token_spec(2),
                pl.BlockSpec((length, PAIR), lambda p, *_: (0, p)),
                pl.BlockSpec((PAIR, length), lambda p, *_: (p, 0)),
                pl.BlockSpec((length, KEY_BLOCK), lambda p, *_: (0, 0)),
                pl.BlockSpec((8, length), lambda p, *_: (0, 0)),
                pl.BlockSpec((1, 8, length), lambda p, *_: (p, 0, 0)),
            ],
            out_specs=pl.BlockSpec((3, length, PAIR), lambda p, *_: (0, 0, p)),
            scratch_shapes=[
                pltpu.VMEM((PAIR, length), F),
                pltpu.VMEM((length, PAIR), F),
                pltpu.VMEM((length, PAIR), F),
            ],
        ),
        out_shape=jax.ShapeDtypeStruct((3, length, breadth), B),
        compiler_params=pltpu.CompilerParams(vmem_limit_bytes=VMEM_MOST),
        cost_estimate=pl.CostEstimate(
            flops=5 * 2 * 2 * length * 512 * breadth,
            bytes_accessed=20 * length * breadth,
            transcendentals=length * 512 * 12,
        ),
        name="attend_back",
    )(
        windows,
        tokens,
        features,
        tokens,
        features,
        tokens,
        grads,
        grads_t,
        key_segments,
        query_segments,
        log_total,
    )


def project_kernel(x_ref, weight_ref, tokens_ref, features_ref, *, score_scale):
    scale = jnp.where(pl.program_id(0) == 0, score_scale, 1.0).astype(F)
    tokens = dot(x_ref[...], weight_ref[...]).astype(B).astype(F)
    tokens_ref[0] = (tokens * scale).astype(B)
    features = contract(weight_ref[...], x_ref[...], TT).astype(B).astype(F)
    features_ref[0] = (features * scale).astype(B)


def project(x, weights, layer):
    length, breadth = x.shape
    return pl.pallas_call(
        functools.partial(project_kernel, score_scale=1.0 / math.sqrt(HD)),
        grid=(3,),
        in_specs=[
            pl.BlockSpec((length, breadth), lambda j: (0, 0)),
            pl.BlockSpec((None, None, breadth, breadth), lambda j: (layer, j, 0, 0)),
        ],
        out_specs=[
            pl.BlockSpec((1, length, breadth), lambda j: (j, 0, 0)),
            pl.BlockSpec((1, breadth, length), lambda j: (j, 0, 0)),
        ],
        out_shape=[
            jax.ShapeDtypeStruct((3, length, breadth), B),
            jax.ShapeDtypeStruct((3, breadth, length), B),
        ],
        compiler_params=pltpu.CompilerParams(vmem_limit_bytes=VMEM_MOST),
        cost_estimate=pl.CostEstimate(
            flops=12 * length * breadth * breadth,
            bytes_accessed=14 * length * breadth + 6 * breadth * breadth,
            transcendentals=0,
        ),
        name="project",
    )(x, weights)


def gelu_and_slope(value):
    density = jnp.exp(value * value * -0.5)
    ratio = pl.reciprocal(1.0 + jnp.abs(value) * (0.3275911 * math.sqrt(0.5)))
    series = ratio * (
        0.127414796
        + ratio
        * (-0.142248368 + ratio * (0.7107068705 + ratio * (-0.7265760135 + ratio * 0.5307027145)))
    )
    tail = series * density
    below = jnp.where(value >= 0, 1.0 - tail, tail)
    return value * below, below + value * density * (1.0 / math.sqrt(2.0 * math.pi))


def feed_kernel(x_ref, up_ref, down_ref, scale_ref, act_ref, slope_ref, out_ref):
    first = pl.program_id(0) == 0
    scale = scale_ref[0]
    act, slope = gelu_and_slope(contract(x_ref[...], up_ref[...], NT))
    act = (act * scale).astype(B)
    act_ref[...] = act
    slope_ref[...] = (slope * scale).astype(B)
    part = dot(act, down_ref[...])

    @pl.when(first)
    def _():
        out_ref[...] = part

    @pl.when(jnp.logical_not(first))
    def _():
        out_ref[...] += part


def feed(x, weights, scale):
    length, breadth = x.shape
    units = weights.shape[1]
    block = UNIT_BLOCK
    return pl.pallas_call(
        feed_kernel,
        grid=(units // block,),
        in_specs=[
            pl.BlockSpec((length, breadth), lambda j: (0, 0)),
            pl.BlockSpec((None, block, breadth), lambda j: (0, j, 0)),
            pl.BlockSpec((None, block, breadth), lambda j: (1, j, 0)),
            pl.BlockSpec((1, 1, block), lambda j: (0, 0, j)),
        ],
        out_specs=[
            pl.BlockSpec((length, block), lambda j: (0, j)),
            pl.BlockSpec((length, block), lambda j: (0, j)),
            pl.BlockSpec((length, breadth), lambda j: (0, 0)),
        ],
        out_shape=[
            jax.ShapeDtypeStruct((length, units), B),
            jax.ShapeDtypeStruct((length, units), B),
            jax.ShapeDtypeStruct((length, breadth), F),
        ],
        compiler_params=pltpu.CompilerParams(vmem_limit_bytes=VMEM_MOST),
        cost_estimate=pl.CostEstimate(
            flops=4 * length * breadth * units,
            bytes_accessed=4 * (length + breadth) * units + 6 * length * breadth,
            transcendentals=2 * length * units,
        ),
        name="feed",
    )(x, weights, weights, scale.reshape(1, 1, units))


def feed_back_kernel(
    grad_ref, x_ref, act_ref, slope_ref, up_ref, down_ref, out_ref, owned_ref, pre_grad
):
    first = pl.program_id(0) == 0
    grad_act = contract(grad_ref[...], down_ref[...], NT)
    grad_pre = (grad_act * slope_ref[...].astype(F)).astype(B)
    pre_grad[...] = grad_pre
    part = dot(grad_pre, up_ref[...])

    @pl.when(first)
    def _():
        out_ref[...] = part

    @pl.when(jnp.logical_not(first))
    def _():
        out_ref[...] += part

    grads = (
        contract(pre_grad[...], x_ref[...], TN).astype(B),
        contract(act_ref[...], grad_ref[...], TN).astype(B),
    )
    owners, _, share, _ = owned_ref.shape
    for which in range(2):
        for owner in range(owners):
            owned_ref[owner, which] = grads[which][owner * share : (owner + 1) * share]


def feed_back(grad, x, act, slope, weights, owners):
    length, breadth = x.shape
    units = weights.shape[1]
    share = units // owners
    block = UNIT_BLOCK
    lanes = pl.BlockSpec((length, block), lambda j: (0, j))
    whole = pl.BlockSpec((length, breadth), lambda j: (0, 0))
    return pl.pallas_call(
        feed_back_kernel,
        grid=(units // block,),
        in_specs=[
            whole,
            whole,
            lanes,
            lanes,
            pl.BlockSpec((None, block, breadth), lambda j: (0, j, 0)),
            pl.BlockSpec((None, block, breadth), lambda j: (1, j, 0)),
        ],
        out_specs=[
            whole,
            pl.BlockSpec((block // share, 2, share, breadth), lambda j: (j, 0, 0, 0)),
        ],
        scratch_shapes=[pltpu.VMEM((length, block), B)],
        out_shape=[
            jax.ShapeDtypeStruct((length, breadth), F),
            jax.ShapeDtypeStruct((owners, 2, share, breadth), B),
        ],
        compiler_params=pltpu.CompilerParams(vmem_limit_bytes=VMEM_MOST),
        cost_estimate=pl.CostEstimate(
            flops=8 * length * breadth * units,
            bytes_accessed=4 * (length + 2 * breadth) * units + 8 * length * breadth,
            transcendentals=0,
        ),
        name="feed_back",
    )(grad, x, act, slope, weights, weights)


def scan_kernel(ids, place, found, ends, *, vocab):
    base = place[0]
    blocks = ends.shape[0]
    streams = math.gcd(blocks, 8)
    for first in range(0, blocks, streams):

        def scan(t, counts):
            after = []
            for k, count in enumerate(counts):
                at = (first + k) * ROW_BLOCK + t
                relative = (ids[at] - base).astype(jnp.uint32)
                found[count] = at
                after.append(count + jnp.where(relative < jnp.uint32(vocab), 1, 0))
            return tuple(after)

        begin = tuple(jnp.int32((first + k) * ROW_BLOCK) for k in range(streams))
        counts = lax.fori_loop(0, ROW_BLOCK, scan, begin, unroll=4)
        for k, count in enumerate(counts):
            ends[first + k] = count


def scan_ids(ids, place, vocab):
    smem = pl.BlockSpec(memory_space=pltpu.SMEM)
    return pl.pallas_call(
        functools.partial(scan_kernel, vocab=vocab),
        in_specs=[smem, smem],
        out_specs=[smem, smem],
        out_shape=[
            jax.ShapeDtypeStruct(ids.shape, jnp.int32),
            jax.ShapeDtypeStruct((ids.shape[0] // ROW_BLOCK,), jnp.int32),
        ],
        name="scan_ids",
    )(ids, place)


def lookup_kernel(ids, place, found, ends, own, other, *rest, blocks, vocab):
    outs = rest[:blocks]
    table, rows, stage, table_sem, out_sem = rest[blocks:]
    base = place[0]
    core = place[1]
    mine = pl.multiple_of(core * vocab, 8)
    theirs = pl.multiple_of((1 - core) * vocab, 8)
    loads = [
        pltpu.make_async_copy(own, table.at[pl.ds(mine, vocab)], table_sem.at[0]),
        pltpu.make_async_copy(other, table.at[pl.ds(theirs, vocab)], table_sem.at[1]),
    ]
    for load in loads:
        load.start()
    for load in loads:
        load.wait()
    copies = [None, None]
    for k in range(blocks):
        rows[...] = jnp.zeros_like(rows)

        def put(entry, carry):
            t = found[entry]
            rows[pl.ds(t - k * ROW_BLOCK, 1), :] = table[pl.ds(ids[t] - base, 1), :]
            return carry

        each_entry(k * ROW_BLOCK, ends[k], put)
        slot = k % 2
        if copies[slot] is not None:
            copies[slot].wait()
        stage[slot] = rows[...].astype(B)
        copies[slot] = pltpu.make_async_copy(stage.at[slot], outs[k], out_sem.at[slot])
        copies[slot].start()
    for copy in copies:
        copy.wait()


def each_entry(low, high, body):
    quads = lax.div(high - low, 4)

    def four(e, carry):
        for j in range(4):
            body(low + e * 4 + j, 0)
        return carry

    lax.fori_loop(0, quads, four, 0)
    lax.fori_loop(low + quads * 4, high, body, 0)


def lookup(ids, place, found, ends, own, other):
    vocab, breadth = own.shape
    blocks = ids.shape[0] // ROW_BLOCK
    hbm = pl.BlockSpec(memory_space=pl.ANY)
    smem = pl.BlockSpec(memory_space=pltpu.SMEM)
    return pl.pallas_call(
        functools.partial(lookup_kernel, blocks=blocks, vocab=vocab),
        in_specs=[smem] * 4 + [hbm] * 2,
        out_specs=[hbm] * blocks,
        out_shape=[jax.ShapeDtypeStruct((ROW_BLOCK, breadth), B)] * blocks,
        scratch_shapes=[
            pltpu.VMEM((2 * vocab, breadth), F),
            pltpu.VMEM((ROW_BLOCK, breadth), F),
            pltpu.VMEM((2, ROW_BLOCK, breadth), B),
            pltpu.SemaphoreType.DMA((2,)),
            pltpu.SemaphoreType.DMA((2,)),
        ],
        compiler_params=pltpu.CompilerParams(vmem_limit_bytes=VMEM_MOST),
        cost_estimate=pl.CostEstimate(
            flops=0,
            bytes_accessed=8 * vocab * breadth + 2 * ids.shape[0] * breadth,
            transcendentals=0,
        ),
        name="lookup",
    )(ids, place, found, ends, own, other)


def spread_kernel(
    ids, other_ids, place, found, ends, other_found, other_ends, begin, *rest, pieces
):
    blocks = len(pieces)
    arrays = max(which for which, _ in pieces) + 1
    grads = [rest[which].at[pl.ds(at, ROW_BLOCK)] for which, at in pieces]
    out, total, rows, stage, half, sem, in_sem, out_sem = rest[arrays:]
    base = place[0]
    vocab = total.shape[0]
    fill = pltpu.make_async_copy(begin, total, sem.at[0])
    fill.start()

    def load(k):
        copy = pltpu.make_async_copy(grads[k], stage.at[k % 2], in_sem.at[k % 2])
        copy.start()
        return copy

    coming = load(0)
    fill.wait()
    for k in range(blocks):
        coming.wait()
        if k + 1 < blocks:
            coming = load(k + 1)
        rows[...] = stage[k % 2].astype(F)

        lists = (ids, found, ends) if k < blocks // 2 else (other_ids, other_found, other_ends)
        first = k % (blocks // 2) * ROW_BLOCK

        def add(entry, carry):
            t = lists[1][entry]
            at = pl.ds(lists[0][t] - base, 1)
            total[at, :] += rows[pl.ds(t - first, 1), :]
            return carry

        each_entry(first, lists[2][k % (blocks // 2)], add)
    step = half.shape[1]
    copies = [None, None]
    for j in range(vocab // step):
        slot = j % 2
        if copies[slot] is not None:
            copies[slot].wait()
        half[slot] = total[j * step : (j + 1) * step, :].astype(B)
        copies[slot] = pltpu.make_async_copy(
            half.at[slot], out.at[pl.ds(j * step, step)], out_sem.at[slot]
        )
        copies[slot].start()
    for copy in copies:
        copy.wait()


def spread(ids, other_ids, place, lists, begin, grads):
    vocab, breadth = begin.shape
    arrays = []
    pieces = []
    for array, at in grads:
        known = [k for k, other in enumerate(arrays) if other is array]
        if not known:
            known = [len(arrays)]
            arrays.append(array)
        pieces.append((known[0], at))
    hbm = pl.BlockSpec(memory_space=pl.ANY)
    smem = pl.BlockSpec(memory_space=pltpu.SMEM)
    return pl.pallas_call(
        functools.partial(spread_kernel, pieces=tuple(pieces)),
        in_specs=[smem] * 7 + [hbm] * (1 + len(arrays)),
        out_specs=hbm,
        out_shape=jax.ShapeDtypeStruct((vocab, breadth), B),
        scratch_shapes=[
            pltpu.VMEM((vocab, breadth), F),
            pltpu.VMEM((ROW_BLOCK, breadth), F),
            pltpu.VMEM((2, ROW_BLOCK, breadth), B),
            pltpu.VMEM((2, vocab // 4, breadth), B),
            pltpu.SemaphoreType.DMA((1,)),
            pltpu.SemaphoreType.DMA((2,)),
            pltpu.SemaphoreType.DMA((2,)),
        ],
        compiler_params=pltpu.CompilerParams(vmem_limit_bytes=VMEM_MOST),
        cost_estimate=pl.CostEstimate(
            flops=0,
            bytes_accessed=6 * vocab * breadth + 2 * len(grads) * ROW_BLOCK * breadth,
            transcendentals=0,
        ),
        name="spread",
    )(ids, other_ids, place, *lists, begin, *arrays)


def stats_kernel(small_ref, row_sums_ref, embed_ref, *rest, layers):
    attn = rest[:layers]
    feeds = rest[layers : 2 * layers]
    out_ref = rest[2 * layers]
    norms = small_ref.shape[0]
    cols = jnp.sum(jnp.square(embed_ref[...].astype(F)), axis=0, keepdims=True)

    @pl.when(pl.program_id(0) == 0)
    def _():
        def put(row, value):
            out_ref[row : row + 1, :] = jnp.sum(
                jnp.square(value.astype(F)), axis=0, keepdims=True
            )

        out_ref[:norms, :] = small_ref[...]
        row = norms
        for parts, count in ((attn, 4), (feeds, 2)):
            for part in parts:
                for k in range(count):
                    put(row, part[k])
                    row += 1
        put(row, attn[layers - 1][4])
        out_ref[row + 1 : row + 2, :] = cols
        row += 2
        out_ref[row : row + 1, :] = row_sums_ref[...]

    @pl.when(pl.program_id(0) > 0)
    def _():
        at = norms + 6 * layers + 1
        out_ref[at : at + 1, :] += cols


def stats(small, row_sums, embed, attn, feeds):
    height, breadth = embed.shape
    block = math.gcd(height, 480)
    rows = small.shape[0] + 3 + 6 * len(attn)
    vmem = pl.BlockSpec(memory_space=pltpu.VMEM)
    return pl.pallas_call(
        functools.partial(stats_kernel, layers=len(attn)),
        grid=(height // block,),
        in_specs=[vmem, vmem, pl.BlockSpec((block, breadth), lambda j: (j, 0))]
        + [vmem] * (2 * len(attn)),
        out_specs=pl.BlockSpec((rows, breadth), lambda j: (0, 0)),
        out_shape=jax.ShapeDtypeStruct((rows, breadth), F),
        compiler_params=pltpu.CompilerParams(vmem_limit_bytes=VMEM_MOST),
        name="stats",
    )(small, row_sums, embed, *attn, *feeds)


def factors_kernel(
    parts_ref,
    cols_ref,
    heights_ref,
    params_ref,
    moment_ref,
    scalars_ref,
    new_cols_ref,
    factor_ref,
    norm_grad_ref,
    new_params_ref,
    new_moment_ref,
):
    packed = parts_ref[0]
    for k in range(1, parts_ref.shape[0]):
        packed = packed + parts_ref[k]
    norms = params_ref.shape[0]
    mats, breadth = cols_ref.shape
    norm_grads = packed[:norms]
    col_sums = packed[norms + 1 : norms + 1 + mats]
    lane = lax.broadcasted_iota(jnp.int32, (mats, breadth), 1)
    row = lax.broadcasted_iota(jnp.int32, (mats, breadth), 0)
    row_sums = jnp.sum(
        jnp.where(lane == row, packed[norms + 1 + mats :], 0.0), axis=1, keepdims=True
    )
    heights = heights_ref[...]
    mat_sums = jnp.sum(col_sums, axis=1, keepdims=True)
    square = jnp.sum(mat_sums, axis=0, keepdims=True) + jnp.sum(
        jnp.sum(norm_grads * norm_grads, axis=1, keepdims=True), axis=0, keepdims=True
    )
    norm = jnp.sqrt(square)
    clip = jnp.minimum(1.0, CLIP_LIMIT / norm)
    scalars_ref[0] = packed[norms, 0]
    scalars_ref[1] = norm[0, 0]
    scalars_ref[2] = clip[0, 0]
    new_cols = DECAY_RATE * cols_ref[...] + (1 - DECAY_RATE) * (
        clip * clip * col_sums / heights + ADA_EPS
    )
    mean_rows = DECAY_RATE * row_sums / heights + (1 - DECAY_RATE) * (
        clip * clip * mat_sums / (heights * breadth) + ADA_EPS
    )
    new_cols_ref[...] = new_cols
    factor_ref[...] = LEARN_RATE * jnp.sqrt(mean_rows) * lax.rsqrt(new_cols)
    norm_grad = norm_grads * clip
    moment = DECAY_RATE * moment_ref[...] + (1 - DECAY_RATE) * (norm_grad * norm_grad + ADA_EPS)
    norm_grad_ref[...] = norm_grad
    new_moment_ref[...] = moment
    new_params_ref[...] = params_ref[...] - LEARN_RATE * norm_grad * lax.rsqrt(moment)


def factors(parts, cols, heights, params, moment):
    vmem = pl.BlockSpec(memory_space=pltpu.VMEM)
    like = [jax.ShapeDtypeStruct(x.shape, F) for x in (cols, cols, params, params, params)]
    return pl.pallas_call(
        factors_kernel,
        in_specs=[vmem] * 5,
        out_specs=[pl.BlockSpec(memory_space=pltpu.SMEM)] + [vmem] * 5,
        out_shape=[jax.ShapeDtypeStruct((3,), F)] + like,
        compiler_params=pltpu.CompilerParams(vmem_limit_bytes=VMEM_MOST),
        name="factors",
    )(parts, cols, heights, params, moment)


def renew_kernel(
    scalars_ref, at_ref, factor_ref, rows_ref, weight_ref, sum_ref, new_ref, grad_ref, new_rows_ref
):
    for m in range(sum_ref.shape[0]):
        grad = sum_ref[m].astype(F) * scalars_ref[2]
        mean = jnp.mean(grad * grad, axis=1, keepdims=True) + ADA_EPS
        new_rows = DECAY_RATE * rows_ref[m] + (1 - DECAY_RATE) * mean
        wide = jnp.broadcast_to(new_rows, (new_rows.shape[0], 128))
        new_rows_ref[m, 0] = jnp.transpose(wide)[:1]
        grad_ref[m] = grad
        new_ref[m] = weight_ref[m] - grad * lax.rsqrt(new_rows) * factor_ref[m]


def renew(scalars, at, factor, first, rows, weight, total, group, most):
    mats, height, breadth = total.shape
    block = math.gcd(height, most)
    per = height // block
    wide = pl.BlockSpec((group, block, breadth), lambda m, j, *_: (m, j, 0))
    new, grad, new_rows = pl.pallas_call(
        renew_kernel,
        grid_spec=pltpu.PrefetchScalarGridSpec(
            num_scalar_prefetch=2,
            grid=(mats // group, per),
            in_specs=[
                pl.BlockSpec((group, 1, breadth), lambda m, j, *_: (first // group + m, 0, 0)),
                pl.BlockSpec((group, block, 1), lambda m, j, *_: (m, j, 0)),
                pl.BlockSpec(
                    (group, block, breadth), lambda m, j, scalars, at: (m, at[0] * per + j, 0)
                ),
                wide,
            ],
            out_specs=[
                wide,
                wide,
                pl.BlockSpec((group, 1, 1, block), lambda m, j, *_: (m, j, 0, 0)),
            ],
        ),
        out_shape=[
            jax.ShapeDtypeStruct((mats, height, breadth), F),
            jax.ShapeDtypeStruct((mats, height, breadth), F),
            jax.ShapeDtypeStruct((mats, per, 1, block), F),
        ],
        compiler_params=pltpu.CompilerParams(vmem_limit_bytes=VMEM_MOST),
        name="renew",
    )(scalars, at, factor, rows[..., None], weight, total)
    return new, grad, new_rows.reshape(rows.shape)


def across(value, step):
    pairs = [(u, ((u // 2) ^ step) * 2 + u % 2) for u in range(lax.axis_size("unit"))]
    return lax.ppermute(value, "unit", pairs)


def swapped(value):
    return lax.ppermute(value, "unit", [(u, u ^ 1) for u in range(lax.axis_size("unit"))])


def gathered(value, beside_core, beside_chip):
    other, *beside_core = together(swapped(value), *beside_core)
    both = jnp.stack([value, other])
    chips = lax.axis_size("unit") // 2
    parts = [across(both, step) for step in range(1, chips)]
    if beside_chip:
        parts[0], *beside_chip = together(parts[0], *beside_chip(*beside_core))
    return jnp.stack([both] + parts), beside_core, beside_chip


def dp_scatter(value):
    size = lax.axis_size("dp")
    at = lax.axis_index("dp")
    share = value.shape[0] // size
    parts = [lax.dynamic_slice_in_dim(value, at * share, share, 0)]
    for step in range(1, size):
        away = lax.dynamic_slice_in_dim(value, (at + step) % size * share, share, 0)
        parts.append(lax.ppermute(away, "dp", [(d, (d + step) % size) for d in range(size)]))
    return parts


def dp_gather(parts):
    size = lax.axis_size("dp")
    at = lax.axis_index("dp")
    total = parts[0].astype(F)
    for part in parts[1:]:
        total = total + part.astype(F)
    total = total.astype(B)
    share = total.shape[0]
    found = [total] + [
        lax.ppermute(total, "dp", [(d, (d + step) % size) for d in range(size)])
        for step in range(1, size)
    ]
    return found, share, at, size


def dp_placed(found, share, at, size):
    result = jnp.zeros((size * share,) + found[0].shape[1:], found[0].dtype)
    for step, part in enumerate(found):
        result = lax.dynamic_update_slice_in_dim(result, part, (at - step) % size * share, 0)
    return result


def dp_sum(value):
    size = lax.axis_size("dp")
    if size & (size - 1):
        return lax.psum(value, "dp")
    step = 1
    while step < size:
        value = value + lax.ppermute(value, "dp", [(d, d ^ step) for d in range(size)])
        step = 2 * step
    return value


def together(*values):
    return lax.optimization_barrier(values)


def chip_sum(mine, swapped_theirs):
    return (mine.astype(F) + swapped_theirs.astype(F)).astype(B)


def sent_to_owners(total, chip, steps):
    return [
        across(lax.dynamic_index_in_dim(total, chip ^ step, 0, keepdims=False), step)
        for step in steps
    ]


def owner_total(total, received, chip):
    result = lax.dynamic_index_in_dim(total, chip, 0, keepdims=False).astype(F)
    for part in received:
        result = result + part.astype(F)
    return result.astype(B)


def rows_of_tokens(served, chips, beside, beside_last):
    halves = len(served[0])
    total = [part.astype(F) for part in served[0]]
    if chips != 4 or halves != 2:
        for step in range(1, chips):
            for k in range(halves):
                total[k] = total[k] + across(served[step][k], step).astype(F)
        return jnp.concatenate(total, axis=0), *beside, *beside_last()
    passing = [across(served[3][0], 2), across(served[3][1], 1)]
    direct = [across(served[2][0], 2), across(served[1][1], 1)]
    passing[0], passing[1], direct[0], direct[1], *beside = together(*passing, *direct, *beside)
    last = [
        across(served[1][0] + passing[0], 1),
        across(served[2][1] + passing[1], 2),
    ]
    last[0], last[1], *after = together(*last, *beside_last())
    total = [a + b.astype(F) + c.astype(F) for a, b, c in zip(total, direct, last)]
    return jnp.concatenate(total, axis=0), *beside, *after


def norm_forward(value, gain, shift):
    centered = value - jnp.mean(value, axis=-1, keepdims=True)
    inverse = lax.rsqrt(jnp.mean(centered * centered, axis=-1, keepdims=True) + LN_EPS)
    normed = centered * inverse
    return (normed * gain + shift, (normed, inverse))


def norm_backward(stored, gain, upstream):
    normed, inverse = stored
    scaled = upstream * gain
    inner = (
        scaled
        - jnp.mean(scaled, axis=-1, keepdims=True)
        - normed * jnp.mean(scaled * normed, axis=-1, keepdims=True)
    )
    return (inverse * inner, jnp.sum(upstream * normed, axis=0), jnp.sum(upstream, axis=0))


def local(
    token_ids,
    segment_ids,
    real_mask,
    positions,
    targets,
    teacher_states,
    head_gate,
    layer_gate,
    hidden_gate,
    unit_gate,
    unit_keep,
    embedding,
    attention,
    feed_forward,
    map_weight,
    norm_params,
    embedding_rows,
    embedding_cols,
    attention_rows,
    attention_cols,
    feed_rows,
    feed_cols,
    map_rows,
    map_cols,
    norm_moment,
):
    unit_count = lax.axis_size("unit")
    chips = unit_count // 2
    unit_at = lax.axis_index("unit")
    data_at = lax.axis_index("dp")
    chip = unit_at // 2
    core = unit_at % 2
    length = token_ids.shape[1]
    pick_count = positions.shape[1]
    breadth = embedding.shape[1]
    vocab_dev = embedding.shape[0]
    units_dev = feed_forward.shape[2]
    layer_count = attention.shape[0]
    slab_rows = breadth // unit_count
    group_first = data_at * unit_count
    place = jnp.stack([chip * 2 * vocab_dev, core]).astype(jnp.int32)

    other_table = swapped(embedding)
    all_ids = jnp.concatenate(
        [token_ids[0]] + [across(token_ids[0], step) for step in range(1, chips)]
    )
    found, ends = scan_ids(all_ids, place, 2 * vocab_dev)
    served = list(lookup(all_ids, place, found, ends, embedding, other_table))
    halves = length // ROW_BLOCK
    own_place = jnp.stack([unit_at * vocab_dev, core]).astype(jnp.int32)
    other_ids = swapped(all_ids)
    table_low = embedding.astype(B)
    attention_low = attention.astype(B)
    map_low = map_weight.astype(B)
    looked, *lows = rows_of_tokens(
        [served[step * halves : (step + 1) * halves] for step in range(chips)],
        chips,
        [table_low, attention_low, map_low, *scan_ids(all_ids, own_place, vocab_dev)],
        lambda: scan_ids(other_ids, own_place, vocab_dev),
    )
    table_low, attention_low, map_low, *lists = lows
    feed_low = []
    for layer_at in range(layer_count):
        own = feed_forward[layer_at].astype(B)
        if layer_at > 0:
            looked, own = together(looked, own)
        feed_low.append(lax.all_gather(own, "unit", axis=1, tiled=True))
    teacher = lax.ppermute(
        teacher_states[0],
        "unit",
        [(u, (u + unit_count // 2) % unit_count) for u in range(unit_count)],
    )
    real_row = lax.dynamic_index_in_dim(real_mask, group_first + unit_at, 0, keepdims=False)
    real_flat = real_row.astype(F)
    count = jnp.sum(real_mask).astype(F)
    scale_all = unit_gate * unit_keep.astype(F)
    segments = segment_ids[0]
    windows = query_windows(segments, QUERY_BLOCK)
    key_segments = jnp.broadcast_to(
        jnp.where(real_row > 0, segments, -1)[:, None], (length, KEY_BLOCK)
    )
    query_segments = jnp.broadcast_to(segments[None, :], (8, length))
    head_scale = jnp.repeat(head_gate, HD, axis=1)

    normed, embed_stored = norm_forward(looked, norm_params[0], norm_params[1])
    hidden = normed * hidden_gate
    stored_layers = []
    for layer_at in range(layer_count):
        hidden_low = hidden.astype(B)
        weights = attention_low[layer_at]
        tokens, features = project(hidden_low, attention_low, layer_at)
        gated_t, log_total = attend(
            windows, head_gate[layer_at], tokens, features, key_segments, query_segments
        )
        branch = jnp.einsum("dr,de->re", gated_t, weights[3], preferred_element_type=F)
        middle, norm_first = norm_forward(
            hidden + branch * layer_gate[layer_at, 0] * hidden_gate,
            norm_params[2 + 4 * layer_at],
            norm_params[3 + 4 * layer_at],
        )
        middle_low = middle.astype(B)
        act, slope, result = feed(middle_low, feed_low[layer_at], scale_all[layer_at])
        if layer_at == 0:
            result, teacher = together(result, teacher)
        hidden, norm_second = norm_forward(
            middle + result * layer_gate[layer_at, 1] * hidden_gate,
            norm_params[4 + 4 * layer_at],
            norm_params[5 + 4 * layer_at],
        )
        stored_layers.append(
            (
                (hidden_low, tokens, features, gated_t, log_total),
                norm_first,
                (middle_low, act, slope),
                norm_second,
            )
        )

    final = hidden.astype(B)
    pick_hot = (positions[0][:, None] == jnp.arange(length)[None, :]).astype(B)
    picked_own = dot(pick_hot, final).astype(B)

    def map_loss(mapped):
        diff = mapped - teacher.astype(F)
        error = jnp.sum(jnp.sum(diff * diff, axis=-1) * real_flat) / breadth
        return error, (diff * (2.0 / (breadth * count)) * real_flat[:, None]).astype(B)

    picked_rows, _, (error_part, grad_mapped) = gathered(
        picked_own, [dot(final, map_low)], map_loss
    )
    picked_rows = picked_rows.reshape(unit_count * pick_count, breadth)
    target_all = jnp.concatenate(
        [
            lax.dynamic_index_in_dim(targets, group_first + (unit_at ^ other), 0, keepdims=False)
            for other in range(unit_count)
        ]
    )
    logits = contract(picked_rows, table_low, NT)
    is_target = (target_all - unit_at * vocab_dev)[:, None] == jnp.arange(vocab_dev)[None, :]
    row_max = jnp.max(logits, axis=1)
    sum_exp = jnp.sum(jnp.exp(logits - row_max[:, None]), axis=1)
    target_logit = jnp.sum(jnp.where(is_target, logits, 0.0), axis=1)
    shares, (grad_map,), (grad_final,) = gathered(
        jnp.stack([row_max, sum_exp, target_logit]).reshape(3, unit_count, pick_count),
        [contract(final, grad_mapped, TN).astype(B)],
        lambda _: (contract(grad_mapped, map_low, NT),),
    )
    shares = shares.reshape(unit_count, 3, unit_count, pick_count)
    shares = jnp.stack(
        [
            jnp.stack([shares[a, :, a ^ b] for a in range(unit_count)])
            for b in range(unit_count)
        ],
        axis=2,
    ).reshape(unit_count, 3, unit_count * pick_count)
    top = jnp.max(shares[:, 0], axis=0)
    log_sum = top + jnp.log(jnp.sum(shares[:, 1] * jnp.exp(shares[:, 0] - top), axis=0))
    own_terms = (log_sum - jnp.sum(shares[:, 2], axis=0))[:pick_count]
    grad_logits = (
        (jnp.exp(logits - log_sum[:, None]) - is_target.astype(F)) / count
    ).astype(B)
    grad_parts = dot(grad_logits, table_low).reshape(chips, 2, pick_count, breadth)
    both = grad_parts[:, 0] + swapped(grad_parts[:, 1])
    grad_picked = both[0]
    for step in range(1, chips):
        grad_picked = grad_picked + across(both[step], step)
    grad_table = contract(grad_logits, picked_rows, TN)

    loss_part = error_part + jnp.sum(own_terms)
    grad_hidden = grad_final + lax.dot_general(
        pick_hot.astype(F),
        grad_picked,
        TN,
        precision=lax.Precision.HIGHEST,
        preferred_element_type=F,
    )

    gain_rows = [None] * norm_params.shape[0]
    feed_parts = [None] * layer_count
    attn_parts = [None] * layer_count
    for layer_at in reversed(range(layer_count)):
        attn_stored, norm_first, feed_stored, norm_second = stored_layers[layer_at]
        hidden_low, tokens, features, gated_t, log_total = attn_stored
        middle_low, act, slope = feed_stored
        weights = attention_low[layer_at]
        grad_second, gain_rows[4 + 4 * layer_at], gain_rows[5 + 4 * layer_at] = norm_backward(
            norm_second, norm_params[4 + 4 * layer_at], grad_hidden
        )
        grad_result = (grad_second * layer_gate[layer_at, 1] * hidden_gate).astype(B)
        if layer_at < layer_count - 1:
            grad_result, attn_owned = together(grad_result, attn_owned)
            attn_parts[layer_at + 1] = lax.psum_scatter(attn_owned, "unit")
        grad_middle, feed_owned = feed_back(
            grad_result, middle_low, act, slope, feed_low[layer_at], unit_count
        )
        feed_parts[layer_at] = lax.psum_scatter(feed_owned, "unit")
        grad_first, gain_rows[2 + 4 * layer_at], gain_rows[3 + 4 * layer_at] = norm_backward(
            norm_first, norm_params[2 + 4 * layer_at], grad_second + grad_middle
        )
        grad_branch = (grad_first * layer_gate[layer_at, 0] * hidden_gate).astype(B)
        scale = head_scale[layer_at]
        grad_mixed = (contract(grad_branch, weights[3], NT) * scale).astype(B)
        grad_mixed_t = (contract(weights[3], grad_branch, NT) * scale[:, None]).astype(B)
        grad_proj = attend_back(
            windows,
            tokens,
            features,
            grad_mixed,
            grad_mixed_t,
            key_segments,
            query_segments,
            log_total,
        )
        grad_input = jnp.einsum("jre,jde->rd", grad_proj, weights[:3], preferred_element_type=F)
        grad_hidden = grad_first + grad_input
        grad_hidden, grad_proj = together(grad_hidden, grad_proj)
        grad_in = jnp.einsum(
            "rd,jre->jde", hidden_low, grad_proj, preferred_element_type=F
        ).astype(B)
        grad_out = dot(gated_t, grad_branch).astype(B)
        stack = [grad_in, grad_out[None]]
        if layer_at == layer_count - 1:
            stack.append(grad_map[None])
        stack = jnp.concatenate(stack, axis=0)
        if layer_at > 0:
            attn_owned = jnp.moveaxis(
                stack.reshape(-1, unit_count, slab_rows, breadth), 1, 0
            )
        else:
            stack = stack.reshape(-1, chips, 2, slab_rows, breadth)
            attn_mine = jnp.moveaxis(
                lax.dynamic_index_in_dim(stack, core, 2, keepdims=False), 1, 0
            )
            attn_theirs = jnp.moveaxis(
                lax.dynamic_index_in_dim(stack, 1 - core, 2, keepdims=False), 1, 0
            )

    grad_looked, gain_rows[0], gain_rows[1] = norm_backward(
        embed_stored, norm_params[0], grad_hidden * hidden_gate
    )
    sent = grad_looked.astype(B)
    small = jnp.concatenate(
        [jnp.stack(gain_rows), jnp.broadcast_to(loss_part, (1, breadth))], axis=0
    )
    pieces = [part.reshape(-1, breadth) for part in feed_parts[1:] + attn_parts[1:]]
    early = jnp.concatenate(pieces, axis=0)
    same = [(sent, 0), (sent, ROW_BLOCK)]
    other = swapped(sent)
    crossed = [(other, 0), (other, ROW_BLOCK)]
    if chips == 4 and length == 2 * ROW_BLOCK:
        near = [across(sent, 1), across(sent, 2)]
        near, early, grad_table, attn_theirs = together(near, early, grad_table, attn_theirs)
        last = [across(near[0][:ROW_BLOCK], 2), across(near[1][ROW_BLOCK:], 1)]
        near_other = [swapped(part) for part in near]
        attn_chip = chip_sum(attn_mine, swapped(attn_theirs))
        early = dp_scatter(early)
        last, near_other, attn_chip, early = together(last, near_other, attn_chip, early)
        early, *early_place = dp_gather(early)
        small = dp_sum(small)
        attn_received = sent_to_owners(attn_chip, chip, range(1, chips))
        last_other = [swapped(part) for part in last]
        for home, parts, ends in ((same, near, last), (crossed, near_other, last_other)):
            home += [(part, at) for part in parts for at in (0, ROW_BLOCK)]
            home += [(part, 0) for part in ends]
    else:
        early, *early_place = dp_gather(dp_scatter(early))
        small = dp_sum(small)
        attn_chip = chip_sum(attn_mine, swapped(attn_theirs))
        attn_received = sent_to_owners(attn_chip, chip, range(1, chips))
        for step in range(1, chips):
            part = across(sent, step)
            for home, part in ((same, part), (crossed, swapped(part))):
                home += [(part, at) for at in range(0, length, ROW_BLOCK)]
    embed_part = spread(all_ids, other_ids, own_place, lists, grad_table, same + crossed)
    embed_part, attn_received, early, small = together(embed_part, attn_received, early, small)
    attn_parts[0] = owner_total(attn_chip, attn_received, chip)
    early = dp_placed(early, *early_place)
    embed_sum, feed_first, attn_first = lax.psum((embed_part, feed_parts[0], attn_parts[0]), "dp")
    feed_sums, attn_sums = [feed_first], [attn_first]
    cursor = 0
    for parts, sums in ((feed_parts, feed_sums), (attn_parts, attn_sums)):
        for part in parts[1:]:
            rows = part.shape[0] * part.shape[1]
            sums.append(early[cursor : cursor + rows].reshape(part.shape))
            cursor += rows

    row_sums = jnp.concatenate(
        [
            jnp.sum(attention_rows, axis=-1).reshape(-1),
            jnp.sum(feed_rows, axis=-1).reshape(-1),
            jnp.sum(map_rows)[None],
            jnp.sum(embedding_rows)[None],
        ]
    )
    row_sums = jnp.pad(row_sums, (0, breadth - row_sums.shape[0]))[None]
    old_cols = jnp.concatenate(
        [
            attention_cols.reshape(-1, breadth),
            feed_cols.reshape(-1, breadth),
            map_cols[None],
            embedding_cols[None],
        ],
        axis=0,
    )
    mats = layer_count * 4
    heights = jnp.array(
        [breadth] * mats
        + [units_dev * unit_count] * (layer_count * 2)
        + [breadth, vocab_dev * unit_count],
        F,
    )[:, None]
    packed = stats(small, row_sums, embed_sum, attn_sums, feed_sums)
    scalars, new_cols, factor, norm_grad, new_norm_params, new_norm_moment = factors(
        lax.all_gather(packed, "unit"), old_cols, heights, norm_params, norm_moment
    )
    total_loss, grad_norm = scalars[0], scalars[1]
    factor = factor[:, None]
    feeds = layer_count * 2
    here = jnp.zeros((1,), jnp.int32)
    slab = jnp.full((1,), unit_at, jnp.int32)
    new_embedding, embed_grad, new_embedding_rows = (
        value[0]
        for value in renew(
            scalars,
            here,
            factor,
            mats + feeds + 1,
            embedding_rows[None],
            embedding[None],
            embed_sum[None],
            1,
            640,
        )
    )
    new_map, map_grad, new_map_rows = (
        value[0]
        for value in renew(
            scalars,
            slab,
            factor,
            mats + feeds,
            map_rows[None],
            map_weight[None],
            attn_sums[layer_count - 1][4:],
            1,
            slab_rows,
        )
    )
    new_attention, attn_grad, new_attention_rows = (
        value.reshape((layer_count, 4) + value.shape[1:])
        for value in renew(
            scalars,
            slab,
            factor,
            0,
            attention_rows.reshape(mats, slab_rows),
            attention.reshape(mats, breadth, breadth),
            jnp.concatenate([part[:4] for part in attn_sums], axis=0),
            4,
            slab_rows,
        )
    )
    new_feed_forward, feed_grad, new_feed_rows = (
        value.reshape((layer_count, 2) + value.shape[1:])
        for value in renew(
            scalars,
            here,
            factor,
            mats,
            feed_rows.reshape(feeds, units_dev),
            feed_forward.reshape(feeds, units_dev, breadth),
            jnp.concatenate(feed_sums, axis=0),
            1,
            units_dev,
        )
    )
    new_attention_cols = new_cols[:mats].reshape(layer_count, 4, breadth)
    new_feed_cols = new_cols[mats : mats + feeds].reshape(layer_count, 2, breadth)
    new_map_cols = new_cols[mats + feeds]
    new_embedding_cols = new_cols[mats + feeds + 1]
    return (
        total_loss,
        count,
        grad_norm,
        new_embedding,
        embed_grad,
        new_embedding_rows,
        new_embedding_cols,
        new_attention,
        attn_grad,
        new_attention_rows,
        new_attention_cols,
        new_feed_forward,
        feed_grad,
        new_feed_rows,
        new_feed_cols,
        new_map,
        map_grad,
        new_map_rows,
        new_map_cols,
        new_norm_params,
        norm_grad,
        new_norm_moment,
    )


def solution(mesh):
    placed = (
        P(("dp", "unit"), None),
        P(("dp", "unit"), None),
        P(),
        P(("dp", "unit"), None),
        P(),
        P(("dp", "unit"), None, None),
        P(),
        P(),
        P(),
        P(),
        P(),
        P("unit", None),
        P(),
        P(None, None, "unit", None),
        P(),
        P(),
        P("unit"),
        P(),
        P(None, None, "unit"),
        P(),
        P(None, None, "unit"),
        P(),
        P("unit"),
        P(),
        P(),
    )
    return jax.shard_map(
        local,
        mesh=mesh,
        in_specs=placed,
        out_specs=(
            P(),
            P(),
            P(),
            P("unit", None),
            P("unit", None),
            P("unit"),
            P(),
            P(None, None, "unit", None),
            P(None, None, "unit", None),
            P(None, None, "unit"),
            P(),
            P(None, None, "unit", None),
            P(None, None, "unit", None),
            P(None, None, "unit"),
            P(),
            P("unit", None),
            P("unit", None),
            P("unit"),
            P(),
            P(),
            P(),
            P(),
        ),
        check_vma=False,
    )
```

```python
import functools
import math

import jax
import jax.numpy as jnp
from jax import lax
from jax.experimental import pallas as pl
from jax.experimental.pallas import tpu as pltpu
from jax.sharding import PartitionSpec as P

H = 12
HD = 64
PAIR = 2 * HD
KEY_BLOCK = 128
QUERY_BLOCK = 256
ROW_BLOCK = 512
UNIT_BLOCK = 768

LN_EPS = 1e-06
ADA_EPS = 1e-30
DECAY_RATE = 0.95
LEARN_RATE = 0.015
CLIP_LIMIT = 0.05
MASK_FILL = 1e30

B = jnp.bfloat16
F = jnp.float32
NT = (((1,), (1,)), ((), ()))
TN = (((0,), (0,)), ((), ()))
TT = (((0,), (1,)), ((), ()))
VMEM_MOST = 58 * 2**20


def dot(left, right):
    return jnp.dot(left, right, preferred_element_type=F)


def contract(left, right, dims):
    return lax.dot_general(left, right, dims, preferred_element_type=F)


def query_windows(segments, block):
    first = segments[::block]
    last = segments[block - 1 :: block]
    start = jnp.sum((segments[None, :] < first[:, None]).astype(jnp.int32), axis=1)
    stop = jnp.sum((segments[None, :] <= last[:, None]).astype(jnp.int32), axis=1)
    low = start // KEY_BLOCK
    high = (stop + KEY_BLOCK - 1) // KEY_BLOCK
    return jnp.concatenate([low, high - low]).astype(jnp.int32)


def most_blocks(length, block):
    return min(length // KEY_BLOCK, block // KEY_BLOCK + 4)


def window_mask(segk_ref, segq_ref, start, width, first_query, block):
    key_seg = segk_ref[pl.ds(start, width), :]
    if block > KEY_BLOCK:
        key_seg = jnp.concatenate([key_seg] * (block // KEY_BLOCK), axis=1)
    query_seg = segq_ref[0:1, pl.ds(first_query, block)]
    key_at = start + lax.broadcasted_iota(jnp.int32, (width, block), 0)
    query_at = first_query + lax.broadcasted_iota(jnp.int32, (width, block), 1)
    return (key_seg == query_seg) | (key_at == query_at)


def head_rows(block):
    empty = jnp.zeros((HD, block.shape[1]), block.dtype)
    first = jnp.concatenate([block[:HD], empty], axis=0)
    second = jnp.concatenate([empty, block[HD:]], axis=0)
    return jnp.concatenate([first, second], axis=1)


def head_lanes(block):
    lane = lax.broadcasted_iota(jnp.int32, block.shape, 1)
    empty = jnp.zeros_like(block)
    return jnp.concatenate(
        [jnp.where(lane < HD, block, empty), jnp.where(lane < HD, empty, block)], axis=0
    )


def attend_kernel(
    window_ref, gate_ref, k_ref, qt_ref, vt_ref, segk_ref, segq_ref, ot_ref, lse_ref, *, block
):
    pair = pl.program_id(0)
    length = k_ref.shape[1]
    count = length // block
    lse_ref[...] = jnp.zeros_like(lse_ref)
    for i in range(count):
        low = window_ref[i]
        number = window_ref[count + i]
        columns = pl.ds(i * block, block)
        for n in range(1, most_blocks(length, block) + 1):

            @pl.when(number == n)
            def _():
                width = n * KEY_BLOCK
                start = pl.multiple_of(low * KEY_BLOCK, KEY_BLOCK)
                keys = k_ref[0, pl.ds(start, width), :]
                mask = window_mask(segk_ref, segq_ref, start, width, i * block, block)
                queries = qt_ref[0, :, columns]
                scores = dot(keys, head_rows(queries))
                scores = jnp.where(jnp.concatenate([mask, mask], axis=1), scores, -MASK_FILL)
                top = jnp.max(scores, axis=0, keepdims=True)
                exponent = jnp.exp(scores - top)
                total = jnp.sum(exponent, axis=0, keepdims=True)
                mixed = dot(vt_ref[0, :, pl.ds(start, width)], exponent.astype(B))
                inverse = 1.0 / total
                log_total = top + jnp.log(total)
                for head in range(2):
                    rows = slice(head * HD, (head + 1) * HD)
                    lanes = slice(head * block, (head + 1) * block)
                    gated = mixed[rows, lanes] * (inverse[:, lanes] * gate_ref[2 * pair + head])
                    ot_ref[rows, columns] = gated.astype(B)
                    lse_ref[0, head : head + 1, columns] = log_total[:, lanes]


def attend(windows, gates, tokens, features, key_segments, query_segments):
    _, length, breadth = tokens.shape
    pairs = breadth // PAIR
    return pl.pallas_call(
        functools.partial(attend_kernel, block=QUERY_BLOCK),
        grid_spec=pltpu.PrefetchScalarGridSpec(
            num_scalar_prefetch=2,
            grid=(pairs,),
            in_specs=[
                pl.BlockSpec((1, length, PAIR), lambda p, *_: (1, 0, p)),
                pl.BlockSpec((1, PAIR, length), lambda p, *_: (0, p, 0)),
                pl.BlockSpec((1, PAIR, length), lambda p, *_: (2, p, 0)),
                pl.BlockSpec((length, KEY_BLOCK), lambda p, *_: (0, 0)),
                pl.BlockSpec((8, length), lambda p, *_: (0, 0)),
            ],
            out_specs=[
                pl.BlockSpec((PAIR, length), lambda p, *_: (p, 0)),
                pl.BlockSpec((1, 8, length), lambda p, *_: (p, 0, 0)),
            ],
        ),
        out_shape=[
            jax.ShapeDtypeStruct((breadth, length), B),
            jax.ShapeDtypeStruct((pairs, 8, length), F),
        ],
        compiler_params=pltpu.CompilerParams(vmem_limit_bytes=VMEM_MOST),
        cost_estimate=pl.CostEstimate(
            flops=2 * 2 * 2 * length * 512 * breadth,
            bytes_accessed=8 * length * breadth,
            transcendentals=length * 512 * 12,
        ),
        name="attend",
    )(windows, gates, tokens, features, features, key_segments, query_segments)


def attend_back_kernel(
    window_ref,
    k_ref,
    kt_ref,
    q_ref,
    qt_ref,
    v_ref,
    do_ref,
    dot_ref,
    segk_ref,
    segq_ref,
    lse_ref,
    grad_ref,
    dq_sum,
    dk_sum,
    dv_sum,
    *,
    block,
    score_scale,
):
    length = k_ref.shape[1]
    count = length // block
    dk_sum[...] = jnp.zeros_like(dk_sum)
    dv_sum[...] = jnp.zeros_like(dv_sum)
    for i in range(count):
        low = window_ref[i]
        number = window_ref[count + i]
        columns = pl.ds(i * block, block)
        for n in range(1, most_blocks(length, block) + 1):

            @pl.when(number == n)
            def _():
                width = n * KEY_BLOCK
                start = pl.multiple_of(low * KEY_BLOCK, KEY_BLOCK)
                window = pl.ds(start, width)
                keys = k_ref[0, window, :]
                values = v_ref[0, window, :]
                mask = window_mask(segk_ref, segq_ref, start, width, i * block, block)
                queries_t = qt_ref[0, :, columns]
                grads_t = dot_ref[:, columns]
                scores = dot(keys, head_rows(queries_t))
                scores = jnp.where(jnp.concatenate([mask, mask], axis=1), scores, -MASK_FILL)
                log_total = jnp.concatenate(
                    [lse_ref[0, 0:1, columns], lse_ref[0, 1:2, columns]], axis=1
                )
                prob = jnp.exp(scores - log_total)
                weighted = prob * dot(values, head_rows(grads_t))
                inner = jnp.sum(weighted, axis=0, keepdims=True)
                grad = (weighted - prob * inner).astype(B)
                grad_q = dot(kt_ref[0, :, window], grad) * score_scale
                dq_sum[:HD, columns] = grad_q[:HD, :block]
                dq_sum[HD:, columns] = grad_q[HD:, block:]
                dv_sum[window, :] += dot(prob.astype(B), head_lanes(do_ref[columns, :]))
                dk_sum[window, :] += dot(grad, head_lanes(q_ref[0, columns, :]))

    grad_ref[0] = jnp.transpose(dq_sum[...]).astype(B)
    grad_ref[1] = dk_sum[...].astype(B)
    grad_ref[2] = dv_sum[...].astype(B)


def attend_back(
    windows, tokens, features, grads, grads_t, key_segments, query_segments, log_total
):
    _, length, breadth = tokens.shape
    pairs = breadth // PAIR

    def token_spec(which):
        return pl.BlockSpec((1, length, PAIR), lambda p, *_: (which, 0, p))

    def feature_spec(which):
        return pl.BlockSpec((1, PAIR, length), lambda p, *_: (which, p, 0))

    return pl.pallas_call(
        functools.partial(
            attend_back_kernel, block=QUERY_BLOCK, score_scale=1.0 / math.sqrt(HD)
        ),
        grid_spec=pltpu.PrefetchScalarGridSpec(
            num_scalar_prefetch=1,
            grid=(pairs,),
            in_specs=[
                token_spec(1),
                feature_spec(1),
                token_spec(0),
                feature_spec(0),
                token_spec(2),
                pl.BlockSpec((length, PAIR), lambda p, *_: (0, p)),
                pl.BlockSpec((PAIR, length), lambda p, *_: (p, 0)),
                pl.BlockSpec((length, KEY_BLOCK), lambda p, *_: (0, 0)),
                pl.BlockSpec((8, length), lambda p, *_: (0, 0)),
                pl.BlockSpec((1, 8, length), lambda p, *_: (p, 0, 0)),
            ],
            out_specs=pl.BlockSpec((3, length, PAIR), lambda p, *_: (0, 0, p)),
            scratch_shapes=[
                pltpu.VMEM((PAIR, length), F),
                pltpu.VMEM((length, PAIR), F),
                pltpu.VMEM((length, PAIR), F),
            ],
        ),
        out_shape=jax.ShapeDtypeStruct((3, length, breadth), B),
        compiler_params=pltpu.CompilerParams(vmem_limit_bytes=VMEM_MOST),
        cost_estimate=pl.CostEstimate(
            flops=5 * 2 * 2 * length * 512 * breadth,
            bytes_accessed=20 * length * breadth,
            transcendentals=length * 512 * 12,
        ),
        name="attend_back",
    )(
        windows,
        tokens,
        features,
        tokens,
        features,
        tokens,
        grads,
        grads_t,
        key_segments,
        query_segments,
        log_total,
    )


def project_kernel(x_ref, weight_ref, tokens_ref, features_ref, *, score_scale):
    scale = jnp.where(pl.program_id(0) == 0, score_scale, 1.0).astype(F)
    tokens = dot(x_ref[...], weight_ref[...]).astype(B).astype(F)
    tokens_ref[0] = (tokens * scale).astype(B)
    features = contract(weight_ref[...], x_ref[...], TT).astype(B).astype(F)
    features_ref[0] = (features * scale).astype(B)


def project(x, weights, layer):
    length, breadth = x.shape
    return pl.pallas_call(
        functools.partial(project_kernel, score_scale=1.0 / math.sqrt(HD)),
        grid=(3,),
        in_specs=[
            pl.BlockSpec((length, breadth), lambda j: (0, 0)),
            pl.BlockSpec((None, None, breadth, breadth), lambda j: (layer, j, 0, 0)),
        ],
        out_specs=[
            pl.BlockSpec((1, length, breadth), lambda j: (j, 0, 0)),
            pl.BlockSpec((1, breadth, length), lambda j: (j, 0, 0)),
        ],
        out_shape=[
            jax.ShapeDtypeStruct((3, length, breadth), B),
            jax.ShapeDtypeStruct((3, breadth, length), B),
        ],
        compiler_params=pltpu.CompilerParams(vmem_limit_bytes=VMEM_MOST),
        cost_estimate=pl.CostEstimate(
            flops=12 * length * breadth * breadth,
            bytes_accessed=14 * length * breadth + 6 * breadth * breadth,
            transcendentals=0,
        ),
        name="project",
    )(x, weights)


def gelu_and_slope(value):
    density = jnp.exp(value * value * -0.5)
    ratio = pl.reciprocal(1.0 + jnp.abs(value) * (0.3275911 * math.sqrt(0.5)))
    series = ratio * (
        0.127414796
        + ratio
        * (-0.142248368 + ratio * (0.7107068705 + ratio * (-0.7265760135 + ratio * 0.5307027145)))
    )
    tail = series * density
    below = jnp.where(value >= 0, 1.0 - tail, tail)
    return value * below, below + value * density * (1.0 / math.sqrt(2.0 * math.pi))


def feed_kernel(x_ref, up_ref, down_ref, scale_ref, act_ref, slope_ref, out_ref):
    first = pl.program_id(0) == 0
    scale = scale_ref[0]
    act, slope = gelu_and_slope(contract(x_ref[...], up_ref[...], NT))
    act = (act * scale).astype(B)
    act_ref[...] = act
    slope_ref[...] = (slope * scale).astype(B)
    part = dot(act, down_ref[...])

    @pl.when(first)
    def _():
        out_ref[...] = part

    @pl.when(jnp.logical_not(first))
    def _():
        out_ref[...] += part


def feed(x, weights, scale):
    length, breadth = x.shape
    units = weights.shape[1]
    block = UNIT_BLOCK
    return pl.pallas_call(
        feed_kernel,
        grid=(units // block,),
        in_specs=[
            pl.BlockSpec((length, breadth), lambda j: (0, 0)),
            pl.BlockSpec((None, block, breadth), lambda j: (0, j, 0)),
            pl.BlockSpec((None, block, breadth), lambda j: (1, j, 0)),
            pl.BlockSpec((1, 1, block), lambda j: (0, 0, j)),
        ],
        out_specs=[
            pl.BlockSpec((length, block), lambda j: (0, j)),
            pl.BlockSpec((length, block), lambda j: (0, j)),
            pl.BlockSpec((length, breadth), lambda j: (0, 0)),
        ],
        out_shape=[
            jax.ShapeDtypeStruct((length, units), B),
            jax.ShapeDtypeStruct((length, units), B),
            jax.ShapeDtypeStruct((length, breadth), F),
        ],
        compiler_params=pltpu.CompilerParams(vmem_limit_bytes=VMEM_MOST),
        cost_estimate=pl.CostEstimate(
            flops=4 * length * breadth * units,
            bytes_accessed=4 * (length + breadth) * units + 6 * length * breadth,
            transcendentals=2 * length * units,
        ),
        name="feed",
    )(x, weights, weights, scale.reshape(1, 1, units))


def feed_back_kernel(
    grad_ref, x_ref, act_ref, slope_ref, up_ref, down_ref, out_ref, owned_ref, pre_grad
):
    first = pl.program_id(0) == 0
    grad_act = contract(grad_ref[...], down_ref[...], NT)
    grad_pre = (grad_act * slope_ref[...].astype(F)).astype(B)
    pre_grad[...] = grad_pre
    part = dot(grad_pre, up_ref[...])

    @pl.when(first)
    def _():
        out_ref[...] = part

    @pl.when(jnp.logical_not(first))
    def _():
        out_ref[...] += part

    grads = (
        contract(pre_grad[...], x_ref[...], TN).astype(B),
        contract(act_ref[...], grad_ref[...], TN).astype(B),
    )
    owners, _, share, _ = owned_ref.shape
    for which in range(2):
        for owner in range(owners):
            owned_ref[owner, which] = grads[which][owner * share : (owner + 1) * share]


def feed_back(grad, x, act, slope, weights, owners):
    length, breadth = x.shape
    units = weights.shape[1]
    share = units // owners
    block = UNIT_BLOCK
    lanes = pl.BlockSpec((length, block), lambda j: (0, j))
    whole = pl.BlockSpec((length, breadth), lambda j: (0, 0))
    return pl.pallas_call(
        feed_back_kernel,
        grid=(units // block,),
        in_specs=[
            whole,
            whole,
            lanes,
            lanes,
            pl.BlockSpec((None, block, breadth), lambda j: (0, j, 0)),
            pl.BlockSpec((None, block, breadth), lambda j: (1, j, 0)),
        ],
        out_specs=[
            whole,
            pl.BlockSpec((block // share, 2, share, breadth), lambda j: (j, 0, 0, 0)),
        ],
        scratch_shapes=[pltpu.VMEM((length, block), B)],
        out_shape=[
            jax.ShapeDtypeStruct((length, breadth), F),
            jax.ShapeDtypeStruct((owners, 2, share, breadth), B),
        ],
        compiler_params=pltpu.CompilerParams(vmem_limit_bytes=VMEM_MOST),
        cost_estimate=pl.CostEstimate(
            flops=8 * length * breadth * units,
            bytes_accessed=4 * (length + 2 * breadth) * units + 8 * length * breadth,
            transcendentals=0,
        ),
        name="feed_back",
    )(grad, x, act, slope, weights, weights)


def scan_kernel(ids, place, found, ends, *, vocab):
    base = place[0]
    blocks = ends.shape[0]
    streams = math.gcd(blocks, 8)
    for first in range(0, blocks, streams):

        def scan(t, counts):
            after = []
            for k, count in enumerate(counts):
                at = (first + k) * ROW_BLOCK + t
                relative = (ids[at] - base).astype(jnp.uint32)
                found[count] = at
                after.append(count + jnp.where(relative < jnp.uint32(vocab), 1, 0))
            return tuple(after)

        begin = tuple(jnp.int32((first + k) * ROW_BLOCK) for k in range(streams))
        counts = lax.fori_loop(0, ROW_BLOCK, scan, begin, unroll=4)
        for k, count in enumerate(counts):
            ends[first + k] = count


def scan_ids(ids, place, vocab):
    smem = pl.BlockSpec(memory_space=pltpu.SMEM)
    return pl.pallas_call(
        functools.partial(scan_kernel, vocab=vocab),
        in_specs=[smem, smem],
        out_specs=[smem, smem],
        out_shape=[
            jax.ShapeDtypeStruct(ids.shape, jnp.int32),
            jax.ShapeDtypeStruct((ids.shape[0] // ROW_BLOCK,), jnp.int32),
        ],
        name="scan_ids",
    )(ids, place)


def lookup_kernel(ids, place, found, ends, own, other, *rest, blocks, vocab):
    outs = rest[:blocks]
    table, rows, stage, table_sem, out_sem = rest[blocks:]
    base = place[0]
    core = place[1]
    mine = pl.multiple_of(core * vocab, 8)
    theirs = pl.multiple_of((1 - core) * vocab, 8)
    loads = [
        pltpu.make_async_copy(own, table.at[pl.ds(mine, vocab)], table_sem.at[0]),
        pltpu.make_async_copy(other, table.at[pl.ds(theirs, vocab)], table_sem.at[1]),
    ]
    for load in loads:
        load.start()
    for load in loads:
        load.wait()
    copies = [None, None]
    for k in range(blocks):
        rows[...] = jnp.zeros_like(rows)

        def put(entry, carry):
            t = found[entry]
            rows[pl.ds(t - k * ROW_BLOCK, 1), :] = table[pl.ds(ids[t] - base, 1), :]
            return carry

        each_entry(k * ROW_BLOCK, ends[k], put)
        slot = k % 2
        if copies[slot] is not None:
            copies[slot].wait()
        stage[slot] = rows[...].astype(B)
        copies[slot] = pltpu.make_async_copy(stage.at[slot], outs[k], out_sem.at[slot])
        copies[slot].start()
    for copy in copies:
        copy.wait()


def each_entry(low, high, body):
    quads = lax.div(high - low, 4)

    def four(e, carry):
        for j in range(4):
            body(low + e * 4 + j, 0)
        return carry

    lax.fori_loop(0, quads, four, 0)
    lax.fori_loop(low + quads * 4, high, body, 0)


def lookup(ids, place, found, ends, own, other):
    vocab, breadth = own.shape
    blocks = ids.shape[0] // ROW_BLOCK
    hbm = pl.BlockSpec(memory_space=pl.ANY)
    smem = pl.BlockSpec(memory_space=pltpu.SMEM)
    return pl.pallas_call(
        functools.partial(lookup_kernel, blocks=blocks, vocab=vocab),
        in_specs=[smem] * 4 + [hbm] * 2,
        out_specs=[hbm] * blocks,
        out_shape=[jax.ShapeDtypeStruct((ROW_BLOCK, breadth), B)] * blocks,
        scratch_shapes=[
            pltpu.VMEM((2 * vocab, breadth), F),
            pltpu.VMEM((ROW_BLOCK, breadth), F),
            pltpu.VMEM((2, ROW_BLOCK, breadth), B),
            pltpu.SemaphoreType.DMA((2,)),
            pltpu.SemaphoreType.DMA((2,)),
        ],
        compiler_params=pltpu.CompilerParams(vmem_limit_bytes=VMEM_MOST),
        cost_estimate=pl.CostEstimate(
            flops=0,
            bytes_accessed=8 * vocab * breadth + 2 * ids.shape[0] * breadth,
            transcendentals=0,
        ),
        name="lookup",
    )(ids, place, found, ends, own, other)


def spread_kernel(
    ids, other_ids, place, found, ends, other_found, other_ends, begin, *rest, pieces
):
    blocks = len(pieces)
    arrays = max(which for which, _ in pieces) + 1
    grads = [rest[which].at[pl.ds(at, ROW_BLOCK)] for which, at in pieces]
    out, total, rows, stage, half, sem, in_sem, out_sem = rest[arrays:]
    base = place[0]
    vocab = total.shape[0]
    fill = pltpu.make_async_copy(begin, total, sem.at[0])
    fill.start()

    def load(k):
        copy = pltpu.make_async_copy(grads[k], stage.at[k % 2], in_sem.at[k % 2])
        copy.start()
        return copy

    coming = load(0)
    fill.wait()
    for k in range(blocks):
        coming.wait()
        if k + 1 < blocks:
            coming = load(k + 1)
        rows[...] = stage[k % 2].astype(F)

        lists = (ids, found, ends) if k < blocks // 2 else (other_ids, other_found, other_ends)
        first = k % (blocks // 2) * ROW_BLOCK

        def add(entry, carry):
            t = lists[1][entry]
            at = pl.ds(lists[0][t] - base, 1)
            total[at, :] += rows[pl.ds(t - first, 1), :]
            return carry

        each_entry(first, lists[2][k % (blocks // 2)], add)
    step = half.shape[1]
    copies = [None, None]
    for j in range(vocab // step):
        slot = j % 2
        if copies[slot] is not None:
            copies[slot].wait()
        half[slot] = total[j * step : (j + 1) * step, :].astype(B)
        copies[slot] = pltpu.make_async_copy(
            half.at[slot], out.at[pl.ds(j * step, step)], out_sem.at[slot]
        )
        copies[slot].start()
    for copy in copies:
        copy.wait()


def spread(ids, other_ids, place, lists, begin, grads):
    vocab, breadth = begin.shape
    arrays = []
    pieces = []
    for array, at in grads:
        known = [k for k, other in enumerate(arrays) if other is array]
        if not known:
            known = [len(arrays)]
            arrays.append(array)
        pieces.append((known[0], at))
    hbm = pl.BlockSpec(memory_space=pl.ANY)
    smem = pl.BlockSpec(memory_space=pltpu.SMEM)
    return pl.pallas_call(
        functools.partial(spread_kernel, pieces=tuple(pieces)),
        in_specs=[smem] * 7 + [hbm] * (1 + len(arrays)),
        out_specs=hbm,
        out_shape=jax.ShapeDtypeStruct((vocab, breadth), B),
        scratch_shapes=[
            pltpu.VMEM((vocab, breadth), F),
            pltpu.VMEM((ROW_BLOCK, breadth), F),
            pltpu.VMEM((2, ROW_BLOCK, breadth), B),
            pltpu.VMEM((2, vocab // 4, breadth), B),
            pltpu.SemaphoreType.DMA((1,)),
            pltpu.SemaphoreType.DMA((2,)),
            pltpu.SemaphoreType.DMA((2,)),
        ],
        compiler_params=pltpu.CompilerParams(vmem_limit_bytes=VMEM_MOST),
        cost_estimate=pl.CostEstimate(
            flops=0,
            bytes_accessed=6 * vocab * breadth + 2 * len(grads) * ROW_BLOCK * breadth,
            transcendentals=0,
        ),
        name="spread",
    )(ids, other_ids, place, *lists, begin, *arrays)


def stats_kernel(small_ref, row_sums_ref, embed_ref, *rest, layers):
    attn = rest[:layers]
    feeds = rest[layers : 2 * layers]
    out_ref = rest[2 * layers]
    norms = small_ref.shape[0]
    cols = jnp.sum(jnp.square(embed_ref[...].astype(F)), axis=0, keepdims=True)

    @pl.when(pl.program_id(0) == 0)
    def _():
        def put(row, value):
            out_ref[row : row + 1, :] = jnp.sum(
                jnp.square(value.astype(F)), axis=0, keepdims=True
            )

        out_ref[:norms, :] = small_ref[...]
        row = norms
        for parts, count in ((attn, 4), (feeds, 2)):
            for part in parts:
                for k in range(count):
                    put(row, part[k])
                    row += 1
        put(row, attn[layers - 1][4])
        out_ref[row + 1 : row + 2, :] = cols
        row += 2
        out_ref[row : row + 1, :] = row_sums_ref[...]

    @pl.when(pl.program_id(0) > 0)
    def _():
        at = norms + 6 * layers + 1
        out_ref[at : at + 1, :] += cols


def stats(small, row_sums, embed, attn, feeds):
    height, breadth = embed.shape
    block = math.gcd(height, 480)
    rows = small.shape[0] + 3 + 6 * len(attn)
    vmem = pl.BlockSpec(memory_space=pltpu.VMEM)
    return pl.pallas_call(
        functools.partial(stats_kernel, layers=len(attn)),
        grid=(height // block,),
        in_specs=[vmem, vmem, pl.BlockSpec((block, breadth), lambda j: (j, 0))]
        + [vmem] * (2 * len(attn)),
        out_specs=pl.BlockSpec((rows, breadth), lambda j: (0, 0)),
        out_shape=jax.ShapeDtypeStruct((rows, breadth), F),
        compiler_params=pltpu.CompilerParams(vmem_limit_bytes=VMEM_MOST),
        name="stats",
    )(small, row_sums, embed, *attn, *feeds)


def factors_kernel(
    parts_ref,
    cols_ref,
    heights_ref,
    params_ref,
    moment_ref,
    scalars_ref,
    new_cols_ref,
    factor_ref,
    norm_grad_ref,
    new_params_ref,
    new_moment_ref,
):
    packed = parts_ref[0]
    for k in range(1, parts_ref.shape[0]):
        packed = packed + parts_ref[k]
    norms = params_ref.shape[0]
    mats, breadth = cols_ref.shape
    norm_grads = packed[:norms]
    col_sums = packed[norms + 1 : norms + 1 + mats]
    lane = lax.broadcasted_iota(jnp.int32, (mats, breadth), 1)
    row = lax.broadcasted_iota(jnp.int32, (mats, breadth), 0)
    row_sums = jnp.sum(
        jnp.where(lane == row, packed[norms + 1 + mats :], 0.0), axis=1, keepdims=True
    )
    heights = heights_ref[...]
    mat_sums = jnp.sum(col_sums, axis=1, keepdims=True)
    square = jnp.sum(mat_sums, axis=0, keepdims=True) + jnp.sum(
        jnp.sum(norm_grads * norm_grads, axis=1, keepdims=True), axis=0, keepdims=True
    )
    norm = jnp.sqrt(square)
    clip = jnp.minimum(1.0, CLIP_LIMIT / norm)
    scalars_ref[0] = packed[norms, 0]
    scalars_ref[1] = norm[0, 0]
    scalars_ref[2] = clip[0, 0]
    new_cols = DECAY_RATE * cols_ref[...] + (1 - DECAY_RATE) * (
        clip * clip * col_sums / heights + ADA_EPS
    )
    mean_rows = DECAY_RATE * row_sums / heights + (1 - DECAY_RATE) * (
        clip * clip * mat_sums / (heights * breadth) + ADA_EPS
    )
    new_cols_ref[...] = new_cols
    factor_ref[...] = LEARN_RATE * jnp.sqrt(mean_rows) * lax.rsqrt(new_cols)
    norm_grad = norm_grads * clip
    moment = DECAY_RATE * moment_ref[...] + (1 - DECAY_RATE) * (norm_grad * norm_grad + ADA_EPS)
    norm_grad_ref[...] = norm_grad
    new_moment_ref[...] = moment
    new_params_ref[...] = params_ref[...] - LEARN_RATE * norm_grad * lax.rsqrt(moment)


def factors(parts, cols, heights, params, moment):
    vmem = pl.BlockSpec(memory_space=pltpu.VMEM)
    like = [jax.ShapeDtypeStruct(x.shape, F) for x in (cols, cols, params, params, params)]
    return pl.pallas_call(
        factors_kernel,
        in_specs=[vmem] * 5,
        out_specs=[pl.BlockSpec(memory_space=pltpu.SMEM)] + [vmem] * 5,
        out_shape=[jax.ShapeDtypeStruct((3,), F)] + like,
        compiler_params=pltpu.CompilerParams(vmem_limit_bytes=VMEM_MOST),
        name="factors",
    )(parts, cols, heights, params, moment)


def renew_kernel(
    scalars_ref, at_ref, factor_ref, rows_ref, weight_ref, sum_ref, new_ref, grad_ref, new_rows_ref
):
    for m in range(sum_ref.shape[0]):
        grad = sum_ref[m].astype(F) * scalars_ref[2]
        mean = jnp.mean(grad * grad, axis=1, keepdims=True) + ADA_EPS
        new_rows = DECAY_RATE * rows_ref[m] + (1 - DECAY_RATE) * mean
        wide = jnp.broadcast_to(new_rows, (new_rows.shape[0], 128))
        new_rows_ref[m, 0] = jnp.transpose(wide)[:1]
        grad_ref[m] = grad
        new_ref[m] = weight_ref[m] - grad * lax.rsqrt(new_rows) * factor_ref[m]


def renew(scalars, at, factor, first, rows, weight, total, group, most):
    mats, height, breadth = total.shape
    block = math.gcd(height, most)
    per = height // block
    wide = pl.BlockSpec((group, block, breadth), lambda m, j, *_: (m, j, 0))
    new, grad, new_rows = pl.pallas_call(
        renew_kernel,
        grid_spec=pltpu.PrefetchScalarGridSpec(
            num_scalar_prefetch=2,
            grid=(mats // group, per),
            in_specs=[
                pl.BlockSpec((group, 1, breadth), lambda m, j, *_: (first // group + m, 0, 0)),
                pl.BlockSpec((group, block, 1), lambda m, j, *_: (m, j, 0)),
                pl.BlockSpec(
                    (group, block, breadth), lambda m, j, scalars, at: (m, at[0] * per + j, 0)
                ),
                wide,
            ],
            out_specs=[
                wide,
                wide,
                pl.BlockSpec((group, 1, 1, block), lambda m, j, *_: (m, j, 0, 0)),
            ],
        ),
        out_shape=[
            jax.ShapeDtypeStruct((mats, height, breadth), F),
            jax.ShapeDtypeStruct((mats, height, breadth), F),
            jax.ShapeDtypeStruct((mats, per, 1, block), F),
        ],
        compiler_params=pltpu.CompilerParams(vmem_limit_bytes=VMEM_MOST),
        name="renew",
    )(scalars, at, factor, rows[..., None], weight, total)
    return new, grad, new_rows.reshape(rows.shape)


def across(value, step):
    pairs = [(u, ((u // 2) ^ step) * 2 + u % 2) for u in range(lax.axis_size("unit"))]
    return lax.ppermute(value, "unit", pairs)


def swapped(value):
    return lax.ppermute(value, "unit", [(u, u ^ 1) for u in range(lax.axis_size("unit"))])


def gathered(value, beside_core, beside_chip):
    other, *beside_core = together(swapped(value), *beside_core)
    both = jnp.stack([value, other])
    chips = lax.axis_size("unit") // 2
    parts = [across(both, step) for step in range(1, chips)]
    if beside_chip:
        parts[0], *beside_chip = together(parts[0], *beside_chip(*beside_core))
    return jnp.stack([both] + parts), beside_core, beside_chip


def dp_scatter(value):
    size = lax.axis_size("dp")
    at = lax.axis_index("dp")
    share = value.shape[0] // size
    parts = [lax.dynamic_slice_in_dim(value, at * share, share, 0)]
    for step in range(1, size):
        away = lax.dynamic_slice_in_dim(value, (at + step) % size * share, share, 0)
        parts.append(lax.ppermute(away, "dp", [(d, (d + step) % size) for d in range(size)]))
    return parts


def dp_gather(parts):
    size = lax.axis_size("dp")
    at = lax.axis_index("dp")
    total = parts[0].astype(F)
    for part in parts[1:]:
        total = total + part.astype(F)
    total = total.astype(B)
    found = [total] + [
        lax.ppermute(total, "dp", [(d, (d + step) % size) for d in range(size)])
        for step in range(1, size)
    ]
    return found


def dp_placed(found):
    size = len(found)
    at = lax.axis_index("dp")
    share = found[0].shape[0]
    result = jnp.zeros((size * share,) + found[0].shape[1:], found[0].dtype)
    for step, part in enumerate(found):
        result = lax.dynamic_update_slice_in_dim(result, part, (at - step) % size * share, 0)
    return result


def dp_sum(value):
    size = lax.axis_size("dp")
    if size & (size - 1):
        return lax.psum(value, "dp")
    step = 1
    while step < size:
        value = value + lax.ppermute(value, "dp", [(d, d ^ step) for d in range(size)])
        step = 2 * step
    return value


def together(*values):
    return lax.optimization_barrier(values)


def chip_sum(mine, swapped_theirs):
    return (mine.astype(F) + swapped_theirs.astype(F)).astype(B)


def sent_to_owners(total, chip, steps):
    return [
        across(lax.dynamic_index_in_dim(total, chip ^ step, 0, keepdims=False), step)
        for step in steps
    ]


def owner_total(total, received, chip):
    result = lax.dynamic_index_in_dim(total, chip, 0, keepdims=False).astype(F)
    for part in received:
        result = result + part.astype(F)
    return result.astype(B)


def rows_of_tokens(served, chips, beside, beside_last):
    halves = len(served[0])
    total = [part.astype(F) for part in served[0]]
    if chips != 4 or halves != 2:
        for step in range(1, chips):
            for k in range(halves):
                total[k] = total[k] + across(served[step][k], step).astype(F)
        return jnp.concatenate(total, axis=0), *beside, *beside_last()
    passing = [across(served[3][0], 2), across(served[3][1], 1)]
    direct = [across(served[2][0], 2), across(served[1][1], 1)]
    passing[0], passing[1], direct[0], direct[1], *beside = together(*passing, *direct, *beside)
    last = [
        across(served[1][0] + passing[0], 1),
        across(served[2][1] + passing[1], 2),
    ]
    last[0], last[1], *after = together(*last, *beside_last())
    total = [a + b.astype(F) + c.astype(F) for a, b, c in zip(total, direct, last)]
    return jnp.concatenate(total, axis=0), *beside, *after


def norm_forward(value, gain, shift):
    centered = value - jnp.mean(value, axis=-1, keepdims=True)
    inverse = lax.rsqrt(jnp.mean(centered * centered, axis=-1, keepdims=True) + LN_EPS)
    normed = centered * inverse
    return (normed * gain + shift, (normed, inverse))


def norm_backward(stored, gain, upstream):
    normed, inverse = stored
    scaled = upstream * gain
    inner = (
        scaled
        - jnp.mean(scaled, axis=-1, keepdims=True)
        - normed * jnp.mean(scaled * normed, axis=-1, keepdims=True)
    )
    return (inverse * inner, jnp.sum(upstream * normed, axis=0), jnp.sum(upstream, axis=0))


def local(
    token_ids,
    segment_ids,
    real_mask,
    positions,
    targets,
    teacher_states,
    head_gate,
    layer_gate,
    hidden_gate,
    unit_gate,
    unit_keep,
    embedding,
    attention,
    feed_forward,
    map_weight,
    norm_params,
    embedding_rows,
    embedding_cols,
    attention_rows,
    attention_cols,
    feed_rows,
    feed_cols,
    map_rows,
    map_cols,
    norm_moment,
):
    unit_count = lax.axis_size("unit")
    chips = unit_count // 2
    unit_at = lax.axis_index("unit")
    data_at = lax.axis_index("dp")
    chip = unit_at // 2
    core = unit_at % 2
    length = token_ids.shape[1]
    pick_count = positions.shape[1]
    breadth = embedding.shape[1]
    vocab_dev = embedding.shape[0]
    units_dev = feed_forward.shape[2]
    layer_count = attention.shape[0]
    slab_rows = breadth // unit_count
    group_first = data_at * unit_count
    place = jnp.stack([chip * 2 * vocab_dev, core]).astype(jnp.int32)

    other_table = swapped(embedding)
    all_ids = jnp.concatenate(
        [token_ids[0]] + [across(token_ids[0], step) for step in range(1, chips)]
    )
    found, ends = scan_ids(all_ids, place, 2 * vocab_dev)
    served = list(lookup(all_ids, place, found, ends, embedding, other_table))
    halves = length // ROW_BLOCK
    own_place = jnp.stack([unit_at * vocab_dev, core]).astype(jnp.int32)
    other_ids = swapped(all_ids)
    table_low = embedding.astype(B)
    attention_low = attention.astype(B)
    map_low = map_weight.astype(B)
    looked, *lows = rows_of_tokens(
        [served[step * halves : (step + 1) * halves] for step in range(chips)],
        chips,
        [table_low, attention_low, map_low, *scan_ids(all_ids, own_place, vocab_dev)],
        lambda: scan_ids(other_ids, own_place, vocab_dev),
    )
    table_low, attention_low, map_low, *lists = lows
    feed_low = []
    for layer_at in range(layer_count):
        own = feed_forward[layer_at].astype(B)
        if layer_at > 0:
            looked, own = together(looked, own)
        feed_low.append(lax.all_gather(own, "unit", axis=1, tiled=True))
    teacher = lax.ppermute(
        teacher_states[0],
        "unit",
        [(u, (u + unit_count // 2) % unit_count) for u in range(unit_count)],
    )
    real_row = lax.dynamic_index_in_dim(real_mask, group_first + unit_at, 0, keepdims=False)
    real_flat = real_row.astype(F)
    count = jnp.sum(real_mask).astype(F)
    scale_all = unit_gate * unit_keep.astype(F)
    segments = segment_ids[0]
    windows = query_windows(segments, QUERY_BLOCK)
    key_segments = jnp.broadcast_to(
        jnp.where(real_row > 0, segments, -1)[:, None], (length, KEY_BLOCK)
    )
    query_segments = jnp.broadcast_to(segments[None, :], (8, length))
    head_scale = jnp.repeat(head_gate, HD, axis=1)

    normed, embed_stored = norm_forward(looked, norm_params[0], norm_params[1])
    hidden = normed * hidden_gate
    stored_layers = []
    for layer_at in range(layer_count):
        hidden_low = hidden.astype(B)
        weights = attention_low[layer_at]
        tokens, features = project(hidden_low, attention_low, layer_at)
        gated_t, log_total = attend(
            windows, head_gate[layer_at], tokens, features, key_segments, query_segments
        )
        branch = jnp.einsum("dr,de->re", gated_t, weights[3], preferred_element_type=F)
        middle, norm_first = norm_forward(
            hidden + branch * layer_gate[layer_at, 0] * hidden_gate,
            norm_params[2 + 4 * layer_at],
            norm_params[3 + 4 * layer_at],
        )
        middle_low = middle.astype(B)
        act, slope, result = feed(middle_low, feed_low[layer_at], scale_all[layer_at])
        if layer_at == 0:
            result, teacher = together(result, teacher)
        hidden, norm_second = norm_forward(
            middle + result * layer_gate[layer_at, 1] * hidden_gate,
            norm_params[4 + 4 * layer_at],
            norm_params[5 + 4 * layer_at],
        )
        stored_layers.append(
            (
                (hidden_low, tokens, features, gated_t, log_total),
                norm_first,
                (middle_low, act, slope),
                norm_second,
            )
        )

    final = hidden.astype(B)
    pick_hot = (positions[0][:, None] == jnp.arange(length)[None, :]).astype(B)
    picked_own = dot(pick_hot, final).astype(B)

    def map_loss(mapped):
        diff = mapped - teacher.astype(F)
        error = jnp.sum(jnp.sum(diff * diff, axis=-1) * real_flat) / breadth
        return error, (diff * (2.0 / (breadth * count)) * real_flat[:, None]).astype(B)

    picked_rows, _, (error_part, grad_mapped) = gathered(
        picked_own, [dot(final, map_low)], map_loss
    )
    picked_rows = picked_rows.reshape(unit_count * pick_count, breadth)
    target_all = jnp.concatenate(
        [
            lax.dynamic_index_in_dim(targets, group_first + (unit_at ^ other), 0, keepdims=False)
            for other in range(unit_count)
        ]
    )
    logits = contract(picked_rows, table_low, NT)
    is_target = (target_all - unit_at * vocab_dev)[:, None] == jnp.arange(vocab_dev)[None, :]
    row_max = jnp.max(logits, axis=1)
    sum_exp = jnp.sum(jnp.exp(logits - row_max[:, None]), axis=1)
    target_logit = jnp.sum(jnp.where(is_target, logits, 0.0), axis=1)
    shares, (grad_map,), (grad_final,) = gathered(
        jnp.stack([row_max, sum_exp, target_logit]).reshape(3, unit_count, pick_count),
        [contract(final, grad_mapped, TN).astype(B)],
        lambda _: (contract(grad_mapped, map_low, NT),),
    )
    shares = shares.reshape(unit_count, 3, unit_count, pick_count)
    shares = jnp.stack(
        [
            jnp.stack([shares[a, :, a ^ b] for a in range(unit_count)])
            for b in range(unit_count)
        ],
        axis=2,
    ).reshape(unit_count, 3, unit_count * pick_count)
    top = jnp.max(shares[:, 0], axis=0)
    log_sum = top + jnp.log(jnp.sum(shares[:, 1] * jnp.exp(shares[:, 0] - top), axis=0))
    own_terms = (log_sum - jnp.sum(shares[:, 2], axis=0))[:pick_count]
    grad_logits = (
        (jnp.exp(logits - log_sum[:, None]) - is_target.astype(F)) / count
    ).astype(B)
    grad_parts = dot(grad_logits, table_low).reshape(chips, 2, pick_count, breadth)
    both = grad_parts[:, 0] + swapped(grad_parts[:, 1])
    grad_picked = both[0]
    for step in range(1, chips):
        grad_picked = grad_picked + across(both[step], step)

    loss_part = error_part + jnp.sum(own_terms)
    grad_hidden = grad_final + lax.dot_general(
        pick_hot.astype(F),
        grad_picked,
        TN,
        precision=lax.Precision.HIGHEST,
        preferred_element_type=F,
    )

    gain_rows = [None] * norm_params.shape[0]
    feed_parts = [None] * layer_count
    attn_parts = [None] * layer_count
    later_feeds = []
    for layer_at in reversed(range(layer_count)):
        attn_stored, norm_first, feed_stored, norm_second = stored_layers[layer_at]
        hidden_low, tokens, features, gated_t, log_total = attn_stored
        middle_low, act, slope = feed_stored
        weights = attention_low[layer_at]
        grad_second, gain_rows[4 + 4 * layer_at], gain_rows[5 + 4 * layer_at] = norm_backward(
            norm_second, norm_params[4 + 4 * layer_at], grad_hidden
        )
        grad_result = (grad_second * layer_gate[layer_at, 1] * hidden_gate).astype(B)
        if layer_at < layer_count - 1:
            grad_result, attn_owned = together(grad_result, attn_owned)
            attn_parts[layer_at + 1] = lax.psum_scatter(attn_owned, "unit")
        grad_middle, feed_owned = feed_back(
            grad_result, middle_low, act, slope, feed_low[layer_at], unit_count
        )
        if layer_at < layer_count - 1:
            grad_middle, later_feed = together(grad_middle, feed_parts[layer_at + 1])
            later_feed = dp_scatter(later_feed.reshape(-1, breadth))
        feed_parts[layer_at] = lax.psum_scatter(feed_owned, "unit")
        grad_first, gain_rows[2 + 4 * layer_at], gain_rows[3 + 4 * layer_at] = norm_backward(
            norm_first, norm_params[2 + 4 * layer_at], grad_second + grad_middle
        )
        grad_branch = (grad_first * layer_gate[layer_at, 0] * hidden_gate).astype(B)
        scale = head_scale[layer_at]
        grad_mixed = (contract(grad_branch, weights[3], NT) * scale).astype(B)
        grad_mixed_t = (contract(weights[3], grad_branch, NT) * scale[:, None]).astype(B)
        grad_proj = attend_back(
            windows,
            tokens,
            features,
            grad_mixed,
            grad_mixed_t,
            key_segments,
            query_segments,
            log_total,
        )
        if layer_at < layer_count - 1:
            grad_proj, later_feed = together(grad_proj, later_feed)
            later_feeds.append(dp_gather(later_feed))
        grad_input = jnp.einsum("jre,jde->rd", grad_proj, weights[:3], preferred_element_type=F)
        grad_hidden = grad_first + grad_input
        grad_hidden, grad_proj = together(grad_hidden, grad_proj)
        grad_in = jnp.einsum(
            "rd,jre->jde", hidden_low, grad_proj, preferred_element_type=F
        ).astype(B)
        grad_out = dot(gated_t, grad_branch).astype(B)
        stack = [grad_in, grad_out[None]]
        if layer_at == layer_count - 1:
            stack.append(grad_map[None])
        stack = jnp.concatenate(stack, axis=0)
        if layer_at > 0:
            attn_owned = jnp.moveaxis(
                stack.reshape(-1, unit_count, slab_rows, breadth), 1, 0
            )
        else:
            stack = stack.reshape(-1, chips, 2, slab_rows, breadth)
            attn_mine = jnp.moveaxis(
                lax.dynamic_index_in_dim(stack, core, 2, keepdims=False), 1, 0
            )
            attn_theirs = jnp.moveaxis(
                lax.dynamic_index_in_dim(stack, 1 - core, 2, keepdims=False), 1, 0
            )

    grad_hidden, grad_logits = together(grad_hidden, grad_logits)
    grad_table = contract(grad_logits, picked_rows, TN)
    grad_looked, gain_rows[0], gain_rows[1] = norm_backward(
        embed_stored, norm_params[0], grad_hidden * hidden_gate
    )
    sent = grad_looked.astype(B)
    small = jnp.concatenate(
        [jnp.stack(gain_rows), jnp.broadcast_to(loss_part, (1, breadth))], axis=0
    )
    same = [(sent, 0), (sent, ROW_BLOCK)]
    other = swapped(sent)
    crossed = [(other, 0), (other, ROW_BLOCK)]
    if chips == 4 and length == 2 * ROW_BLOCK:
        near = [across(sent, 1), across(sent, 2)]
        near, later_feeds, later_attn, grad_table, attn_theirs = together(
            near, later_feeds, attn_parts[1:], grad_table, attn_theirs
        )
        last = [across(near[0][:ROW_BLOCK], 2), across(near[1][ROW_BLOCK:], 1)]
        near_other = [swapped(part) for part in near]
        attn_chip = chip_sum(attn_mine, swapped(attn_theirs))
        later_attn = [dp_scatter(part.reshape(-1, breadth)) for part in later_attn]
        last, near_other, attn_chip, later_attn = together(
            last, near_other, attn_chip, later_attn
        )
        small = dp_sum(small)
        attn_received = sent_to_owners(attn_chip, chip, range(1, chips))
        last_other = [swapped(part) for part in last]
        for home, parts, ends in ((same, near, last), (crossed, near_other, last_other)):
            home += [(part, at) for part in parts for at in (0, ROW_BLOCK)]
            home += [(part, 0) for part in ends]
        later_attn = [dp_gather(part) for part in later_attn]
    else:
        small = dp_sum(small)
        later_attn = [
            dp_gather(dp_scatter(part.reshape(-1, breadth))) for part in attn_parts[1:]
        ]
        attn_chip = chip_sum(attn_mine, swapped(attn_theirs))
        attn_received = sent_to_owners(attn_chip, chip, range(1, chips))
        for step in range(1, chips):
            part = across(sent, step)
            for home, part in ((same, part), (crossed, swapped(part))):
                home += [(part, at) for at in range(0, length, ROW_BLOCK)]
    embed_part = spread(all_ids, other_ids, own_place, lists, grad_table, same + crossed)
    embed_part, attn_received, small, later_attn = together(
        embed_part, attn_received, small, later_attn
    )
    attn_parts[0] = owner_total(attn_chip, attn_received, chip)
    embed_sum, feed_first, attn_first = lax.psum((embed_part, feed_parts[0], attn_parts[0]), "dp")
    attn_sums = [attn_first] + [
        dp_placed(found).reshape(part.shape) for found, part in zip(later_attn, attn_parts[1:])
    ]
    feed_sums = [feed_first] + [
        dp_placed(part).reshape(feed_first.shape) for part in reversed(later_feeds)
    ]
    row_sums = jnp.concatenate(
        [
            jnp.sum(attention_rows, axis=-1).reshape(-1),
            jnp.sum(feed_rows, axis=-1).reshape(-1),
            jnp.sum(map_rows)[None],
            jnp.sum(embedding_rows)[None],
        ]
    )
    row_sums = jnp.pad(row_sums, (0, breadth - row_sums.shape[0]))[None]
    old_cols = jnp.concatenate(
        [
            attention_cols.reshape(-1, breadth),
            feed_cols.reshape(-1, breadth),
            map_cols[None],
            embedding_cols[None],
        ],
        axis=0,
    )
    mats = layer_count * 4
    heights = jnp.array(
        [breadth] * mats
        + [units_dev * unit_count] * (layer_count * 2)
        + [breadth, vocab_dev * unit_count],
        F,
    )[:, None]
    packed = stats(small, row_sums, embed_sum, attn_sums, feed_sums)
    scalars, new_cols, factor, norm_grad, new_norm_params, new_norm_moment = factors(
        lax.all_gather(packed, "unit"), old_cols, heights, norm_params, norm_moment
    )
    total_loss, grad_norm = scalars[0], scalars[1]
    factor = factor[:, None]
    feeds = layer_count * 2
    here = jnp.zeros((1,), jnp.int32)
    slab = jnp.full((1,), unit_at, jnp.int32)
    new_embedding, embed_grad, new_embedding_rows = (
        value[0]
        for value in renew(
            scalars,
            here,
            factor,
            mats + feeds + 1,
            embedding_rows[None],
            embedding[None],
            embed_sum[None],
            1,
            640,
        )
    )
    new_map, map_grad, new_map_rows = (
        value[0]
        for value in renew(
            scalars,
            slab,
            factor,
            mats + feeds,
            map_rows[None],
            map_weight[None],
            attn_sums[layer_count - 1][4:],
            1,
            slab_rows,
        )
    )
    new_attention, attn_grad, new_attention_rows = (
        value.reshape((layer_count, 4) + value.shape[1:])
        for value in renew(
            scalars,
            slab,
            factor,
            0,
            attention_rows.reshape(mats, slab_rows),
            attention.reshape(mats, breadth, breadth),
            jnp.concatenate([part[:4] for part in attn_sums], axis=0),
            4,
            slab_rows,
        )
    )
    new_feed_forward, feed_grad, new_feed_rows = (
        value.reshape((layer_count, 2) + value.shape[1:])
        for value in renew(
            scalars,
            here,
            factor,
            mats,
            feed_rows.reshape(feeds, units_dev),
            feed_forward.reshape(feeds, units_dev, breadth),
            jnp.concatenate(feed_sums, axis=0),
            1,
            units_dev,
        )
    )
    new_attention_cols = new_cols[:mats].reshape(layer_count, 4, breadth)
    new_feed_cols = new_cols[mats : mats + feeds].reshape(layer_count, 2, breadth)
    new_map_cols = new_cols[mats + feeds]
    new_embedding_cols = new_cols[mats + feeds + 1]
    return (
        total_loss,
        count,
        grad_norm,
        new_embedding,
        embed_grad,
        new_embedding_rows,
        new_embedding_cols,
        new_attention,
        attn_grad,
        new_attention_rows,
        new_attention_cols,
        new_feed_forward,
        feed_grad,
        new_feed_rows,
        new_feed_cols,
        new_map,
        map_grad,
        new_map_rows,
        new_map_cols,
        new_norm_params,
        norm_grad,
        new_norm_moment,
    )


def solution(mesh):
    placed = (
        P(("dp", "unit"), None),
        P(("dp", "unit"), None),
        P(),
        P(("dp", "unit"), None),
        P(),
        P(("dp", "unit"), None, None),
        P(),
        P(),
        P(),
        P(),
        P(),
        P("unit", None),
        P(),
        P(None, None, "unit", None),
        P(),
        P(),
        P("unit"),
        P(),
        P(None, None, "unit"),
        P(),
        P(None, None, "unit"),
        P(),
        P("unit"),
        P(),
        P(),
    )
    return jax.shard_map(
        local,
        mesh=mesh,
        in_specs=placed,
        out_specs=(
            P(),
            P(),
            P(),
            P("unit", None),
            P("unit", None),
            P("unit"),
            P(),
            P(None, None, "unit", None),
            P(None, None, "unit", None),
            P(None, None, "unit"),
            P(),
            P(None, None, "unit", None),
            P(None, None, "unit", None),
            P(None, None, "unit"),
            P(),
            P("unit", None),
            P("unit", None),
            P("unit"),
            P(),
            P(),
            P(),
            P(),
        ),
        check_vma=False,
    )
```

```python
import functools
import math

import jax
import jax.numpy as jnp
from jax import lax
from jax.experimental import pallas as pl
from jax.experimental.pallas import tpu as pltpu
from jax.sharding import PartitionSpec as P

H = 12
HD = 64
PAIR = 2 * HD
KEY_BLOCK = 128
QUERY_BLOCK = 256
ROW_BLOCK = 512
UNIT_BLOCK = 768

LN_EPS = 1e-06
ADA_EPS = 1e-30
DECAY_RATE = 0.95
LEARN_RATE = 0.015
CLIP_LIMIT = 0.05
MASK_FILL = 1e30

B = jnp.bfloat16
F = jnp.float32
NT = (((1,), (1,)), ((), ()))
TN = (((0,), (0,)), ((), ()))
TT = (((0,), (1,)), ((), ()))
VMEM_MOST = 58 * 2**20


def dot(left, right):
    return jnp.dot(left, right, preferred_element_type=F)


def contract(left, right, dims):
    return lax.dot_general(left, right, dims, preferred_element_type=F)


def query_windows(segments, block):
    first = segments[::block]
    last = segments[block - 1 :: block]
    start = jnp.sum((segments[None, :] < first[:, None]).astype(jnp.int32), axis=1)
    stop = jnp.sum((segments[None, :] <= last[:, None]).astype(jnp.int32), axis=1)
    low = start // KEY_BLOCK
    high = (stop + KEY_BLOCK - 1) // KEY_BLOCK
    return jnp.concatenate([low, high - low]).astype(jnp.int32)


def most_blocks(length, block):
    return min(length // KEY_BLOCK, block // KEY_BLOCK + 4)


def window_mask(segk_ref, segq_ref, start, width, first_query, block):
    key_seg = segk_ref[pl.ds(start, width), :]
    if block > KEY_BLOCK:
        key_seg = jnp.concatenate([key_seg] * (block // KEY_BLOCK), axis=1)
    query_seg = segq_ref[0:1, pl.ds(first_query, block)]
    key_at = start + lax.broadcasted_iota(jnp.int32, (width, block), 0)
    query_at = first_query + lax.broadcasted_iota(jnp.int32, (width, block), 1)
    return (key_seg == query_seg) | (key_at == query_at)


def head_rows(block):
    empty = jnp.zeros((HD, block.shape[1]), block.dtype)
    first = jnp.concatenate([block[:HD], empty], axis=0)
    second = jnp.concatenate([empty, block[HD:]], axis=0)
    return jnp.concatenate([first, second], axis=1)


def head_lanes(block):
    lane = lax.broadcasted_iota(jnp.int32, block.shape, 1)
    empty = jnp.zeros_like(block)
    return jnp.concatenate(
        [jnp.where(lane < HD, block, empty), jnp.where(lane < HD, empty, block)], axis=0
    )


def attend_kernel(
    window_ref, gate_ref, k_ref, qt_ref, vt_ref, segk_ref, segq_ref, ot_ref, lse_ref, *, block
):
    pair = pl.program_id(0)
    length = k_ref.shape[1]
    count = length // block
    lse_ref[...] = jnp.zeros_like(lse_ref)
    for i in range(count):
        low = window_ref[i]
        number = window_ref[count + i]
        columns = pl.ds(i * block, block)
        for n in range(1, most_blocks(length, block) + 1):

            @pl.when(number == n)
            def _():
                width = n * KEY_BLOCK
                start = pl.multiple_of(low * KEY_BLOCK, KEY_BLOCK)
                keys = k_ref[0, pl.ds(start, width), :]
                mask = window_mask(segk_ref, segq_ref, start, width, i * block, block)
                queries = qt_ref[0, :, columns]
                scores = dot(keys, head_rows(queries))
                scores = jnp.where(jnp.concatenate([mask, mask], axis=1), scores, -MASK_FILL)
                top = jnp.max(scores, axis=0, keepdims=True)
                exponent = jnp.exp(scores - top)
                total = jnp.sum(exponent, axis=0, keepdims=True)
                mixed = dot(vt_ref[0, :, pl.ds(start, width)], exponent.astype(B))
                inverse = 1.0 / total
                log_total = top + jnp.log(total)
                for head in range(2):
                    rows = slice(head * HD, (head + 1) * HD)
                    lanes = slice(head * block, (head + 1) * block)
                    gated = mixed[rows, lanes] * (inverse[:, lanes] * gate_ref[2 * pair + head])
                    ot_ref[rows, columns] = gated.astype(B)
                    lse_ref[0, head : head + 1, columns] = log_total[:, lanes]


def attend(windows, gates, tokens, features, key_segments, query_segments):
    _, length, breadth = tokens.shape
    pairs = breadth // PAIR
    return pl.pallas_call(
        functools.partial(attend_kernel, block=QUERY_BLOCK),
        grid_spec=pltpu.PrefetchScalarGridSpec(
            num_scalar_prefetch=2,
            grid=(pairs,),
            in_specs=[
                pl.BlockSpec((1, length, PAIR), lambda p, *_: (1, 0, p)),
                pl.BlockSpec((1, PAIR, length), lambda p, *_: (0, p, 0)),
                pl.BlockSpec((1, PAIR, length), lambda p, *_: (2, p, 0)),
                pl.BlockSpec((length, KEY_BLOCK), lambda p, *_: (0, 0)),
                pl.BlockSpec((8, length), lambda p, *_: (0, 0)),
            ],
            out_specs=[
                pl.BlockSpec((PAIR, length), lambda p, *_: (p, 0)),
                pl.BlockSpec((1, 8, length), lambda p, *_: (p, 0, 0)),
            ],
        ),
        out_shape=[
            jax.ShapeDtypeStruct((breadth, length), B),
            jax.ShapeDtypeStruct((pairs, 8, length), F),
        ],
        compiler_params=pltpu.CompilerParams(vmem_limit_bytes=VMEM_MOST),
        cost_estimate=pl.CostEstimate(
            flops=2 * 2 * 2 * length * 512 * breadth,
            bytes_accessed=8 * length * breadth,
            transcendentals=length * 512 * 12,
        ),
        name="attend",
    )(windows, gates, tokens, features, features, key_segments, query_segments)


def attend_back_kernel(
    window_ref,
    k_ref,
    kt_ref,
    q_ref,
    qt_ref,
    v_ref,
    do_ref,
    dot_ref,
    segk_ref,
    segq_ref,
    lse_ref,
    grad_ref,
    dq_sum,
    dk_sum,
    dv_sum,
    *,
    block,
    score_scale,
):
    length = k_ref.shape[1]
    count = length // block
    dk_sum[...] = jnp.zeros_like(dk_sum)
    dv_sum[...] = jnp.zeros_like(dv_sum)
    for i in range(count):
        low = window_ref[i]
        number = window_ref[count + i]
        columns = pl.ds(i * block, block)
        for n in range(1, most_blocks(length, block) + 1):

            @pl.when(number == n)
            def _():
                width = n * KEY_BLOCK
                start = pl.multiple_of(low * KEY_BLOCK, KEY_BLOCK)
                window = pl.ds(start, width)
                keys = k_ref[0, window, :]
                values = v_ref[0, window, :]
                mask = window_mask(segk_ref, segq_ref, start, width, i * block, block)
                queries_t = qt_ref[0, :, columns]
                grads_t = dot_ref[:, columns]
                scores = dot(keys, head_rows(queries_t))
                scores = jnp.where(jnp.concatenate([mask, mask], axis=1), scores, -MASK_FILL)
                log_total = jnp.concatenate(
                    [lse_ref[0, 0:1, columns], lse_ref[0, 1:2, columns]], axis=1
                )
                prob = jnp.exp(scores - log_total)
                weighted = prob * dot(values, head_rows(grads_t))
                inner = jnp.sum(weighted, axis=0, keepdims=True)
                grad = (weighted - prob * inner).astype(B)
                grad_q = dot(kt_ref[0, :, window], grad) * score_scale
                dq_sum[:HD, columns] = grad_q[:HD, :block]
                dq_sum[HD:, columns] = grad_q[HD:, block:]
                dv_sum[window, :] += dot(prob.astype(B), head_lanes(do_ref[columns, :]))
                dk_sum[window, :] += dot(grad, head_lanes(q_ref[0, columns, :]))

    grad_ref[0] = jnp.transpose(dq_sum[...]).astype(B)
    grad_ref[1] = dk_sum[...].astype(B)
    grad_ref[2] = dv_sum[...].astype(B)


def attend_back(
    windows, tokens, features, grads, grads_t, key_segments, query_segments, log_total
):
    _, length, breadth = tokens.shape
    pairs = breadth // PAIR

    def token_spec(which):
        return pl.BlockSpec((1, length, PAIR), lambda p, *_: (which, 0, p))

    def feature_spec(which):
        return pl.BlockSpec((1, PAIR, length), lambda p, *_: (which, p, 0))

    return pl.pallas_call(
        functools.partial(
            attend_back_kernel, block=QUERY_BLOCK, score_scale=1.0 / math.sqrt(HD)
        ),
        grid_spec=pltpu.PrefetchScalarGridSpec(
            num_scalar_prefetch=1,
            grid=(pairs,),
            in_specs=[
                token_spec(1),
                feature_spec(1),
                token_spec(0),
                feature_spec(0),
                token_spec(2),
                pl.BlockSpec((length, PAIR), lambda p, *_: (0, p)),
                pl.BlockSpec((PAIR, length), lambda p, *_: (p, 0)),
                pl.BlockSpec((length, KEY_BLOCK), lambda p, *_: (0, 0)),
                pl.BlockSpec((8, length), lambda p, *_: (0, 0)),
                pl.BlockSpec((1, 8, length), lambda p, *_: (p, 0, 0)),
            ],
            out_specs=pl.BlockSpec((3, length, PAIR), lambda p, *_: (0, 0, p)),
            scratch_shapes=[
                pltpu.VMEM((PAIR, length), F),
                pltpu.VMEM((length, PAIR), F),
                pltpu.VMEM((length, PAIR), F),
            ],
        ),
        out_shape=jax.ShapeDtypeStruct((3, length, breadth), B),
        compiler_params=pltpu.CompilerParams(vmem_limit_bytes=VMEM_MOST),
        cost_estimate=pl.CostEstimate(
            flops=5 * 2 * 2 * length * 512 * breadth,
            bytes_accessed=20 * length * breadth,
            transcendentals=length * 512 * 12,
        ),
        name="attend_back",
    )(
        windows,
        tokens,
        features,
        tokens,
        features,
        tokens,
        grads,
        grads_t,
        key_segments,
        query_segments,
        log_total,
    )


def project_kernel(x_ref, weight_ref, tokens_ref, features_ref, *, score_scale):
    scale = jnp.where(pl.program_id(0) == 0, score_scale, 1.0).astype(F)
    tokens = dot(x_ref[...], weight_ref[...]).astype(B).astype(F)
    tokens_ref[0] = (tokens * scale).astype(B)
    features = contract(weight_ref[...], x_ref[...], TT).astype(B).astype(F)
    features_ref[0] = (features * scale).astype(B)


def project(x, weights, layer):
    length, breadth = x.shape
    return pl.pallas_call(
        functools.partial(project_kernel, score_scale=1.0 / math.sqrt(HD)),
        grid=(3,),
        in_specs=[
            pl.BlockSpec((length, breadth), lambda j: (0, 0)),
            pl.BlockSpec((None, None, breadth, breadth), lambda j: (layer, j, 0, 0)),
        ],
        out_specs=[
            pl.BlockSpec((1, length, breadth), lambda j: (j, 0, 0)),
            pl.BlockSpec((1, breadth, length), lambda j: (j, 0, 0)),
        ],
        out_shape=[
            jax.ShapeDtypeStruct((3, length, breadth), B),
            jax.ShapeDtypeStruct((3, breadth, length), B),
        ],
        compiler_params=pltpu.CompilerParams(vmem_limit_bytes=VMEM_MOST),
        cost_estimate=pl.CostEstimate(
            flops=12 * length * breadth * breadth,
            bytes_accessed=14 * length * breadth + 6 * breadth * breadth,
            transcendentals=0,
        ),
        name="project",
    )(x, weights)


def gelu_and_slope(value):
    density = jnp.exp(value * value * -0.5)
    ratio = pl.reciprocal(1.0 + jnp.abs(value) * (0.3275911 * math.sqrt(0.5)))
    series = ratio * (
        0.127414796
        + ratio
        * (-0.142248368 + ratio * (0.7107068705 + ratio * (-0.7265760135 + ratio * 0.5307027145)))
    )
    tail = series * density
    below = jnp.where(value >= 0, 1.0 - tail, tail)
    return value * below, below + value * density * (1.0 / math.sqrt(2.0 * math.pi))


def feed_kernel(x_ref, up_ref, down_ref, scale_ref, act_ref, slope_ref, out_ref):
    first = pl.program_id(0) == 0
    scale = scale_ref[0]
    act, slope = gelu_and_slope(contract(x_ref[...], up_ref[...], NT))
    act = (act * scale).astype(B)
    act_ref[...] = act
    slope_ref[...] = (slope * scale).astype(B)
    part = dot(act, down_ref[...])

    @pl.when(first)
    def _():
        out_ref[...] = part

    @pl.when(jnp.logical_not(first))
    def _():
        out_ref[...] += part


def feed(x, weights, scale):
    length, breadth = x.shape
    units = weights.shape[1]
    block = UNIT_BLOCK
    return pl.pallas_call(
        feed_kernel,
        grid=(units // block,),
        in_specs=[
            pl.BlockSpec((length, breadth), lambda j: (0, 0)),
            pl.BlockSpec((None, block, breadth), lambda j: (0, j, 0)),
            pl.BlockSpec((None, block, breadth), lambda j: (1, j, 0)),
            pl.BlockSpec((1, 1, block), lambda j: (0, 0, j)),
        ],
        out_specs=[
            pl.BlockSpec((length, block), lambda j: (0, j)),
            pl.BlockSpec((length, block), lambda j: (0, j)),
            pl.BlockSpec((length, breadth), lambda j: (0, 0)),
        ],
        out_shape=[
            jax.ShapeDtypeStruct((length, units), B),
            jax.ShapeDtypeStruct((length, units), B),
            jax.ShapeDtypeStruct((length, breadth), F),
        ],
        compiler_params=pltpu.CompilerParams(vmem_limit_bytes=VMEM_MOST),
        cost_estimate=pl.CostEstimate(
            flops=4 * length * breadth * units,
            bytes_accessed=4 * (length + breadth) * units + 6 * length * breadth,
            transcendentals=2 * length * units,
        ),
        name="feed",
    )(x, weights, weights, scale.reshape(1, 1, units))


def feed_back_kernel(
    grad_ref, x_ref, act_ref, slope_ref, up_ref, down_ref, out_ref, owned_ref, pre_grad
):
    first = pl.program_id(0) == 0
    grad_act = contract(grad_ref[...], down_ref[...], NT)
    grad_pre = (grad_act * slope_ref[...].astype(F)).astype(B)
    pre_grad[...] = grad_pre
    part = dot(grad_pre, up_ref[...])

    @pl.when(first)
    def _():
        out_ref[...] = part

    @pl.when(jnp.logical_not(first))
    def _():
        out_ref[...] += part

    grads = (
        contract(pre_grad[...], x_ref[...], TN).astype(B),
        contract(act_ref[...], grad_ref[...], TN).astype(B),
    )
    owners, _, share, _ = owned_ref.shape
    for which in range(2):
        for owner in range(owners):
            owned_ref[owner, which] = grads[which][owner * share : (owner + 1) * share]


def feed_back(grad, x, act, slope, weights, owners):
    length, breadth = x.shape
    units = weights.shape[1]
    share = units // owners
    block = UNIT_BLOCK
    lanes = pl.BlockSpec((length, block), lambda j: (0, j))
    whole = pl.BlockSpec((length, breadth), lambda j: (0, 0))
    return pl.pallas_call(
        feed_back_kernel,
        grid=(units // block,),
        in_specs=[
            whole,
            whole,
            lanes,
            lanes,
            pl.BlockSpec((None, block, breadth), lambda j: (0, j, 0)),
            pl.BlockSpec((None, block, breadth), lambda j: (1, j, 0)),
        ],
        out_specs=[
            whole,
            pl.BlockSpec((block // share, 2, share, breadth), lambda j: (j, 0, 0, 0)),
        ],
        scratch_shapes=[pltpu.VMEM((length, block), B)],
        out_shape=[
            jax.ShapeDtypeStruct((length, breadth), F),
            jax.ShapeDtypeStruct((owners, 2, share, breadth), B),
        ],
        compiler_params=pltpu.CompilerParams(vmem_limit_bytes=VMEM_MOST),
        cost_estimate=pl.CostEstimate(
            flops=8 * length * breadth * units,
            bytes_accessed=4 * (length + 2 * breadth) * units + 8 * length * breadth,
            transcendentals=0,
        ),
        name="feed_back",
    )(grad, x, act, slope, weights, weights)


def scan_kernel(ids, place, found, ends, *, vocab):
    base = place[0]
    blocks = ends.shape[0]
    streams = math.gcd(blocks, 8)
    for first in range(0, blocks, streams):

        def scan(t, counts):
            after = []
            for k, count in enumerate(counts):
                at = (first + k) * ROW_BLOCK + t
                relative = (ids[at] - base).astype(jnp.uint32)
                found[count] = at
                after.append(count + jnp.where(relative < jnp.uint32(vocab), 1, 0))
            return tuple(after)

        begin = tuple(jnp.int32((first + k) * ROW_BLOCK) for k in range(streams))
        counts = lax.fori_loop(0, ROW_BLOCK, scan, begin, unroll=4)
        for k, count in enumerate(counts):
            ends[first + k] = count


def scan_ids(ids, place, vocab):
    smem = pl.BlockSpec(memory_space=pltpu.SMEM)
    return pl.pallas_call(
        functools.partial(scan_kernel, vocab=vocab),
        in_specs=[smem, smem],
        out_specs=[smem, smem],
        out_shape=[
            jax.ShapeDtypeStruct(ids.shape, jnp.int32),
            jax.ShapeDtypeStruct((ids.shape[0] // ROW_BLOCK,), jnp.int32),
        ],
        name="scan_ids",
    )(ids, place)


def lookup_kernel(ids, place, found, ends, own, other, *rest, blocks, vocab):
    outs = rest[:blocks]
    table, rows, stage, table_sem, out_sem = rest[blocks:]
    base = place[0]
    core = place[1]
    mine = pl.multiple_of(core * vocab, 8)
    theirs = pl.multiple_of((1 - core) * vocab, 8)
    loads = [
        pltpu.make_async_copy(own, table.at[pl.ds(mine, vocab)], table_sem.at[0]),
        pltpu.make_async_copy(other, table.at[pl.ds(theirs, vocab)], table_sem.at[1]),
    ]
    for load in loads:
        load.start()
    for load in loads:
        load.wait()
    copies = [None, None]
    for k in range(blocks):
        rows[...] = jnp.zeros_like(rows)

        def put(entry, carry):
            t = found[entry]
            rows[pl.ds(t - k * ROW_BLOCK, 1), :] = table[pl.ds(ids[t] - base, 1), :]
            return carry

        each_entry(k * ROW_BLOCK, ends[k], put)
        slot = k % 2
        if copies[slot] is not None:
            copies[slot].wait()
        stage[slot] = rows[...].astype(B)
        copies[slot] = pltpu.make_async_copy(stage.at[slot], outs[k], out_sem.at[slot])
        copies[slot].start()
    for copy in copies:
        copy.wait()


def each_entry(low, high, body):
    quads = lax.div(high - low, 4)

    def four(e, carry):
        for j in range(4):
            body(low + e * 4 + j, 0)
        return carry

    lax.fori_loop(0, quads, four, 0)
    lax.fori_loop(low + quads * 4, high, body, 0)


def lookup(ids, place, found, ends, own, other):
    vocab, breadth = own.shape
    blocks = ids.shape[0] // ROW_BLOCK
    hbm = pl.BlockSpec(memory_space=pl.ANY)
    smem = pl.BlockSpec(memory_space=pltpu.SMEM)
    return pl.pallas_call(
        functools.partial(lookup_kernel, blocks=blocks, vocab=vocab),
        in_specs=[smem] * 4 + [hbm] * 2,
        out_specs=[hbm] * blocks,
        out_shape=[jax.ShapeDtypeStruct((ROW_BLOCK, breadth), B)] * blocks,
        scratch_shapes=[
            pltpu.VMEM((2 * vocab, breadth), F),
            pltpu.VMEM((ROW_BLOCK, breadth), F),
            pltpu.VMEM((2, ROW_BLOCK, breadth), B),
            pltpu.SemaphoreType.DMA((2,)),
            pltpu.SemaphoreType.DMA((2,)),
        ],
        compiler_params=pltpu.CompilerParams(vmem_limit_bytes=VMEM_MOST),
        cost_estimate=pl.CostEstimate(
            flops=0,
            bytes_accessed=8 * vocab * breadth + 2 * ids.shape[0] * breadth,
            transcendentals=0,
        ),
        name="lookup",
    )(ids, place, found, ends, own, other)


def spread_kernel(
    ids, other_ids, place, found, ends, other_found, other_ends, begin, *rest, pieces
):
    blocks = len(pieces)
    arrays = max(which for which, _ in pieces) + 1
    grads = [rest[which].at[pl.ds(at, ROW_BLOCK)] for which, at in pieces]
    out, total, rows, stage, half, sem, in_sem, out_sem = rest[arrays:]
    base = place[0]
    vocab = total.shape[0]
    fill = pltpu.make_async_copy(begin, total, sem.at[0])
    fill.start()

    def load(k):
        copy = pltpu.make_async_copy(grads[k], stage.at[k % 2], in_sem.at[k % 2])
        copy.start()
        return copy

    coming = load(0)
    fill.wait()
    for k in range(blocks):
        coming.wait()
        if k + 1 < blocks:
            coming = load(k + 1)
        rows[...] = stage[k % 2].astype(F)

        lists = (ids, found, ends) if k < blocks // 2 else (other_ids, other_found, other_ends)
        first = k % (blocks // 2) * ROW_BLOCK

        def add(entry, carry):
            t = lists[1][entry]
            at = pl.ds(lists[0][t] - base, 1)
            total[at, :] += rows[pl.ds(t - first, 1), :]
            return carry

        each_entry(first, lists[2][k % (blocks // 2)], add)
    step = half.shape[1]
    copies = [None, None]
    for j in range(vocab // step):
        slot = j % 2
        if copies[slot] is not None:
            copies[slot].wait()
        half[slot] = total[j * step : (j + 1) * step, :].astype(B)
        copies[slot] = pltpu.make_async_copy(
            half.at[slot], out.at[pl.ds(j * step, step)], out_sem.at[slot]
        )
        copies[slot].start()
    for copy in copies:
        copy.wait()


def spread(ids, other_ids, place, lists, begin, grads):
    vocab, breadth = begin.shape
    arrays = []
    pieces = []
    for array, at in grads:
        known = [k for k, other in enumerate(arrays) if other is array]
        if not known:
            known = [len(arrays)]
            arrays.append(array)
        pieces.append((known[0], at))
    hbm = pl.BlockSpec(memory_space=pl.ANY)
    smem = pl.BlockSpec(memory_space=pltpu.SMEM)
    return pl.pallas_call(
        functools.partial(spread_kernel, pieces=tuple(pieces)),
        in_specs=[smem] * 7 + [hbm] * (1 + len(arrays)),
        out_specs=hbm,
        out_shape=jax.ShapeDtypeStruct((vocab, breadth), B),
        scratch_shapes=[
            pltpu.VMEM((vocab, breadth), F),
            pltpu.VMEM((ROW_BLOCK, breadth), F),
            pltpu.VMEM((2, ROW_BLOCK, breadth), B),
            pltpu.VMEM((2, vocab // 4, breadth), B),
            pltpu.SemaphoreType.DMA((1,)),
            pltpu.SemaphoreType.DMA((2,)),
            pltpu.SemaphoreType.DMA((2,)),
        ],
        compiler_params=pltpu.CompilerParams(vmem_limit_bytes=VMEM_MOST),
        cost_estimate=pl.CostEstimate(
            flops=0,
            bytes_accessed=6 * vocab * breadth + 2 * len(grads) * ROW_BLOCK * breadth,
            transcendentals=0,
        ),
        name="spread",
    )(ids, other_ids, place, *lists, begin, *arrays)


def stats_kernel(small_ref, row_sums_ref, embed_ref, *rest, layers):
    attn = rest[:layers]
    feeds = rest[layers : 2 * layers]
    out_ref = rest[2 * layers]
    norms = small_ref.shape[0]
    cols = jnp.sum(jnp.square(embed_ref[...].astype(F)), axis=0, keepdims=True)

    @pl.when(pl.program_id(0) == 0)
    def _():
        def put(row, value):
            out_ref[row : row + 1, :] = jnp.sum(
                jnp.square(value.astype(F)), axis=0, keepdims=True
            )

        out_ref[:norms, :] = small_ref[...]
        row = norms
        for parts, count in ((attn, 4), (feeds, 2)):
            for part in parts:
                for k in range(count):
                    put(row, part[k])
                    row += 1
        put(row, attn[layers - 1][4])
        out_ref[row + 1 : row + 2, :] = cols
        row += 2
        out_ref[row : row + 1, :] = row_sums_ref[...]

    @pl.when(pl.program_id(0) > 0)
    def _():
        at = norms + 6 * layers + 1
        out_ref[at : at + 1, :] += cols


def stats(small, row_sums, embed, attn, feeds):
    height, breadth = embed.shape
    block = math.gcd(height, 480)
    rows = small.shape[0] + 3 + 6 * len(attn)
    vmem = pl.BlockSpec(memory_space=pltpu.VMEM)
    return pl.pallas_call(
        functools.partial(stats_kernel, layers=len(attn)),
        grid=(height // block,),
        in_specs=[vmem, vmem, pl.BlockSpec((block, breadth), lambda j: (j, 0))]
        + [vmem] * (2 * len(attn)),
        out_specs=pl.BlockSpec((rows, breadth), lambda j: (0, 0)),
        out_shape=jax.ShapeDtypeStruct((rows, breadth), F),
        compiler_params=pltpu.CompilerParams(vmem_limit_bytes=VMEM_MOST),
        name="stats",
    )(small, row_sums, embed, *attn, *feeds)


def factors_kernel(
    parts_ref,
    cols_ref,
    heights_ref,
    params_ref,
    moment_ref,
    scalars_ref,
    new_cols_ref,
    factor_ref,
    norm_grad_ref,
    new_params_ref,
    new_moment_ref,
):
    packed = parts_ref[0]
    for k in range(1, parts_ref.shape[0]):
        packed = packed + parts_ref[k]
    norms = params_ref.shape[0]
    mats, breadth = cols_ref.shape
    norm_grads = packed[:norms]
    col_sums = packed[norms + 1 : norms + 1 + mats]
    lane = lax.broadcasted_iota(jnp.int32, (mats, breadth), 1)
    row = lax.broadcasted_iota(jnp.int32, (mats, breadth), 0)
    row_sums = jnp.sum(
        jnp.where(lane == row, packed[norms + 1 + mats :], 0.0), axis=1, keepdims=True
    )
    heights = heights_ref[...]
    mat_sums = jnp.sum(col_sums, axis=1, keepdims=True)
    square = jnp.sum(mat_sums, axis=0, keepdims=True) + jnp.sum(
        jnp.sum(norm_grads * norm_grads, axis=1, keepdims=True), axis=0, keepdims=True
    )
    norm = jnp.sqrt(square)
    clip = jnp.minimum(1.0, CLIP_LIMIT / norm)
    scalars_ref[0] = packed[norms, 0]
    scalars_ref[1] = norm[0, 0]
    scalars_ref[2] = clip[0, 0]
    new_cols = DECAY_RATE * cols_ref[...] + (1 - DECAY_RATE) * (
        clip * clip * col_sums / heights + ADA_EPS
    )
    mean_rows = DECAY_RATE * row_sums / heights + (1 - DECAY_RATE) * (
        clip * clip * mat_sums / (heights * breadth) + ADA_EPS
    )
    new_cols_ref[...] = new_cols
    factor_ref[...] = LEARN_RATE * jnp.sqrt(mean_rows) * lax.rsqrt(new_cols)
    norm_grad = norm_grads * clip
    moment = DECAY_RATE * moment_ref[...] + (1 - DECAY_RATE) * (norm_grad * norm_grad + ADA_EPS)
    norm_grad_ref[...] = norm_grad
    new_moment_ref[...] = moment
    new_params_ref[...] = params_ref[...] - LEARN_RATE * norm_grad * lax.rsqrt(moment)


def factors(parts, cols, heights, params, moment):
    vmem = pl.BlockSpec(memory_space=pltpu.VMEM)
    like = [jax.ShapeDtypeStruct(x.shape, F) for x in (cols, cols, params, params, params)]
    return pl.pallas_call(
        factors_kernel,
        in_specs=[vmem] * 5,
        out_specs=[pl.BlockSpec(memory_space=pltpu.SMEM)] + [vmem] * 5,
        out_shape=[jax.ShapeDtypeStruct((3,), F)] + like,
        compiler_params=pltpu.CompilerParams(vmem_limit_bytes=VMEM_MOST),
        name="factors",
    )(parts, cols, heights, params, moment)


def renew_kernel(
    scalars_ref, at_ref, factor_ref, rows_ref, weight_ref, sum_ref, new_ref, grad_ref, new_rows_ref
):
    for m in range(sum_ref.shape[0]):
        grad = sum_ref[m].astype(F) * scalars_ref[2]
        mean = jnp.mean(grad * grad, axis=1, keepdims=True) + ADA_EPS
        new_rows = DECAY_RATE * rows_ref[m] + (1 - DECAY_RATE) * mean
        wide = jnp.broadcast_to(new_rows, (new_rows.shape[0], 128))
        new_rows_ref[m, 0] = jnp.transpose(wide)[:1]
        grad_ref[m] = grad
        new_ref[m] = weight_ref[m] - grad * lax.rsqrt(new_rows) * factor_ref[m]


def renew(scalars, at, factor, first, rows, weight, total, group, most):
    mats, height, breadth = total.shape
    block = math.gcd(height, most)
    per = height // block
    wide = pl.BlockSpec((group, block, breadth), lambda m, j, *_: (m, j, 0))
    new, grad, new_rows = pl.pallas_call(
        renew_kernel,
        grid_spec=pltpu.PrefetchScalarGridSpec(
            num_scalar_prefetch=2,
            grid=(mats // group, per),
            in_specs=[
                pl.BlockSpec((group, 1, breadth), lambda m, j, *_: (first // group + m, 0, 0)),
                pl.BlockSpec((group, block, 1), lambda m, j, *_: (m, j, 0)),
                pl.BlockSpec(
                    (group, block, breadth), lambda m, j, scalars, at: (m, at[0] * per + j, 0)
                ),
                wide,
            ],
            out_specs=[
                wide,
                wide,
                pl.BlockSpec((group, 1, 1, block), lambda m, j, *_: (m, j, 0, 0)),
            ],
        ),
        out_shape=[
            jax.ShapeDtypeStruct((mats, height, breadth), F),
            jax.ShapeDtypeStruct((mats, height, breadth), F),
            jax.ShapeDtypeStruct((mats, per, 1, block), F),
        ],
        compiler_params=pltpu.CompilerParams(vmem_limit_bytes=VMEM_MOST),
        name="renew",
    )(scalars, at, factor, rows[..., None], weight, total)
    return new, grad, new_rows.reshape(rows.shape)


def across(value, step):
    pairs = [(u, ((u // 2) ^ step) * 2 + u % 2) for u in range(lax.axis_size("unit"))]
    return lax.ppermute(value, "unit", pairs)


def swapped(value):
    return lax.ppermute(value, "unit", [(u, u ^ 1) for u in range(lax.axis_size("unit"))])


def gathered(value, beside_core, beside_chip):
    other, *beside_core = together(swapped(value), *beside_core)
    both = jnp.stack([value, other])
    chips = lax.axis_size("unit") // 2
    parts = [across(both, step) for step in range(1, chips)]
    if beside_chip:
        parts[0], *beside_chip = together(parts[0], *beside_chip(*beside_core))
    return jnp.stack([both] + parts), beside_core, beside_chip


def dp_scatter(value):
    size = lax.axis_size("dp")
    at = lax.axis_index("dp")
    share = value.shape[0] // size
    parts = [lax.dynamic_slice_in_dim(value, at * share, share, 0)]
    for step in range(1, size):
        away = lax.dynamic_slice_in_dim(value, (at + step) % size * share, share, 0)
        parts.append(lax.ppermute(away, "dp", [(d, (d + step) % size) for d in range(size)]))
    return parts


def dp_gather(parts):
    size = lax.axis_size("dp")
    at = lax.axis_index("dp")
    total = parts[0].astype(F)
    for part in parts[1:]:
        total = total + part.astype(F)
    total = total.astype(B)
    found = [total] + [
        lax.ppermute(total, "dp", [(d, (d + step) % size) for d in range(size)])
        for step in range(1, size)
    ]
    return found


def dp_placed(found):
    size = len(found)
    at = lax.axis_index("dp")
    share = found[0].shape[0]
    result = jnp.zeros((size * share,) + found[0].shape[1:], found[0].dtype)
    for step, part in enumerate(found):
        result = lax.dynamic_update_slice_in_dim(result, part, (at - step) % size * share, 0)
    return result


def dp_sum(value):
    size = lax.axis_size("dp")
    if size & (size - 1):
        return lax.psum(value, "dp")
    step = 1
    while step < size:
        value = value + lax.ppermute(value, "dp", [(d, d ^ step) for d in range(size)])
        step = 2 * step
    return value


def together(*values):
    return lax.optimization_barrier(values)


def chip_sum(mine, swapped_theirs):
    return (mine.astype(F) + swapped_theirs.astype(F)).astype(B)


def sent_to_owners(total, chip, steps):
    return [
        across(lax.dynamic_index_in_dim(total, chip ^ step, 0, keepdims=False), step)
        for step in steps
    ]


def owner_total(total, received, chip):
    result = lax.dynamic_index_in_dim(total, chip, 0, keepdims=False).astype(F)
    for part in received:
        result = result + part.astype(F)
    return result.astype(B)


def rows_of_tokens(served, chips, beside, beside_last):
    halves = len(served[0])
    total = [part.astype(F) for part in served[0]]
    if chips != 4 or halves != 2:
        for step in range(1, chips):
            for k in range(halves):
                total[k] = total[k] + across(served[step][k], step).astype(F)
        return jnp.concatenate(total, axis=0), *beside, *beside_last()
    passing = [across(served[3][0], 2), across(served[3][1], 1)]
    direct = [across(served[2][0], 2), across(served[1][1], 1)]
    passing[0], passing[1], direct[0], direct[1], *beside = together(*passing, *direct, *beside)
    last = [
        across(served[1][0] + passing[0], 1),
        across(served[2][1] + passing[1], 2),
    ]
    last[0], last[1], *after = together(*last, *beside_last())
    total = [a + b.astype(F) + c.astype(F) for a, b, c in zip(total, direct, last)]
    return jnp.concatenate(total, axis=0), *beside, *after


def norm_forward(value, gain, shift):
    centered = value - jnp.mean(value, axis=-1, keepdims=True)
    inverse = lax.rsqrt(jnp.mean(centered * centered, axis=-1, keepdims=True) + LN_EPS)
    normed = centered * inverse
    return (normed * gain + shift, (normed, inverse))


def norm_backward(stored, gain, upstream):
    normed, inverse = stored
    scaled = upstream * gain
    inner = (
        scaled
        - jnp.mean(scaled, axis=-1, keepdims=True)
        - normed * jnp.mean(scaled * normed, axis=-1, keepdims=True)
    )
    return (inverse * inner, jnp.sum(upstream * normed, axis=0), jnp.sum(upstream, axis=0))


def local(
    token_ids,
    segment_ids,
    real_mask,
    positions,
    targets,
    teacher_states,
    head_gate,
    layer_gate,
    hidden_gate,
    unit_gate,
    unit_keep,
    embedding,
    attention,
    feed_forward,
    map_weight,
    norm_params,
    embedding_rows,
    embedding_cols,
    attention_rows,
    attention_cols,
    feed_rows,
    feed_cols,
    map_rows,
    map_cols,
    norm_moment,
):
    unit_count = lax.axis_size("unit")
    chips = unit_count // 2
    unit_at = lax.axis_index("unit")
    data_at = lax.axis_index("dp")
    chip = unit_at // 2
    core = unit_at % 2
    length = token_ids.shape[1]
    pick_count = positions.shape[1]
    breadth = embedding.shape[1]
    vocab_dev = embedding.shape[0]
    units_dev = feed_forward.shape[2]
    layer_count = attention.shape[0]
    slab_rows = breadth // unit_count
    group_first = data_at * unit_count
    place = jnp.stack([chip * 2 * vocab_dev, core]).astype(jnp.int32)

    other_table = swapped(embedding)
    all_ids = jnp.concatenate(
        [token_ids[0]] + [across(token_ids[0], step) for step in range(1, chips)]
    )
    found, ends = scan_ids(all_ids, place, 2 * vocab_dev)
    served = list(lookup(all_ids, place, found, ends, embedding, other_table))
    halves = length // ROW_BLOCK
    own_place = jnp.stack([unit_at * vocab_dev, core]).astype(jnp.int32)
    other_ids = swapped(all_ids)
    table_low = embedding.astype(B)
    attention_low = attention.astype(B)
    map_low = map_weight.astype(B)
    looked, *lows = rows_of_tokens(
        [served[step * halves : (step + 1) * halves] for step in range(chips)],
        chips,
        [table_low, attention_low, map_low, *scan_ids(all_ids, own_place, vocab_dev)],
        lambda: scan_ids(other_ids, own_place, vocab_dev),
    )
    table_low, attention_low, map_low, *lists = lows
    feed_low = []
    for layer_at in range(layer_count):
        own = feed_forward[layer_at].astype(B)
        if layer_at > 0:
            looked, own = together(looked, own)
        feed_low.append(lax.all_gather(own, "unit", axis=1, tiled=True))
    teacher = lax.ppermute(
        teacher_states[0],
        "unit",
        [(u, (u + unit_count // 2) % unit_count) for u in range(unit_count)],
    )
    real_row = lax.dynamic_index_in_dim(real_mask, group_first + unit_at, 0, keepdims=False)
    real_flat = real_row.astype(F)
    count = jnp.sum(real_mask).astype(F)
    scale_all = unit_gate * unit_keep.astype(F)
    segments = segment_ids[0]
    windows = query_windows(segments, QUERY_BLOCK)
    key_segments = jnp.broadcast_to(
        jnp.where(real_row > 0, segments, -1)[:, None], (length, KEY_BLOCK)
    )
    query_segments = jnp.broadcast_to(segments[None, :], (8, length))
    head_scale = jnp.repeat(head_gate, HD, axis=1)

    normed, embed_stored = norm_forward(looked, norm_params[0], norm_params[1])
    hidden = normed * hidden_gate
    stored_layers = []
    for layer_at in range(layer_count):
        hidden_low = hidden.astype(B)
        weights = attention_low[layer_at]
        tokens, features = project(hidden_low, attention_low, layer_at)
        gated_t, log_total = attend(
            windows, head_gate[layer_at], tokens, features, key_segments, query_segments
        )
        branch = jnp.einsum("dr,de->re", gated_t, weights[3], preferred_element_type=F)
        middle, norm_first = norm_forward(
            hidden + branch * layer_gate[layer_at, 0] * hidden_gate,
            norm_params[2 + 4 * layer_at],
            norm_params[3 + 4 * layer_at],
        )
        middle_low = middle.astype(B)
        act, slope, result = feed(middle_low, feed_low[layer_at], scale_all[layer_at])
        if layer_at == 0:
            result, teacher = together(result, teacher)
        hidden, norm_second = norm_forward(
            middle + result * layer_gate[layer_at, 1] * hidden_gate,
            norm_params[4 + 4 * layer_at],
            norm_params[5 + 4 * layer_at],
        )
        stored_layers.append(
            (
                (hidden_low, tokens, features, gated_t, log_total),
                norm_first,
                (middle_low, act, slope),
                norm_second,
            )
        )

    final = hidden.astype(B)
    pick_hot = (positions[0][:, None] == jnp.arange(length)[None, :]).astype(B)
    picked_own = dot(pick_hot, final).astype(B)

    def map_loss(mapped):
        diff = mapped - teacher.astype(F)
        error = jnp.sum(jnp.sum(diff * diff, axis=-1) * real_flat) / breadth
        return error, (diff * (2.0 / (breadth * count)) * real_flat[:, None]).astype(B)

    picked_rows, _, (error_part, grad_mapped) = gathered(
        picked_own, [dot(final, map_low)], map_loss
    )
    picked_rows = picked_rows.reshape(unit_count * pick_count, breadth)
    target_all = jnp.concatenate(
        [
            lax.dynamic_index_in_dim(targets, group_first + (unit_at ^ other), 0, keepdims=False)
            for other in range(unit_count)
        ]
    )
    logits = contract(picked_rows, table_low, NT)
    is_target = (target_all - unit_at * vocab_dev)[:, None] == jnp.arange(vocab_dev)[None, :]
    row_max = jnp.max(logits, axis=1)
    sum_exp = jnp.sum(jnp.exp(logits - row_max[:, None]), axis=1)
    target_logit = jnp.sum(jnp.where(is_target, logits, 0.0), axis=1)
    shares, (grad_map,), (grad_final,) = gathered(
        jnp.stack([row_max, sum_exp, target_logit]).reshape(3, unit_count, pick_count),
        [contract(final, grad_mapped, TN).astype(B)],
        lambda _: (contract(grad_mapped, map_low, NT),),
    )
    shares = shares.reshape(unit_count, 3, unit_count, pick_count)
    shares = jnp.stack(
        [
            jnp.stack([shares[a, :, a ^ b] for a in range(unit_count)])
            for b in range(unit_count)
        ],
        axis=2,
    ).reshape(unit_count, 3, unit_count * pick_count)
    top = jnp.max(shares[:, 0], axis=0)
    log_sum = top + jnp.log(jnp.sum(shares[:, 1] * jnp.exp(shares[:, 0] - top), axis=0))
    own_terms = (log_sum - jnp.sum(shares[:, 2], axis=0))[:pick_count]
    grad_logits = (
        (jnp.exp(logits - log_sum[:, None]) - is_target.astype(F)) / count
    ).astype(B)
    grad_parts = dot(grad_logits, table_low).reshape(chips, 2, pick_count, breadth)
    both = grad_parts[:, 0] + swapped(grad_parts[:, 1])
    grad_picked = both[0]
    for step in range(1, chips):
        grad_picked = grad_picked + across(both[step], step)

    loss_part = error_part + jnp.sum(own_terms)
    grad_hidden = grad_final + lax.dot_general(
        pick_hot.astype(F),
        grad_picked,
        TN,
        precision=lax.Precision.HIGHEST,
        preferred_element_type=F,
    )

    gain_rows = [None] * norm_params.shape[0]
    feed_parts = [None] * layer_count
    attn_parts = [None] * layer_count
    later_feeds = []
    for layer_at in reversed(range(layer_count)):
        attn_stored, norm_first, feed_stored, norm_second = stored_layers[layer_at]
        hidden_low, tokens, features, gated_t, log_total = attn_stored
        middle_low, act, slope = feed_stored
        weights = attention_low[layer_at]
        grad_second, gain_rows[4 + 4 * layer_at], gain_rows[5 + 4 * layer_at] = norm_backward(
            norm_second, norm_params[4 + 4 * layer_at], grad_hidden
        )
        grad_result = (grad_second * layer_gate[layer_at, 1] * hidden_gate).astype(B)
        if layer_at < layer_count - 1:
            grad_result, attn_owned = together(grad_result, attn_owned)
            attn_parts[layer_at + 1] = lax.psum_scatter(attn_owned, "unit")
        grad_middle, feed_owned = feed_back(
            grad_result, middle_low, act, slope, feed_low[layer_at], unit_count
        )
        if layer_at < layer_count - 1:
            grad_middle, later_feed = together(grad_middle, feed_parts[layer_at + 1])
            later_feed = dp_scatter(later_feed.reshape(-1, breadth))
        feed_parts[layer_at] = lax.psum_scatter(feed_owned, "unit")
        grad_first, gain_rows[2 + 4 * layer_at], gain_rows[3 + 4 * layer_at] = norm_backward(
            norm_first, norm_params[2 + 4 * layer_at], grad_second + grad_middle
        )
        grad_branch = (grad_first * layer_gate[layer_at, 0] * hidden_gate).astype(B)
        scale = head_scale[layer_at]
        grad_mixed = (contract(grad_branch, weights[3], NT) * scale).astype(B)
        grad_mixed_t = (contract(weights[3], grad_branch, NT) * scale[:, None]).astype(B)
        grad_proj = attend_back(
            windows,
            tokens,
            features,
            grad_mixed,
            grad_mixed_t,
            key_segments,
            query_segments,
            log_total,
        )
        if layer_at < layer_count - 1:
            grad_proj, later_feed = together(grad_proj, later_feed)
            later_feeds.append(dp_gather(later_feed))
        grad_input = jnp.einsum("jre,jde->rd", grad_proj, weights[:3], preferred_element_type=F)
        grad_hidden = grad_first + grad_input
        grad_hidden, grad_proj = together(grad_hidden, grad_proj)
        grad_in = jnp.einsum(
            "rd,jre->jde", hidden_low, grad_proj, preferred_element_type=F
        ).astype(B)
        grad_out = dot(gated_t, grad_branch).astype(B)
        stack = [grad_in, grad_out[None]]
        if layer_at == layer_count - 1:
            stack.append(grad_map[None])
        stack = jnp.concatenate(stack, axis=0)
        if layer_at > 0:
            attn_owned = jnp.moveaxis(
                stack.reshape(-1, unit_count, slab_rows, breadth), 1, 0
            )
        else:
            stack = stack.reshape(-1, chips, 2, slab_rows, breadth)
            attn_mine = jnp.moveaxis(
                lax.dynamic_index_in_dim(stack, core, 2, keepdims=False), 1, 0
            )
            attn_theirs = jnp.moveaxis(
                lax.dynamic_index_in_dim(stack, 1 - core, 2, keepdims=False), 1, 0
            )

    grad_hidden, grad_logits = together(grad_hidden, grad_logits)
    grad_table = contract(grad_logits, picked_rows, TN)
    grad_looked, gain_rows[0], gain_rows[1] = norm_backward(
        embed_stored, norm_params[0], grad_hidden * hidden_gate
    )
    sent = grad_looked.astype(B)
    small = jnp.concatenate(
        [jnp.stack(gain_rows), jnp.broadcast_to(loss_part, (1, breadth))], axis=0
    )
    same = [(sent, 0), (sent, ROW_BLOCK)]
    other = swapped(sent)
    crossed = [(other, 0), (other, ROW_BLOCK)]
    if chips == 4 and length == 2 * ROW_BLOCK:
        near = [across(sent, 1), across(sent, 2)]
        later_feeds, later_attn = together(later_feeds, attn_parts[1:])
        later_attn = [dp_scatter(part.reshape(-1, breadth)) for part in later_attn]
        near, later_attn, grad_table, attn_theirs = together(
            near, later_attn, grad_table, attn_theirs
        )
        last = [across(near[0][:ROW_BLOCK], 2), across(near[1][ROW_BLOCK:], 1)]
        near_other = [swapped(part) for part in near]
        attn_chip = chip_sum(attn_mine, swapped(attn_theirs))
        later_attn = [dp_gather(part) for part in later_attn]
        last, near_other, attn_chip = together(last, near_other, attn_chip)
        last_other = [swapped(part) for part in last]
        attn_received = sent_to_owners(attn_chip, chip, range(1, chips))
        for home, parts, ends in ((same, near, last), (crossed, near_other, last_other)):
            home += [(part, at) for part in parts for at in (0, ROW_BLOCK)]
            home += [(part, 0) for part in ends]
    else:
        later_attn = [
            dp_gather(dp_scatter(part.reshape(-1, breadth))) for part in attn_parts[1:]
        ]
        attn_chip = chip_sum(attn_mine, swapped(attn_theirs))
        attn_received = sent_to_owners(attn_chip, chip, range(1, chips))
        for step in range(1, chips):
            part = across(sent, step)
            for home, part in ((same, part), (crossed, swapped(part))):
                home += [(part, at) for at in range(0, length, ROW_BLOCK)]
    embed_part = spread(all_ids, other_ids, own_place, lists, grad_table, same + crossed)
    embed_part, attn_received, later_attn = together(embed_part, attn_received, later_attn)
    small = dp_sum(small)
    attn_parts[0] = owner_total(attn_chip, attn_received, chip)
    embed_sum, feed_first, attn_first = lax.psum((embed_part, feed_parts[0], attn_parts[0]), "dp")
    attn_sums = [attn_first] + [
        dp_placed(found).reshape(part.shape) for found, part in zip(later_attn, attn_parts[1:])
    ]
    feed_sums = [feed_first] + [
        dp_placed(part).reshape(feed_first.shape) for part in reversed(later_feeds)
    ]
    row_sums = jnp.concatenate(
        [
            jnp.sum(attention_rows, axis=-1).reshape(-1),
            jnp.sum(feed_rows, axis=-1).reshape(-1),
            jnp.sum(map_rows)[None],
            jnp.sum(embedding_rows)[None],
        ]
    )
    row_sums = jnp.pad(row_sums, (0, breadth - row_sums.shape[0]))[None]
    old_cols = jnp.concatenate(
        [
            attention_cols.reshape(-1, breadth),
            feed_cols.reshape(-1, breadth),
            map_cols[None],
            embedding_cols[None],
        ],
        axis=0,
    )
    mats = layer_count * 4
    heights = jnp.array(
        [breadth] * mats
        + [units_dev * unit_count] * (layer_count * 2)
        + [breadth, vocab_dev * unit_count],
        F,
    )[:, None]
    packed = stats(small, row_sums, embed_sum, attn_sums, feed_sums)
    scalars, new_cols, factor, norm_grad, new_norm_params, new_norm_moment = factors(
        lax.all_gather(packed, "unit"), old_cols, heights, norm_params, norm_moment
    )
    total_loss, grad_norm = scalars[0], scalars[1]
    factor = factor[:, None]
    feeds = layer_count * 2
    here = jnp.zeros((1,), jnp.int32)
    slab = jnp.full((1,), unit_at, jnp.int32)
    new_embedding, embed_grad, new_embedding_rows = (
        value[0]
        for value in renew(
            scalars,
            here,
            factor,
            mats + feeds + 1,
            embedding_rows[None],
            embedding[None],
            embed_sum[None],
            1,
            640,
        )
    )
    new_map, map_grad, new_map_rows = (
        value[0]
        for value in renew(
            scalars,
            slab,
            factor,
            mats + feeds,
            map_rows[None],
            map_weight[None],
            attn_sums[layer_count - 1][4:],
            1,
            slab_rows,
        )
    )
    new_attention, attn_grad, new_attention_rows = (
        value.reshape((layer_count, 4) + value.shape[1:])
        for value in renew(
            scalars,
            slab,
            factor,
            0,
            attention_rows.reshape(mats, slab_rows),
            attention.reshape(mats, breadth, breadth),
            jnp.concatenate([part[:4] for part in attn_sums], axis=0),
            4,
            slab_rows,
        )
    )
    new_feed_forward, feed_grad, new_feed_rows = (
        value.reshape((layer_count, 2) + value.shape[1:])
        for value in renew(
            scalars,
            here,
            factor,
            mats,
            feed_rows.reshape(feeds, units_dev),
            feed_forward.reshape(feeds, units_dev, breadth),
            jnp.concatenate(feed_sums, axis=0),
            1,
            units_dev,
        )
    )
    new_attention_cols = new_cols[:mats].reshape(layer_count, 4, breadth)
    new_feed_cols = new_cols[mats : mats + feeds].reshape(layer_count, 2, breadth)
    new_map_cols = new_cols[mats + feeds]
    new_embedding_cols = new_cols[mats + feeds + 1]
    return (
        total_loss,
        count,
        grad_norm,
        new_embedding,
        embed_grad,
        new_embedding_rows,
        new_embedding_cols,
        new_attention,
        attn_grad,
        new_attention_rows,
        new_attention_cols,
        new_feed_forward,
        feed_grad,
        new_feed_rows,
        new_feed_cols,
        new_map,
        map_grad,
        new_map_rows,
        new_map_cols,
        new_norm_params,
        norm_grad,
        new_norm_moment,
    )


def solution(mesh):
    placed = (
        P(("dp", "unit"), None),
        P(("dp", "unit"), None),
        P(),
        P(("dp", "unit"), None),
        P(),
        P(("dp", "unit"), None, None),
        P(),
        P(),
        P(),
        P(),
        P(),
        P("unit", None),
        P(),
        P(None, None, "unit", None),
        P(),
        P(),
        P("unit"),
        P(),
        P(None, None, "unit"),
        P(),
        P(None, None, "unit"),
        P(),
        P("unit"),
        P(),
        P(),
    )
    return jax.shard_map(
        local,
        mesh=mesh,
        in_specs=placed,
        out_specs=(
            P(),
            P(),
            P(),
            P("unit", None),
            P("unit", None),
            P("unit"),
            P(),
            P(None, None, "unit", None),
            P(None, None, "unit", None),
            P(None, None, "unit"),
            P(),
            P(None, None, "unit", None),
            P(None, None, "unit", None),
            P(None, None, "unit"),
            P(),
            P("unit", None),
            P("unit", None),
            P("unit"),
            P(),
            P(),
            P(),
            P(),
        ),
        check_vma=False,
    )
```

```python
import functools
import math

import jax
import jax.numpy as jnp
from jax import lax
from jax.experimental import pallas as pl
from jax.experimental.pallas import tpu as pltpu
from jax.sharding import PartitionSpec as P

H = 12
HD = 64
PAIR = 2 * HD
KEY_BLOCK = 128
QUERY_BLOCK = 256
ROW_BLOCK = 512
UNIT_BLOCK = 768
FEED_BLOCK = 1536
FEED_PART = 512

LN_EPS = 1e-06
ADA_EPS = 1e-30
DECAY_RATE = 0.95
LEARN_RATE = 0.015
CLIP_LIMIT = 0.05
MASK_FILL = 1e30

B = jnp.bfloat16
F = jnp.float32
NT = (((1,), (1,)), ((), ()))
TN = (((0,), (0,)), ((), ()))
TT = (((0,), (1,)), ((), ()))
VMEM_MOST = 58 * 2**20


def dot(left, right):
    return jnp.dot(left, right, preferred_element_type=F)


def contract(left, right, dims):
    return lax.dot_general(left, right, dims, preferred_element_type=F)


def query_windows(segments, block):
    first = segments[::block]
    last = segments[block - 1 :: block]
    start = jnp.sum((segments[None, :] < first[:, None]).astype(jnp.int32), axis=1)
    stop = jnp.sum((segments[None, :] <= last[:, None]).astype(jnp.int32), axis=1)
    low = start // KEY_BLOCK
    high = (stop + KEY_BLOCK - 1) // KEY_BLOCK
    return jnp.concatenate([low, high - low]).astype(jnp.int32)


def most_blocks(length, block):
    return min(length // KEY_BLOCK, block // KEY_BLOCK + 4)


def window_mask(segk_ref, segq_ref, start, width, first_query, block):
    key_seg = segk_ref[pl.ds(start, width), :]
    if block > KEY_BLOCK:
        key_seg = jnp.concatenate([key_seg] * (block // KEY_BLOCK), axis=1)
    query_seg = segq_ref[0:1, pl.ds(first_query, block)]
    key_at = start + lax.broadcasted_iota(jnp.int32, (width, block), 0)
    query_at = first_query + lax.broadcasted_iota(jnp.int32, (width, block), 1)
    return (key_seg == query_seg) | (key_at == query_at)


def head_rows(block):
    empty = jnp.zeros((HD, block.shape[1]), block.dtype)
    first = jnp.concatenate([block[:HD], empty], axis=0)
    second = jnp.concatenate([empty, block[HD:]], axis=0)
    return jnp.concatenate([first, second], axis=1)


def head_lanes(block):
    lane = lax.broadcasted_iota(jnp.int32, block.shape, 1)
    empty = jnp.zeros_like(block)
    return jnp.concatenate(
        [jnp.where(lane < HD, block, empty), jnp.where(lane < HD, empty, block)], axis=0
    )


def attend_kernel(
    window_ref, gate_ref, k_ref, qt_ref, vt_ref, segk_ref, segq_ref, ot_ref, lse_ref, *, block
):
    pair = pl.program_id(0)
    length = k_ref.shape[1]
    count = length // block
    lse_ref[...] = jnp.zeros_like(lse_ref)
    for i in range(count):
        low = window_ref[i]
        number = window_ref[count + i]
        columns = pl.ds(i * block, block)
        for n in range(1, most_blocks(length, block) + 1):

            @pl.when(number == n)
            def _():
                width = n * KEY_BLOCK
                start = pl.multiple_of(low * KEY_BLOCK, KEY_BLOCK)
                keys = k_ref[0, pl.ds(start, width), :]
                mask = window_mask(segk_ref, segq_ref, start, width, i * block, block)
                queries = qt_ref[0, :, columns]
                scores = dot(keys, head_rows(queries))
                scores = jnp.where(jnp.concatenate([mask, mask], axis=1), scores, -MASK_FILL)
                top = jnp.max(scores, axis=0, keepdims=True)
                exponent = jnp.exp(scores - top)
                total = jnp.sum(exponent, axis=0, keepdims=True)
                mixed = dot(vt_ref[0, :, pl.ds(start, width)], exponent.astype(B))
                inverse = 1.0 / total
                log_total = top + jnp.log(total)
                for head in range(2):
                    rows = slice(head * HD, (head + 1) * HD)
                    lanes = slice(head * block, (head + 1) * block)
                    gated = mixed[rows, lanes] * (inverse[:, lanes] * gate_ref[2 * pair + head])
                    ot_ref[rows, columns] = gated.astype(B)
                    lse_ref[0, head : head + 1, columns] = log_total[:, lanes]


def attend(windows, gates, tokens, features, key_segments, query_segments):
    _, length, breadth = tokens.shape
    pairs = breadth // PAIR
    return pl.pallas_call(
        functools.partial(attend_kernel, block=QUERY_BLOCK),
        grid_spec=pltpu.PrefetchScalarGridSpec(
            num_scalar_prefetch=2,
            grid=(pairs,),
            in_specs=[
                pl.BlockSpec((1, length, PAIR), lambda p, *_: (1, 0, p)),
                pl.BlockSpec((1, PAIR, length), lambda p, *_: (0, p, 0)),
                pl.BlockSpec((1, PAIR, length), lambda p, *_: (2, p, 0)),
                pl.BlockSpec((length, KEY_BLOCK), lambda p, *_: (0, 0)),
                pl.BlockSpec((8, length), lambda p, *_: (0, 0)),
            ],
            out_specs=[
                pl.BlockSpec((PAIR, length), lambda p, *_: (p, 0)),
                pl.BlockSpec((1, 8, length), lambda p, *_: (p, 0, 0)),
            ],
        ),
        out_shape=[
            jax.ShapeDtypeStruct((breadth, length), B),
            jax.ShapeDtypeStruct((pairs, 8, length), F),
        ],
        compiler_params=pltpu.CompilerParams(vmem_limit_bytes=VMEM_MOST),
        cost_estimate=pl.CostEstimate(
            flops=2 * 2 * 2 * length * 512 * breadth,
            bytes_accessed=8 * length * breadth,
            transcendentals=length * 512 * 12,
        ),
        name="attend",
    )(windows, gates, tokens, features, features, key_segments, query_segments)


def attend_back_kernel(
    window_ref,
    k_ref,
    kt_ref,
    q_ref,
    qt_ref,
    v_ref,
    do_ref,
    segk_ref,
    segq_ref,
    lse_ref,
    grad_ref,
    dq_sum,
    dk_sum,
    dv_sum,
    do_t,
    *,
    block,
    score_scale,
):
    length = k_ref.shape[1]
    count = length // block
    do_t[...] = jnp.transpose(do_ref[...].astype(F)).astype(B)
    dk_sum[...] = jnp.zeros_like(dk_sum)
    dv_sum[...] = jnp.zeros_like(dv_sum)
    for i in range(count):
        low = window_ref[i]
        number = window_ref[count + i]
        columns = pl.ds(i * block, block)
        for n in range(1, most_blocks(length, block) + 1):

            @pl.when(number == n)
            def _():
                width = n * KEY_BLOCK
                start = pl.multiple_of(low * KEY_BLOCK, KEY_BLOCK)
                window = pl.ds(start, width)
                keys = k_ref[0, window, :]
                values = v_ref[0, window, :]
                mask = window_mask(segk_ref, segq_ref, start, width, i * block, block)
                queries_t = qt_ref[0, :, columns]
                grads_t = do_t[:, columns]
                scores = dot(keys, head_rows(queries_t))
                scores = jnp.where(jnp.concatenate([mask, mask], axis=1), scores, -MASK_FILL)
                log_total = jnp.concatenate(
                    [lse_ref[0, 0:1, columns], lse_ref[0, 1:2, columns]], axis=1
                )
                prob = jnp.exp(scores - log_total)
                weighted = prob * dot(values, head_rows(grads_t))
                inner = jnp.sum(weighted, axis=0, keepdims=True)
                grad = (weighted - prob * inner).astype(B)
                grad_q = dot(kt_ref[0, :, window], grad) * score_scale
                dq_sum[:HD, columns] = grad_q[:HD, :block]
                dq_sum[HD:, columns] = grad_q[HD:, block:]
                dv_sum[window, :] += dot(prob.astype(B), head_lanes(do_ref[columns, :]))
                dk_sum[window, :] += dot(grad, head_lanes(q_ref[0, columns, :]))

    grad_ref[0] = jnp.transpose(dq_sum[...]).astype(B)
    grad_ref[1] = dk_sum[...].astype(B)
    grad_ref[2] = dv_sum[...].astype(B)


def attend_back(
    windows, tokens, features, grads, key_segments, query_segments, log_total
):
    _, length, breadth = tokens.shape
    pairs = breadth // PAIR

    def token_spec(which):
        return pl.BlockSpec((1, length, PAIR), lambda p, *_: (which, 0, p))

    def feature_spec(which):
        return pl.BlockSpec((1, PAIR, length), lambda p, *_: (which, p, 0))

    return pl.pallas_call(
        functools.partial(
            attend_back_kernel, block=QUERY_BLOCK, score_scale=1.0 / math.sqrt(HD)
        ),
        grid_spec=pltpu.PrefetchScalarGridSpec(
            num_scalar_prefetch=1,
            grid=(pairs,),
            in_specs=[
                token_spec(1),
                feature_spec(1),
                token_spec(0),
                feature_spec(0),
                token_spec(2),
                pl.BlockSpec((length, PAIR), lambda p, *_: (0, p)),
                pl.BlockSpec((length, KEY_BLOCK), lambda p, *_: (0, 0)),
                pl.BlockSpec((8, length), lambda p, *_: (0, 0)),
                pl.BlockSpec((1, 8, length), lambda p, *_: (p, 0, 0)),
            ],
            out_specs=pl.BlockSpec((3, length, PAIR), lambda p, *_: (0, 0, p)),
            scratch_shapes=[
                pltpu.VMEM((PAIR, length), F),
                pltpu.VMEM((length, PAIR), F),
                pltpu.VMEM((length, PAIR), F),
                pltpu.VMEM((PAIR, length), B),
            ],
        ),
        out_shape=jax.ShapeDtypeStruct((3, length, breadth), B),
        compiler_params=pltpu.CompilerParams(vmem_limit_bytes=VMEM_MOST),
        cost_estimate=pl.CostEstimate(
            flops=5 * 2 * 2 * length * 512 * breadth,
            bytes_accessed=20 * length * breadth,
            transcendentals=length * 512 * 12,
        ),
        name="attend_back",
    )(
        windows,
        tokens,
        features,
        tokens,
        features,
        tokens,
        grads,
        key_segments,
        query_segments,
        log_total,
    )


def project_kernel(x_ref, weight_ref, tokens_ref, features_ref, *, score_scale):
    scale = jnp.where(pl.program_id(0) == 0, score_scale, 1.0).astype(F)
    tokens = dot(x_ref[...], weight_ref[...]).astype(B).astype(F)
    tokens_ref[0] = (tokens * scale).astype(B)
    features = contract(weight_ref[...], x_ref[...], TT).astype(B).astype(F)
    features_ref[0] = (features * scale).astype(B)


def project(x, weights, layer):
    length, breadth = x.shape
    return pl.pallas_call(
        functools.partial(project_kernel, score_scale=1.0 / math.sqrt(HD)),
        grid=(3,),
        in_specs=[
            pl.BlockSpec((length, breadth), lambda j: (0, 0)),
            pl.BlockSpec((None, None, breadth, breadth), lambda j: (layer, j, 0, 0)),
        ],
        out_specs=[
            pl.BlockSpec((1, length, breadth), lambda j: (j, 0, 0)),
            pl.BlockSpec((1, breadth, length), lambda j: (j, 0, 0)),
        ],
        out_shape=[
            jax.ShapeDtypeStruct((3, length, breadth), B),
            jax.ShapeDtypeStruct((3, breadth, length), B),
        ],
        compiler_params=pltpu.CompilerParams(vmem_limit_bytes=VMEM_MOST),
        cost_estimate=pl.CostEstimate(
            flops=12 * length * breadth * breadth,
            bytes_accessed=14 * length * breadth + 6 * breadth * breadth,
            transcendentals=0,
        ),
        name="project",
    )(x, weights)


def gelu_and_slope(value):
    density = jnp.exp(value * value * -0.5)
    ratio = pl.reciprocal(1.0 + jnp.abs(value) * (0.3275911 * math.sqrt(0.5)))
    series = ratio * (
        0.127414796
        + ratio
        * (-0.142248368 + ratio * (0.7107068705 + ratio * (-0.7265760135 + ratio * 0.5307027145)))
    )
    tail = series * density
    below = jnp.where(value >= 0, 1.0 - tail, tail)
    return value * below, below + value * density * (1.0 / math.sqrt(2.0 * math.pi))


def feed_kernel(x_ref, up_ref, down_ref, scale_ref, act_ref, slope_ref, out_ref):
    first = pl.program_id(0) == 0
    parts = [slice(at, at + FEED_PART) for at in range(0, up_ref.shape[0], FEED_PART)]
    ahead = contract(x_ref[...], up_ref[parts[0], :], NT)
    part = None
    for k, lanes in enumerate(parts):
        before = ahead
        if k + 1 < len(parts):
            ahead = contract(x_ref[...], up_ref[parts[k + 1], :], NT)
        act, slope = gelu_and_slope(before)
        scale = scale_ref[0, :, lanes]
        act = (act * scale).astype(B)
        act_ref[:, lanes] = act
        slope_ref[:, lanes] = (slope * scale).astype(B)
        term = dot(act, down_ref[lanes, :])
        part = term if part is None else part + term

    @pl.when(first)
    def _():
        out_ref[...] = part

    @pl.when(jnp.logical_not(first))
    def _():
        out_ref[...] += part


def feed(x, weights, scale):
    length, breadth = x.shape
    units = weights.shape[1]
    block = FEED_BLOCK
    return pl.pallas_call(
        feed_kernel,
        grid=(units // block,),
        in_specs=[
            pl.BlockSpec((length, breadth), lambda j: (0, 0)),
            pl.BlockSpec((None, block, breadth), lambda j: (0, j, 0)),
            pl.BlockSpec((None, block, breadth), lambda j: (1, j, 0)),
            pl.BlockSpec((1, 1, block), lambda j: (0, 0, j)),
        ],
        out_specs=[
            pl.BlockSpec((length, block), lambda j: (0, j)),
            pl.BlockSpec((length, block), lambda j: (0, j)),
            pl.BlockSpec((length, breadth), lambda j: (0, 0)),
        ],
        out_shape=[
            jax.ShapeDtypeStruct((length, units), B),
            jax.ShapeDtypeStruct((length, units), B),
            jax.ShapeDtypeStruct((length, breadth), F),
        ],
        compiler_params=pltpu.CompilerParams(vmem_limit_bytes=VMEM_MOST),
        cost_estimate=pl.CostEstimate(
            flops=4 * length * breadth * units,
            bytes_accessed=4 * (length + breadth) * units + 6 * length * breadth,
            transcendentals=2 * length * units,
        ),
        name="feed",
    )(x, weights, weights, scale.reshape(1, 1, units))


def feed_back_kernel(
    grad_ref, x_ref, act_ref, slope_ref, up_ref, down_ref, out_ref, owned_ref, pre_grad
):
    first = pl.program_id(0) == 0
    grad_act = contract(grad_ref[...], down_ref[...], NT)
    grad_pre = (grad_act * slope_ref[...].astype(F)).astype(B)
    pre_grad[...] = grad_pre
    part = dot(grad_pre, up_ref[...])

    @pl.when(first)
    def _():
        out_ref[...] = part

    @pl.when(jnp.logical_not(first))
    def _():
        out_ref[...] += part

    grads = (
        contract(pre_grad[...], x_ref[...], TN).astype(B),
        contract(act_ref[...], grad_ref[...], TN).astype(B),
    )
    owners, _, share, _ = owned_ref.shape
    for which in range(2):
        for owner in range(owners):
            owned_ref[owner, which] = grads[which][owner * share : (owner + 1) * share]


def feed_back(grad, x, act, slope, weights, owners):
    length, breadth = x.shape
    units = weights.shape[1]
    share = units // owners
    block = UNIT_BLOCK
    lanes = pl.BlockSpec((length, block), lambda j: (0, j))
    whole = pl.BlockSpec((length, breadth), lambda j: (0, 0))
    return pl.pallas_call(
        feed_back_kernel,
        grid=(units // block,),
        in_specs=[
            whole,
            whole,
            lanes,
            lanes,
            pl.BlockSpec((None, block, breadth), lambda j: (0, j, 0)),
            pl.BlockSpec((None, block, breadth), lambda j: (1, j, 0)),
        ],
        out_specs=[
            whole,
            pl.BlockSpec((block // share, 2, share, breadth), lambda j: (j, 0, 0, 0)),
        ],
        scratch_shapes=[pltpu.VMEM((length, block), B)],
        out_shape=[
            jax.ShapeDtypeStruct((length, breadth), F),
            jax.ShapeDtypeStruct((owners, 2, share, breadth), B),
        ],
        compiler_params=pltpu.CompilerParams(vmem_limit_bytes=VMEM_MOST),
        cost_estimate=pl.CostEstimate(
            flops=8 * length * breadth * units,
            bytes_accessed=4 * (length + 2 * breadth) * units + 8 * length * breadth,
            transcendentals=0,
        ),
        name="feed_back",
    )(grad, x, act, slope, weights, weights)


def scan_kernel(ids, place, found, ends, *, vocab):
    base = place[0]
    blocks = ends.shape[0]
    streams = math.gcd(blocks, 8)
    for first in range(0, blocks, streams):

        def scan(t, counts):
            after = []
            for k, count in enumerate(counts):
                at = (first + k) * ROW_BLOCK + t
                relative = (ids[at] - base).astype(jnp.uint32)
                found[count] = at
                after.append(count + jnp.where(relative < jnp.uint32(vocab), 1, 0))
            return tuple(after)

        begin = tuple(jnp.int32((first + k) * ROW_BLOCK) for k in range(streams))
        counts = lax.fori_loop(0, ROW_BLOCK, scan, begin, unroll=4)
        for k, count in enumerate(counts):
            ends[first + k] = count


def scan_ids(ids, place, vocab):
    smem = pl.BlockSpec(memory_space=pltpu.SMEM)
    return pl.pallas_call(
        functools.partial(scan_kernel, vocab=vocab),
        in_specs=[smem, smem],
        out_specs=[smem, smem],
        out_shape=[
            jax.ShapeDtypeStruct(ids.shape, jnp.int32),
            jax.ShapeDtypeStruct((ids.shape[0] // ROW_BLOCK,), jnp.int32),
        ],
        name="scan_ids",
    )(ids, place)


def lookup_kernel(ids, place, found, ends, own, other, *rest, blocks, vocab):
    outs = rest[:blocks]
    table, rows, stage, table_sem, out_sem = rest[blocks:]
    base = place[0]
    core = place[1]
    mine = pl.multiple_of(core * vocab, 8)
    theirs = pl.multiple_of((1 - core) * vocab, 8)
    loads = [
        pltpu.make_async_copy(own, table.at[pl.ds(mine, vocab)], table_sem.at[0]),
        pltpu.make_async_copy(other, table.at[pl.ds(theirs, vocab)], table_sem.at[1]),
    ]
    for load in loads:
        load.start()
    for load in loads:
        load.wait()
    copies = [None, None]
    for k in range(blocks):
        rows[...] = jnp.zeros_like(rows)

        def put(entry, carry):
            t = found[entry]
            rows[pl.ds(t - k * ROW_BLOCK, 1), :] = table[pl.ds(ids[t] - base, 1), :]
            return carry

        each_entry(k * ROW_BLOCK, ends[k], put)
        slot = k % 2
        if copies[slot] is not None:
            copies[slot].wait()
        stage[slot] = rows[...].astype(B)
        copies[slot] = pltpu.make_async_copy(stage.at[slot], outs[k], out_sem.at[slot])
        copies[slot].start()
    for copy in copies:
        copy.wait()


def each_entry(low, high, body):
    quads = lax.div(high - low, 4)

    def four(e, carry):
        for j in range(4):
            body(low + e * 4 + j, 0)
        return carry

    lax.fori_loop(0, quads, four, 0)
    lax.fori_loop(low + quads * 4, high, body, 0)


def lookup(ids, place, found, ends, own, other):
    vocab, breadth = own.shape
    blocks = ids.shape[0] // ROW_BLOCK
    hbm = pl.BlockSpec(memory_space=pl.ANY)
    smem = pl.BlockSpec(memory_space=pltpu.SMEM)
    return pl.pallas_call(
        functools.partial(lookup_kernel, blocks=blocks, vocab=vocab),
        in_specs=[smem] * 4 + [hbm] * 2,
        out_specs=[hbm] * blocks,
        out_shape=[jax.ShapeDtypeStruct((ROW_BLOCK, breadth), B)] * blocks,
        scratch_shapes=[
            pltpu.VMEM((2 * vocab, breadth), F),
            pltpu.VMEM((ROW_BLOCK, breadth), F),
            pltpu.VMEM((2, ROW_BLOCK, breadth), B),
            pltpu.SemaphoreType.DMA((2,)),
            pltpu.SemaphoreType.DMA((2,)),
        ],
        compiler_params=pltpu.CompilerParams(vmem_limit_bytes=VMEM_MOST),
        cost_estimate=pl.CostEstimate(
            flops=0,
            bytes_accessed=8 * vocab * breadth + 2 * ids.shape[0] * breadth,
            transcendentals=0,
        ),
        name="lookup",
    )(ids, place, found, ends, own, other)


def spread_kernel(
    ids, other_ids, place, found, ends, other_found, other_ends, begin, *rest, pieces
):
    blocks = len(pieces)
    arrays = max(which for which, _ in pieces) + 1
    grads = [rest[which].at[pl.ds(at, ROW_BLOCK)] for which, at in pieces]
    out, total, rows, stage, half, sem, in_sem, out_sem = rest[arrays:]
    base = place[0]
    vocab = total.shape[0]
    fill = pltpu.make_async_copy(begin, total, sem.at[0])
    fill.start()

    def load(k):
        copy = pltpu.make_async_copy(grads[k], stage.at[k % 2], in_sem.at[k % 2])
        copy.start()
        return copy

    coming = load(0)
    fill.wait()
    for k in range(blocks):
        coming.wait()
        if k + 1 < blocks:
            coming = load(k + 1)
        rows[...] = stage[k % 2].astype(F)

        lists = (ids, found, ends) if k < blocks // 2 else (other_ids, other_found, other_ends)
        first = k % (blocks // 2) * ROW_BLOCK

        def add(entry, carry):
            t = lists[1][entry]
            at = pl.ds(lists[0][t] - base, 1)
            total[at, :] += rows[pl.ds(t - first, 1), :]
            return carry

        each_entry(first, lists[2][k % (blocks // 2)], add)
    step = half.shape[1]
    copies = [None, None]
    for j in range(vocab // step):
        slot = j % 2
        if copies[slot] is not None:
            copies[slot].wait()
        half[slot] = total[j * step : (j + 1) * step, :].astype(B)
        copies[slot] = pltpu.make_async_copy(
            half.at[slot], out.at[pl.ds(j * step, step)], out_sem.at[slot]
        )
        copies[slot].start()
    for copy in copies:
        copy.wait()


def spread(ids, other_ids, place, lists, begin, grads):
    vocab, breadth = begin.shape
    arrays = []
    pieces = []
    for array, at in grads:
        known = [k for k, other in enumerate(arrays) if other is array]
        if not known:
            known = [len(arrays)]
            arrays.append(array)
        pieces.append((known[0], at))
    hbm = pl.BlockSpec(memory_space=pl.ANY)
    smem = pl.BlockSpec(memory_space=pltpu.SMEM)
    return pl.pallas_call(
        functools.partial(spread_kernel, pieces=tuple(pieces)),
        in_specs=[smem] * 7 + [hbm] * (1 + len(arrays)),
        out_specs=hbm,
        out_shape=jax.ShapeDtypeStruct((vocab, breadth), B),
        scratch_shapes=[
            pltpu.VMEM((vocab, breadth), F),
            pltpu.VMEM((ROW_BLOCK, breadth), F),
            pltpu.VMEM((2, ROW_BLOCK, breadth), B),
            pltpu.VMEM((2, vocab // 4, breadth), B),
            pltpu.SemaphoreType.DMA((1,)),
            pltpu.SemaphoreType.DMA((2,)),
            pltpu.SemaphoreType.DMA((2,)),
        ],
        compiler_params=pltpu.CompilerParams(vmem_limit_bytes=VMEM_MOST),
        cost_estimate=pl.CostEstimate(
            flops=0,
            bytes_accessed=6 * vocab * breadth + 2 * len(grads) * ROW_BLOCK * breadth,
            transcendentals=0,
        ),
        name="spread",
    )(ids, other_ids, place, *lists, begin, *arrays)


def stats_kernel(small_ref, row_sums_ref, embed_ref, *rest, layers):
    attn = rest[:layers]
    feeds = rest[layers : 2 * layers]
    out_ref = rest[2 * layers]
    norms = small_ref.shape[0]
    cols = jnp.sum(jnp.square(embed_ref[...].astype(F)), axis=0, keepdims=True)

    @pl.when(pl.program_id(0) == 0)
    def _():
        def put(row, value):
            out_ref[row : row + 1, :] = jnp.sum(
                jnp.square(value.astype(F)), axis=0, keepdims=True
            )

        out_ref[:norms, :] = small_ref[...]
        row = norms
        for parts, count in ((attn, 4), (feeds, 2)):
            for part in parts:
                for k in range(count):
                    put(row, part[k])
                    row += 1
        put(row, attn[layers - 1][4])
        out_ref[row + 1 : row + 2, :] = cols
        row += 2
        out_ref[row : row + 1, :] = row_sums_ref[...]

    @pl.when(pl.program_id(0) > 0)
    def _():
        at = norms + 6 * layers + 1
        out_ref[at : at + 1, :] += cols


def stats(small, row_sums, embed, attn, feeds):
    height, breadth = embed.shape
    block = math.gcd(height, 480)
    rows = small.shape[0] + 3 + 6 * len(attn)
    vmem = pl.BlockSpec(memory_space=pltpu.VMEM)
    return pl.pallas_call(
        functools.partial(stats_kernel, layers=len(attn)),
        grid=(height // block,),
        in_specs=[vmem, vmem, pl.BlockSpec((block, breadth), lambda j: (j, 0))]
        + [vmem] * (2 * len(attn)),
        out_specs=pl.BlockSpec((rows, breadth), lambda j: (0, 0)),
        out_shape=jax.ShapeDtypeStruct((rows, breadth), F),
        compiler_params=pltpu.CompilerParams(vmem_limit_bytes=VMEM_MOST),
        name="stats",
    )(small, row_sums, embed, *attn, *feeds)


def factors_kernel(
    parts_ref,
    cols_ref,
    heights_ref,
    params_ref,
    moment_ref,
    scalars_ref,
    new_cols_ref,
    factor_ref,
    norm_grad_ref,
    new_params_ref,
    new_moment_ref,
):
    packed = parts_ref[0]
    for k in range(1, parts_ref.shape[0]):
        packed = packed + parts_ref[k]
    norms = params_ref.shape[0]
    mats, breadth = cols_ref.shape
    norm_grads = packed[:norms]
    col_sums = packed[norms + 1 : norms + 1 + mats]
    lane = lax.broadcasted_iota(jnp.int32, (mats, breadth), 1)
    row = lax.broadcasted_iota(jnp.int32, (mats, breadth), 0)
    row_sums = jnp.sum(
        jnp.where(lane == row, packed[norms + 1 + mats :], 0.0), axis=1, keepdims=True
    )
    heights = heights_ref[...]
    mat_sums = jnp.sum(col_sums, axis=1, keepdims=True)
    square = jnp.sum(mat_sums, axis=0, keepdims=True) + jnp.sum(
        jnp.sum(norm_grads * norm_grads, axis=1, keepdims=True), axis=0, keepdims=True
    )
    norm = jnp.sqrt(square)
    clip = jnp.minimum(1.0, CLIP_LIMIT / norm)
    scalars_ref[0] = packed[norms, 0]
    scalars_ref[1] = norm[0, 0]
    scalars_ref[2] = clip[0, 0]
    new_cols = DECAY_RATE * cols_ref[...] + (1 - DECAY_RATE) * (
        clip * clip * col_sums / heights + ADA_EPS
    )
    mean_rows = DECAY_RATE * row_sums / heights + (1 - DECAY_RATE) * (
        clip * clip * mat_sums / (heights * breadth) + ADA_EPS
    )
    new_cols_ref[...] = new_cols
    factor_ref[...] = LEARN_RATE * jnp.sqrt(mean_rows) * lax.rsqrt(new_cols)
    norm_grad = norm_grads * clip
    moment = DECAY_RATE * moment_ref[...] + (1 - DECAY_RATE) * (norm_grad * norm_grad + ADA_EPS)
    norm_grad_ref[...] = norm_grad
    new_moment_ref[...] = moment
    new_params_ref[...] = params_ref[...] - LEARN_RATE * norm_grad * lax.rsqrt(moment)


def factors(parts, cols, heights, params, moment):
    vmem = pl.BlockSpec(memory_space=pltpu.VMEM)
    like = [jax.ShapeDtypeStruct(x.shape, F) for x in (cols, cols, params, params, params)]
    return pl.pallas_call(
        factors_kernel,
        in_specs=[vmem] * 5,
        out_specs=[pl.BlockSpec(memory_space=pltpu.SMEM)] + [vmem] * 5,
        out_shape=[jax.ShapeDtypeStruct((3,), F)] + like,
        compiler_params=pltpu.CompilerParams(vmem_limit_bytes=VMEM_MOST),
        name="factors",
    )(parts, cols, heights, params, moment)


def renew_kernel(
    scalars_ref, at_ref, factor_ref, rows_ref, weight_ref, sum_ref, new_ref, grad_ref, new_rows_ref
):
    for m in range(sum_ref.shape[0]):
        grad = sum_ref[m].astype(F) * scalars_ref[2]
        mean = jnp.mean(grad * grad, axis=1, keepdims=True) + ADA_EPS
        new_rows = DECAY_RATE * rows_ref[m] + (1 - DECAY_RATE) * mean
        wide = jnp.broadcast_to(new_rows, (new_rows.shape[0], 128))
        new_rows_ref[m, 0] = jnp.transpose(wide)[:1]
        grad_ref[m] = grad
        new_ref[m] = weight_ref[m] - grad * lax.rsqrt(new_rows) * factor_ref[m]


def renew(scalars, at, factor, first, rows, weight, total, group, most):
    mats, height, breadth = total.shape
    block = math.gcd(height, most)
    per = height // block
    wide = pl.BlockSpec((group, block, breadth), lambda m, j, *_: (m, j, 0))
    new, grad, new_rows = pl.pallas_call(
        renew_kernel,
        grid_spec=pltpu.PrefetchScalarGridSpec(
            num_scalar_prefetch=2,
            grid=(mats // group, per),
            in_specs=[
                pl.BlockSpec((group, 1, breadth), lambda m, j, *_: (first // group + m, 0, 0)),
                pl.BlockSpec((group, block, 1), lambda m, j, *_: (m, j, 0)),
                pl.BlockSpec(
                    (group, block, breadth), lambda m, j, scalars, at: (m, at[0] * per + j, 0)
                ),
                wide,
            ],
            out_specs=[
                wide,
                wide,
                pl.BlockSpec((group, 1, 1, block), lambda m, j, *_: (m, j, 0, 0)),
            ],
        ),
        out_shape=[
            jax.ShapeDtypeStruct((mats, height, breadth), F),
            jax.ShapeDtypeStruct((mats, height, breadth), F),
            jax.ShapeDtypeStruct((mats, per, 1, block), F),
        ],
        compiler_params=pltpu.CompilerParams(vmem_limit_bytes=VMEM_MOST),
        name="renew",
    )(scalars, at, factor, rows[..., None], weight, total)
    return new, grad, new_rows.reshape(rows.shape)


def across(value, step):
    pairs = [(u, ((u // 2) ^ step) * 2 + u % 2) for u in range(lax.axis_size("unit"))]
    return lax.ppermute(value, "unit", pairs)


def swapped(value):
    return lax.ppermute(value, "unit", [(u, u ^ 1) for u in range(lax.axis_size("unit"))])


def gathered(value, beside_core, beside_chip):
    other, *beside_core = together(swapped(value), *beside_core)
    both = jnp.stack([value, other])
    chips = lax.axis_size("unit") // 2
    parts = [across(both, step) for step in range(1, chips)]
    if beside_chip:
        parts[0], *beside_chip = together(parts[0], *beside_chip(*beside_core))
    return jnp.stack([both] + parts), beside_core, beside_chip


def dp_scatter(value):
    size = lax.axis_size("dp")
    at = lax.axis_index("dp")
    share = value.shape[0] // size
    parts = [lax.dynamic_slice_in_dim(value, at * share, share, 0)]
    for step in range(1, size):
        away = lax.dynamic_slice_in_dim(value, (at + step) % size * share, share, 0)
        parts.append(lax.ppermute(away, "dp", [(d, (d + step) % size) for d in range(size)]))
    return parts


def dp_gather(parts):
    size = lax.axis_size("dp")
    at = lax.axis_index("dp")
    total = parts[0].astype(F)
    for part in parts[1:]:
        total = total + part.astype(F)
    total = total.astype(B)
    found = [total] + [
        lax.ppermute(total, "dp", [(d, (d + step) % size) for d in range(size)])
        for step in range(1, size)
    ]
    return found


def dp_placed(found):
    size = len(found)
    at = lax.axis_index("dp")
    share = found[0].shape[0]
    result = jnp.zeros((size * share,) + found[0].shape[1:], found[0].dtype)
    for step, part in enumerate(found):
        result = lax.dynamic_update_slice_in_dim(result, part, (at - step) % size * share, 0)
    return result


def dp_sum(value):
    size = lax.axis_size("dp")
    if size & (size - 1):
        return lax.psum(value, "dp")
    step = 1
    while step < size:
        value = value + lax.ppermute(value, "dp", [(d, d ^ step) for d in range(size)])
        step = 2 * step
    return value


def together(*values):
    return lax.optimization_barrier(values)


def chip_sum(mine, swapped_theirs):
    return (mine.astype(F) + swapped_theirs.astype(F)).astype(B)


def sent_to_owners(total, chip, steps):
    return [
        across(lax.dynamic_index_in_dim(total, chip ^ step, 0, keepdims=False), step)
        for step in steps
    ]


def owner_total(total, received, chip):
    result = lax.dynamic_index_in_dim(total, chip, 0, keepdims=False).astype(F)
    for part in received:
        result = result + part.astype(F)
    return result.astype(B)


def rows_of_tokens(served, chips, beside, beside_last):
    halves = len(served[0])
    total = [part.astype(F) for part in served[0]]
    if chips != 4 or halves != 2:
        for step in range(1, chips):
            for k in range(halves):
                total[k] = total[k] + across(served[step][k], step).astype(F)
        return jnp.concatenate(total, axis=0), *beside, *beside_last()
    passing = [across(served[3][0], 2), across(served[3][1], 1)]
    direct = [across(served[2][0], 2), across(served[1][1], 1)]
    passing[0], passing[1], direct[0], direct[1], *beside = together(*passing, *direct, *beside)
    last = [
        across(served[1][0] + passing[0], 1),
        across(served[2][1] + passing[1], 2),
    ]
    last[0], last[1], *after = together(*last, *beside_last())
    total = [a + b.astype(F) + c.astype(F) for a, b, c in zip(total, direct, last)]
    return jnp.concatenate(total, axis=0), *beside, *after


def norm_forward(value, gain, shift):
    centered = value - jnp.mean(value, axis=-1, keepdims=True)
    inverse = lax.rsqrt(jnp.mean(centered * centered, axis=-1, keepdims=True) + LN_EPS)
    normed = centered * inverse
    return (normed * gain + shift, (normed, inverse))


def norm_backward(stored, gain, upstream):
    normed, inverse = stored
    scaled = upstream * gain
    inner = (
        scaled
        - jnp.mean(scaled, axis=-1, keepdims=True)
        - normed * jnp.mean(scaled * normed, axis=-1, keepdims=True)
    )
    return (inverse * inner, jnp.sum(upstream * normed, axis=0), jnp.sum(upstream, axis=0))


def local(
    token_ids,
    segment_ids,
    real_mask,
    positions,
    targets,
    teacher_states,
    head_gate,
    layer_gate,
    hidden_gate,
    unit_gate,
    unit_keep,
    embedding,
    attention,
    feed_forward,
    map_weight,
    norm_params,
    embedding_rows,
    embedding_cols,
    attention_rows,
    attention_cols,
    feed_rows,
    feed_cols,
    map_rows,
    map_cols,
    norm_moment,
):
    unit_count = lax.axis_size("unit")
    chips = unit_count // 2
    unit_at = lax.axis_index("unit")
    data_at = lax.axis_index("dp")
    chip = unit_at // 2
    core = unit_at % 2
    length = token_ids.shape[1]
    pick_count = positions.shape[1]
    breadth = embedding.shape[1]
    vocab_dev = embedding.shape[0]
    units_dev = feed_forward.shape[2]
    layer_count = attention.shape[0]
    slab_rows = breadth // unit_count
    group_first = data_at * unit_count
    place = jnp.stack([chip * 2 * vocab_dev, core]).astype(jnp.int32)

    other_table = swapped(embedding)
    all_ids = jnp.concatenate(
        [token_ids[0]] + [across(token_ids[0], step) for step in range(1, chips)]
    )
    found, ends = scan_ids(all_ids, place, 2 * vocab_dev)
    served = list(lookup(all_ids, place, found, ends, embedding, other_table))
    halves = length // ROW_BLOCK
    own_place = jnp.stack([unit_at * vocab_dev, core]).astype(jnp.int32)
    other_ids = swapped(all_ids)
    table_low = embedding.astype(B)
    attention_low = attention.astype(B)
    map_low = map_weight.astype(B)
    looked, *lows = rows_of_tokens(
        [served[step * halves : (step + 1) * halves] for step in range(chips)],
        chips,
        [table_low, attention_low, map_low, *scan_ids(all_ids, own_place, vocab_dev)],
        lambda: scan_ids(other_ids, own_place, vocab_dev),
    )
    table_low, attention_low, map_low, *lists = lows
    feed_low = []
    for layer_at in range(layer_count):
        own = feed_forward[layer_at].astype(B)
        if layer_at > 0:
            looked, own = together(looked, own)
        feed_low.append(lax.all_gather(own, "unit", axis=1, tiled=True))
    teacher = lax.ppermute(
        teacher_states[0],
        "unit",
        [(u, (u + unit_count // 2) % unit_count) for u in range(unit_count)],
    )
    real_row = lax.dynamic_index_in_dim(real_mask, group_first + unit_at, 0, keepdims=False)
    real_flat = real_row.astype(F)
    count = jnp.sum(real_mask).astype(F)
    scale_all = unit_gate * unit_keep.astype(F)
    segments = segment_ids[0]
    windows = query_windows(segments, QUERY_BLOCK)
    key_segments = jnp.broadcast_to(
        jnp.where(real_row > 0, segments, -1)[:, None], (length, KEY_BLOCK)
    )
    query_segments = jnp.broadcast_to(segments[None, :], (8, length))
    head_scale = jnp.repeat(head_gate, HD, axis=1)

    normed, embed_stored = norm_forward(looked, norm_params[0], norm_params[1])
    hidden = normed * hidden_gate
    stored_layers = []
    for layer_at in range(layer_count):
        hidden_low = hidden.astype(B)
        weights = attention_low[layer_at]
        tokens, features = project(hidden_low, attention_low, layer_at)
        gated_t, log_total = attend(
            windows, head_gate[layer_at], tokens, features, key_segments, query_segments
        )
        branch = jnp.einsum("dr,de->re", gated_t, weights[3], preferred_element_type=F)
        middle, norm_first = norm_forward(
            hidden + branch * layer_gate[layer_at, 0] * hidden_gate,
            norm_params[2 + 4 * layer_at],
            norm_params[3 + 4 * layer_at],
        )
        middle_low = middle.astype(B)
        act, slope, result = feed(middle_low, feed_low[layer_at], scale_all[layer_at])
        if layer_at == 0:
            result, teacher = together(result, teacher)
        hidden, norm_second = norm_forward(
            middle + result * layer_gate[layer_at, 1] * hidden_gate,
            norm_params[4 + 4 * layer_at],
            norm_params[5 + 4 * layer_at],
        )
        stored_layers.append(
            (
                (hidden_low, tokens, features, gated_t, log_total),
                norm_first,
                (middle_low, act, slope),
                norm_second,
            )
        )

    final = hidden.astype(B)
    pick_hot = (positions[0][:, None] == jnp.arange(length)[None, :]).astype(B)
    picked_own = dot(pick_hot, final).astype(B)

    def map_loss(mapped):
        diff = mapped - teacher.astype(F)
        error = jnp.sum(jnp.sum(diff * diff, axis=-1) * real_flat) / breadth
        return error, (diff * (2.0 / (breadth * count)) * real_flat[:, None]).astype(B)

    picked_rows, _, (error_part, grad_mapped) = gathered(
        picked_own, [dot(final, map_low)], map_loss
    )
    picked_rows = picked_rows.reshape(unit_count * pick_count, breadth)
    target_all = jnp.concatenate(
        [
            lax.dynamic_index_in_dim(targets, group_first + (unit_at ^ other), 0, keepdims=False)
            for other in range(unit_count)
        ]
    )
    logits = contract(picked_rows, table_low, NT)
    is_target = (target_all - unit_at * vocab_dev)[:, None] == jnp.arange(vocab_dev)[None, :]
    row_max = jnp.max(logits, axis=1)
    sum_exp = jnp.sum(jnp.exp(logits - row_max[:, None]), axis=1)
    target_logit = jnp.sum(jnp.where(is_target, logits, 0.0), axis=1)
    shares, (grad_map,), (grad_final,) = gathered(
        jnp.stack([row_max, sum_exp, target_logit]).reshape(3, unit_count, pick_count),
        [contract(final, grad_mapped, TN).astype(B)],
        lambda _: (contract(grad_mapped, map_low, NT),),
    )
    shares = shares.reshape(unit_count, 3, unit_count, pick_count)
    shares = jnp.stack(
        [
            jnp.stack([shares[a, :, a ^ b] for a in range(unit_count)])
            for b in range(unit_count)
        ],
        axis=2,
    ).reshape(unit_count, 3, unit_count * pick_count)
    top = jnp.max(shares[:, 0], axis=0)
    log_sum = top + jnp.log(jnp.sum(shares[:, 1] * jnp.exp(shares[:, 0] - top), axis=0))
    own_terms = (log_sum - jnp.sum(shares[:, 2], axis=0))[:pick_count]
    grad_logits = (
        (jnp.exp(logits - log_sum[:, None]) - is_target.astype(F)) / count
    ).astype(B)
    grad_parts = dot(grad_logits, table_low).reshape(chips, 2, pick_count, breadth)
    both = grad_parts[:, 0] + swapped(grad_parts[:, 1])
    grad_picked = both[0]
    for step in range(1, chips):
        grad_picked = grad_picked + across(both[step], step)

    loss_part = error_part + jnp.sum(own_terms)
    grad_hidden = grad_final + lax.dot_general(
        pick_hot.astype(F),
        grad_picked,
        TN,
        precision=lax.Precision.HIGHEST,
        preferred_element_type=F,
    )

    gain_rows = [None] * norm_params.shape[0]
    feed_parts = [None] * layer_count
    attn_parts = [None] * layer_count
    later_feeds = []
    for layer_at in reversed(range(layer_count)):
        attn_stored, norm_first, feed_stored, norm_second = stored_layers[layer_at]
        hidden_low, tokens, features, gated_t, log_total = attn_stored
        middle_low, act, slope = feed_stored
        weights = attention_low[layer_at]
        grad_second, gain_rows[4 + 4 * layer_at], gain_rows[5 + 4 * layer_at] = norm_backward(
            norm_second, norm_params[4 + 4 * layer_at], grad_hidden
        )
        grad_result = (grad_second * layer_gate[layer_at, 1] * hidden_gate).astype(B)
        if layer_at < layer_count - 1:
            grad_result, attn_owned = together(grad_result, attn_owned)
            attn_parts[layer_at + 1] = lax.psum_scatter(attn_owned, "unit")
        grad_middle, feed_owned = feed_back(
            grad_result, middle_low, act, slope, feed_low[layer_at], unit_count
        )
        if layer_at < layer_count - 1:
            grad_middle, later_feed = together(grad_middle, feed_parts[layer_at + 1])
            later_feed = dp_scatter(later_feed.reshape(-1, breadth))
        feed_parts[layer_at] = lax.psum_scatter(feed_owned, "unit")
        grad_first, gain_rows[2 + 4 * layer_at], gain_rows[3 + 4 * layer_at] = norm_backward(
            norm_first, norm_params[2 + 4 * layer_at], grad_second + grad_middle
        )
        grad_branch = (grad_first * layer_gate[layer_at, 0] * hidden_gate).astype(B)
        scale = head_scale[layer_at]
        grad_mixed = (contract(grad_branch, weights[3], NT) * scale).astype(B)
        grad_proj = attend_back(
            windows,
            tokens,
            features,
            grad_mixed,
            key_segments,
            query_segments,
            log_total,
        )
        if layer_at < layer_count - 1:
            grad_proj, later_feed = together(grad_proj, later_feed)
            later_feeds.append(dp_gather(later_feed))
        grad_input = jnp.einsum("jre,jde->rd", grad_proj, weights[:3], preferred_element_type=F)
        grad_hidden = grad_first + grad_input
        grad_hidden, grad_proj = together(grad_hidden, grad_proj)
        grad_in = jnp.einsum(
            "rd,jre->jde", hidden_low, grad_proj, preferred_element_type=F
        ).astype(B)
        grad_out = dot(gated_t, grad_branch).astype(B)
        stack = [grad_in, grad_out[None]]
        if layer_at == layer_count - 1:
            stack.append(grad_map[None])
        stack = jnp.concatenate(stack, axis=0)
        if layer_at > 0:
            attn_owned = jnp.moveaxis(
                stack.reshape(-1, unit_count, slab_rows, breadth), 1, 0
            )
        else:
            stack = stack.reshape(-1, chips, 2, slab_rows, breadth)
            attn_mine = jnp.moveaxis(
                lax.dynamic_index_in_dim(stack, core, 2, keepdims=False), 1, 0
            )
            attn_theirs = jnp.moveaxis(
                lax.dynamic_index_in_dim(stack, 1 - core, 2, keepdims=False), 1, 0
            )

    grad_hidden, grad_logits = together(grad_hidden, grad_logits)
    grad_table = contract(grad_logits, picked_rows, TN)
    grad_looked, gain_rows[0], gain_rows[1] = norm_backward(
        embed_stored, norm_params[0], grad_hidden * hidden_gate
    )
    sent = grad_looked.astype(B)
    small = jnp.concatenate(
        [jnp.stack(gain_rows), jnp.broadcast_to(loss_part, (1, breadth))], axis=0
    )
    same = [(sent, 0), (sent, ROW_BLOCK)]
    other = swapped(sent)
    crossed = [(other, 0), (other, ROW_BLOCK)]
    if chips == 4 and length == 2 * ROW_BLOCK:
        near = [across(sent, 1), across(sent, 2)]
        later_feeds, later_attn = together(later_feeds, attn_parts[1:])
        later_attn = [dp_scatter(part.reshape(-1, breadth)) for part in later_attn]
        near, later_attn, grad_table, attn_theirs = together(
            near, later_attn, grad_table, attn_theirs
        )
        last = [across(near[0][:ROW_BLOCK], 2), across(near[1][ROW_BLOCK:], 1)]
        near_other = [swapped(part) for part in near]
        attn_chip = chip_sum(attn_mine, swapped(attn_theirs))
        later_attn = [dp_gather(part) for part in later_attn]
        last, near_other, attn_chip = together(last, near_other, attn_chip)
        last_other = [swapped(part) for part in last]
        attn_received = sent_to_owners(attn_chip, chip, range(1, chips))
        for home, parts, ends in ((same, near, last), (crossed, near_other, last_other)):
            home += [(part, at) for part in parts for at in (0, ROW_BLOCK)]
            home += [(part, 0) for part in ends]
    else:
        later_attn = [
            dp_gather(dp_scatter(part.reshape(-1, breadth))) for part in attn_parts[1:]
        ]
        attn_chip = chip_sum(attn_mine, swapped(attn_theirs))
        attn_received = sent_to_owners(attn_chip, chip, range(1, chips))
        for step in range(1, chips):
            part = across(sent, step)
            for home, part in ((same, part), (crossed, swapped(part))):
                home += [(part, at) for at in range(0, length, ROW_BLOCK)]
    embed_part = spread(all_ids, other_ids, own_place, lists, grad_table, same + crossed)
    embed_part, attn_received, later_attn = together(embed_part, attn_received, later_attn)
    small = dp_sum(small)
    attn_parts[0] = owner_total(attn_chip, attn_received, chip)
    embed_sum, feed_first, attn_first = lax.psum((embed_part, feed_parts[0], attn_parts[0]), "dp")
    attn_sums = [attn_first] + [
        dp_placed(found).reshape(part.shape) for found, part in zip(later_attn, attn_parts[1:])
    ]
    feed_sums = [feed_first] + [
        dp_placed(part).reshape(feed_first.shape) for part in reversed(later_feeds)
    ]
    row_sums = jnp.concatenate(
        [
            jnp.sum(attention_rows, axis=-1).reshape(-1),
            jnp.sum(feed_rows, axis=-1).reshape(-1),
            jnp.sum(map_rows)[None],
            jnp.sum(embedding_rows)[None],
        ]
    )
    row_sums = jnp.pad(row_sums, (0, breadth - row_sums.shape[0]))[None]
    old_cols = jnp.concatenate(
        [
            attention_cols.reshape(-1, breadth),
            feed_cols.reshape(-1, breadth),
            map_cols[None],
            embedding_cols[None],
        ],
        axis=0,
    )
    mats = layer_count * 4
    heights = jnp.array(
        [breadth] * mats
        + [units_dev * unit_count] * (layer_count * 2)
        + [breadth, vocab_dev * unit_count],
        F,
    )[:, None]
    packed = stats(small, row_sums, embed_sum, attn_sums, feed_sums)
    scalars, new_cols, factor, norm_grad, new_norm_params, new_norm_moment = factors(
        lax.all_gather(packed, "unit"), old_cols, heights, norm_params, norm_moment
    )
    total_loss, grad_norm = scalars[0], scalars[1]
    factor = factor[:, None]
    feeds = layer_count * 2
    here = jnp.zeros((1,), jnp.int32)
    slab = jnp.full((1,), unit_at, jnp.int32)
    new_embedding, embed_grad, new_embedding_rows = (
        value[0]
        for value in renew(
            scalars,
            here,
            factor,
            mats + feeds + 1,
            embedding_rows[None],
            embedding[None],
            embed_sum[None],
            1,
            640,
        )
    )
    new_map, map_grad, new_map_rows = (
        value[0]
        for value in renew(
            scalars,
            slab,
            factor,
            mats + feeds,
            map_rows[None],
            map_weight[None],
            attn_sums[layer_count - 1][4:],
            1,
            slab_rows,
        )
    )
    new_attention, attn_grad, new_attention_rows = (
        value.reshape((layer_count, 4) + value.shape[1:])
        for value in renew(
            scalars,
            slab,
            factor,
            0,
            attention_rows.reshape(mats, slab_rows),
            attention.reshape(mats, breadth, breadth),
            jnp.concatenate([part[:4] for part in attn_sums], axis=0),
            4,
            slab_rows,
        )
    )
    new_feed_forward, feed_grad, new_feed_rows = (
        value.reshape((layer_count, 2) + value.shape[1:])
        for value in renew(
            scalars,
            here,
            factor,
            mats,
            feed_rows.reshape(feeds, units_dev),
            feed_forward.reshape(feeds, units_dev, breadth),
            jnp.concatenate(feed_sums, axis=0),
            1,
            units_dev,
        )
    )
    new_attention_cols = new_cols[:mats].reshape(layer_count, 4, breadth)
    new_feed_cols = new_cols[mats : mats + feeds].reshape(layer_count, 2, breadth)
    new_map_cols = new_cols[mats + feeds]
    new_embedding_cols = new_cols[mats + feeds + 1]
    return (
        total_loss,
        count,
        grad_norm,
        new_embedding,
        embed_grad,
        new_embedding_rows,
        new_embedding_cols,
        new_attention,
        attn_grad,
        new_attention_rows,
        new_attention_cols,
        new_feed_forward,
        feed_grad,
        new_feed_rows,
        new_feed_cols,
        new_map,
        map_grad,
        new_map_rows,
        new_map_cols,
        new_norm_params,
        norm_grad,
        new_norm_moment,
    )


def solution(mesh):
    placed = (
        P(("dp", "unit"), None),
        P(("dp", "unit"), None),
        P(),
        P(("dp", "unit"), None),
        P(),
        P(("dp", "unit"), None, None),
        P(),
        P(),
        P(),
        P(),
        P(),
        P("unit", None),
        P(),
        P(None, None, "unit", None),
        P(),
        P(),
        P("unit"),
        P(),
        P(None, None, "unit"),
        P(),
        P(None, None, "unit"),
        P(),
        P("unit"),
        P(),
        P(),
    )
    return jax.shard_map(
        local,
        mesh=mesh,
        in_specs=placed,
        out_specs=(
            P(),
            P(),
            P(),
            P("unit", None),
            P("unit", None),
            P("unit"),
            P(),
            P(None, None, "unit", None),
            P(None, None, "unit", None),
            P(None, None, "unit"),
            P(),
            P(None, None, "unit", None),
            P(None, None, "unit", None),
            P(None, None, "unit"),
            P(),
            P("unit", None),
            P("unit", None),
            P("unit"),
            P(),
            P(),
            P(),
            P(),
        ),
        check_vma=False,
    )
```
